32 devices in a mesh: wide: 16 (over z, y, core), narrow: 2 (over x).
Axes of the slice: x: 2, y: 2, z: 4, core: 2. Of those that a mesh axis runs over, the one named last changes fastest.
Arguments:
- dark: bfloat16 [64, 16, 2, 16], P(None, None, 'narrow'), may hold values from -6 to 6
- w_enc: bfloat16 [27, 64, 64], replicated, may hold values from -0.15625 to 0.15625
- up_weight: bfloat16 [512, 16, 64], replicated, may hold values from -0.75 to 0.75
- w_dec: bfloat16 [27, 16, 16], replicated, may hold values from -0.3125 to 0.3125
- cotangent: bfloat16 [16, 128, 16, 128], P(None, 'wide', 'narrow'), may hold values from -6 to 6
Outputs:
- grad_dark: float32 [64, 16, 2, 16], P(None, None, 'narrow')
- grad_w_enc: float32 [27, 64, 64], replicated
- grad_up_weight: float32 [512, 16, 64], P(('wide', 'narrow'))
- grad_w_dec: float32 [27, 16, 16], replicated
The draws below stay inside these ranges and needn't reach their ends.
All inputs are finite; a program needn't handle non-finite values.
Results may differ from the reference program's by a relative error of at most 0.0053.
Values may be sent and summed in bfloat16 or wider, within the bound.
No kernel may reach another device: no remote copies, remote signals or barrier semaphores. Data moves between devices by JAX's collectives and lax.ppermute only.
A program may use at most 64 MiB of HBM per device.

```python
import math
import jax
import jax.numpy as jnp
from jax import lax

CH = 64
FCH = 16
RATIO = 8
CY = 16
FY = 128
XC = 16
ZC = 2
XF = 128
ZF = 16
SUBS = 512
NCOARSE = 512
NFINE = 262144


def steps_of(own_key, dims, pieces, low, top_value):
    loudness = 1.0
    for dim, parts in pieces:
        steps = jax.random.uniform(jax.random.fold_in(jax.random.fold_in(own_key, 6), dim), (parts,), jnp.float32, low / len(pieces), top_value / len(pieces))
        loudness = loudness * jnp.repeat(jnp.exp(steps), dims[dim] // parts).reshape((-1,) + (1,) * (len(dims) - 1 - dim))
    return loudness


def bell_draw(stream_key, dims, spread, bound, shards=(), kind=jnp.bfloat16):
    values = jax.random.normal(stream_key, dims, jnp.float32) * spread
    if len(shards) > 0:
        values = steps_of(stream_key, dims, shards, -0.22, 0.18) * values
    return jnp.clip(values, min=-bound, max=bound).astype(kind)


def setup_inputs(seed: int = 0) -> dict:
    keys = jax.random.split(jax.random.key(seed), 6)
    dark = bell_draw(keys[0], (CH, XC, ZC, CY), 1.0, 6.0, ((2, 2),))
    w_enc = bell_draw(keys[1], (27, CH, CH), (27 * CH) ** -0.5, 0.15625)
    up_weight = bell_draw(keys[2], (SUBS, FCH, CH), CH ** -0.5, 0.75)
    w_dec = bell_draw(keys[3], (27, FCH, FCH), (27 * FCH) ** -0.5, 0.3125)
    cotangent = bell_draw(keys[4], (FCH, XF, ZF, FY), 1.0, 6.0, ((1, 16), (2, 2)))
    return {"dark": dark, "w_enc": w_enc, "up_weight": up_weight, "w_dec": w_dec, "cotangent": cotangent}


def convolve(field, kernel):
    outputs = kernel.shape[1]
    inputs = kernel.shape[2]
    taps = kernel.reshape(3, 3, 3, outputs, inputs).transpose(3, 4, 0, 1, 2)
    result = lax.conv_general_dilated(field[None], taps, (1, 1, 1), ((1, 1), (1, 1), (1, 1)), dimension_numbers=('NCDHW', 'OIDHW', 'NCDHW'), precision=lax.Precision.HIGHEST)
    return result[0]

def silu_slope(values):
    sigma = jax.nn.sigmoid(values)
    return sigma * (1.0 + values * (1.0 - sigma))

def reference(dark, w_enc, up_weight, w_dec, cotangent):
    ratio = RATIO
    dark_float = dark.astype(jnp.float32)
    enc_kernel = w_enc.astype(jnp.float32)
    enc_pre = convolve(dark_float, enc_kernel)
    encoded = jax.nn.silu(enc_pre).astype(jnp.bfloat16)
    planes = encoded.shape[1]
    depth = encoded.shape[2]
    width = encoded.shape[3]
    table = up_weight.astype(jnp.float32).reshape(ratio, ratio, ratio, FCH, CH)
    enc_float = encoded.astype(jnp.float32)
    upsampled = jnp.einsum('ijkoc,cxzy->oxizjyk', table, enc_float).reshape(FCH, planes * ratio, depth * ratio, width * ratio).astype(jnp.bfloat16)
    up_float = upsampled.astype(jnp.float32)
    dec_kernel = w_dec.astype(jnp.float32)
    dec_pre = convolve(up_float, dec_kernel)
    cot_float = cotangent.astype(jnp.float32)
    dec_grad = (cot_float * silu_slope(dec_pre)).astype(jnp.bfloat16)
    _, pull_fine = jax.vjp(convolve, up_float, dec_kernel)
    back_up, grad_dec = pull_fine(dec_grad.astype(jnp.float32))
    up_grad = (cot_float + back_up).astype(jnp.bfloat16)
    grad_blocks = up_grad.astype(jnp.float32).reshape(FCH, planes, ratio, depth, ratio, width, ratio)
    grad_up = jnp.einsum('oxizjyk,cxzy->ijkoc', grad_blocks, enc_float).reshape(ratio * ratio * ratio, FCH, CH)
    enc_grad = jnp.einsum('ijkoc,oxizjyk->cxzy', table, grad_blocks).astype(jnp.bfloat16)
    enc_pre_grad = (enc_grad.astype(jnp.float32) * silu_slope(enc_pre)).astype(jnp.bfloat16)
    _, pull_coarse = jax.vjp(convolve, dark_float, enc_kernel)
    grad_dark, grad_enc = pull_coarse(enc_pre_grad.astype(jnp.float32))
    coarse_scale = 1.0 / math.sqrt(NCOARSE)
    fine_scale = 1.0 / math.sqrt(NFINE)
    return (grad_dark, grad_enc * coarse_scale, grad_up * coarse_scale, grad_dec * fine_scale)
```

```python
import functools
import math

import jax
import jax.numpy as jnp
from jax import lax
from jax.experimental import pallas as pl
from jax.experimental.pallas import tpu as pltpu
from jax.sharding import PartitionSpec as P

RATIO = 8
F32 = jnp.float32
BF16 = jnp.bfloat16
VMEM_LIMIT = 48 * 1024 * 1024
VMEM = pltpu.VMEM
AXES = ("wide", "narrow")


def slope_of(values):
    sigma = jax.nn.sigmoid(values)
    return sigma * (1.0 + values * (1.0 - sigma))


def dot(left, right):
    return jnp.dot(left, right, preferred_element_type=F32)


def dot_nt(left, right):
    return lax.dot_general(left, right, (((1,), (1,)), ((), ())), preferred_element_type=F32)


def dot_tn(left, right):
    return lax.dot_general(left, right, (((0,), (0,)), ((), ())), preferred_element_type=F32)


def iota(shape, dim):
    return lax.broadcasted_iota(jnp.int32, shape, dim)


def one_hot(condition):
    return jnp.where(condition, 1.0, 0.0).astype(BF16)


def row_place(rows, columns, fine_ch):
    index = iota((rows, columns), 0)
    return place(index, fine_ch)


def place(index, fine_ch):
    main = fine_ch * RATIO
    over = index - main
    channel = jnp.where(index < main, index // RATIO, over % fine_ch)
    z = jnp.where(index < main, index % RATIO, jnp.where(over < fine_ch, -1, RATIO))
    return channel, z


def lane_shift(values, by):
    width = values.shape[1]
    lane = iota(values.shape, 1)
    if by > 0:
        return jnp.where(lane < by, 0.0, pltpu.roll(values, by, 1))
    return jnp.where(lane >= width + by, 0.0, pltpu.roll(values, width + by, 1))


def three_lanes(values):
    return jnp.concatenate(
        [
            lane_shift(values, 1).astype(BF16),
            values.astype(BF16),
            lane_shift(values, -1).astype(BF16),
        ],
        0,
    )


def prepare_kernel(table_ref, dec_ref, enc_ref, wide_ref, conv_ref, back_ref, enc3_ref):
    fine_ch = dec_ref.shape[1]
    chans = table_ref.shape[-1]
    for i in range(RATIO):
        rows = [
            table_ref[i, :, k].reshape(RATIO * fine_ch, chans) for k in range(RATIO)
        ]
        wide_ref[i] = jnp.concatenate(rows, 1)
    for ab in range(9):
        enc3_ref[ab] = jnp.concatenate([enc_ref[3 * ab + e] for e in range(3)], 1)
    rows = fine_ch * (RATIO + 2)
    columns = fine_ch * (RATIO + 4)
    channel, _ = row_place(rows, fine_ch, fine_ch)
    pick = one_hot(channel == iota((rows, fine_ch), 1))
    spread = one_hot(iota((fine_ch, columns), 0) == iota((fine_ch, columns), 1) % fine_ch)
    _, z_out = row_place(rows, columns, fine_ch)
    z_in = iota((rows, columns), 1) // fine_ch - 2
    pieces = []
    for a in range(3):
        for e in range(3):
            piece = jnp.zeros((rows, columns), F32)
            for b in range(3):
                tap = dot(pick, dec_ref[9 * a + 3 * b + e]).astype(BF16)
                piece = jnp.where(z_in - z_out + 1 == b, dot(tap, spread), piece)
            pieces.append(piece)
    conv_ref[...] = jnp.concatenate(pieces, 1).astype(BF16)
    out_rows = fine_ch * RATIO
    pick = one_hot(iota((out_rows, fine_ch), 0) % fine_ch == iota((out_rows, fine_ch), 1))
    channel, _ = place(iota((fine_ch, rows), 1), fine_ch)
    spread = one_hot(iota((fine_ch, rows), 0) == channel)
    _, z_in = place(iota((out_rows, rows), 1), fine_ch)
    z_out = iota((out_rows, rows), 0) // fine_ch
    pieces = []
    for a in range(3):
        for e in range(3):
            piece = jnp.zeros((out_rows, rows), F32)
            for b in range(3):
                tap = dot_nt(pick, dec_ref[26 - (9 * a + 3 * b + e)]).astype(BF16)
                piece = jnp.where(z_in - z_out + 1 == b, dot(tap, spread), piece)
            pieces.append(piece)
    back_ref[...] = jnp.concatenate(pieces, 1).astype(BF16)


def shifted_rows(values, width):
    count = values.shape[0]
    block = min(count, 256)
    row = iota((block, block), 0)
    column = iota((block, block), 1)
    down = one_hot((column == row - 1) & (row % width > 0))
    up = one_hot((column == row + 1) & (row % width < width - 1))
    pieces = []
    for first in range(0, count, block):
        part = values[first : first + block]
        pieces.append(
            jnp.concatenate([dot(down, part), part.astype(F32), dot(up, part)], 1).astype(BF16)
        )
    return jnp.concatenate(pieces, 0)


def encode_kernel(
    place_ref, dark_ref, enc3_ref, wide_ref, pre_ref, encoded_ref, dark3_ref, up_ref, pad_ref
):
    depth, planes, width, chans = dark_ref.shape
    fine_rows = wide_ref.shape[1]
    fine_ch = fine_rows // RATIO
    dark3_ref[...] = jnp.zeros(dark3_ref.shape, BF16)
    for z in range(depth):
        rows = dark_ref[z].reshape(planes * width, chans)
        dark3_ref[1 : planes + 1, z + 1] = shifted_rows(rows, width).reshape(
            planes, width, 3 * chans
        )
    cells = planes * depth * width
    pre = jnp.zeros((cells, chans), F32)
    for a in range(3):
        for b in range(3):
            window = dark3_ref[a : a + planes, b : b + depth].reshape(cells, 3 * chans)
            pre = pre + dot_nt(window, enc3_ref[3 * a + b])
    pre_ref[...] = pre
    encoded = jax.nn.silu(pre).astype(BF16)
    encoded_ref[...] = encoded
    pad_ref[...] = jnp.zeros(pad_ref.shape, BF16)
    pad_ref[1 : planes + 1, 1 : depth + 1] = encoded.reshape(planes, depth, width, chans)
    first_x = place_ref[0]
    first_z = place_ref[1]
    fine_width = width * RATIO
    repeat = one_hot(
        iota((fine_width, width), 0) // RATIO == iota((fine_width, width), 1)
    )
    tile = one_hot(
        iota((chans, RATIO * chans), 0) == iota((chans, RATIO * chans), 1) % chans
    )
    shape = (fine_width, RATIO * chans)
    mask = iota(shape, 0) % RATIO == iota(shape, 1) // chans
    spread = {}
    for dx in range(3):
        for dz in range(3):
            cell = pad_ref[first_x + dx, first_z + dz]
            tiled = dot(cell, tile).astype(BF16)
            spread[dx, dz] = jnp.where(mask, dot(repeat, tiled), 0.0).astype(BF16)
    margin = 2 * fine_ch
    plan = ((0, range(RATIO - 2, RATIO), 0), (1, range(RATIO), 2), (2, range(2), RATIO + 2))
    for dx, picks, base in plan:
        count = len(picks)
        low = dot_nt(
            jnp.concatenate([wide_ref[i, fine_rows - margin :] for i in picks], 0), spread[dx, 0]
        )
        middle = dot_nt(jnp.concatenate([wide_ref[i] for i in picks], 0), spread[dx, 1])
        high = dot_nt(jnp.concatenate([wide_ref[i, :margin] for i in picks], 0), spread[dx, 2])
        for n in range(count):
            plane = jnp.concatenate(
                [
                    low[n * margin : (n + 1) * margin],
                    middle[n * fine_rows : (n + 1) * fine_rows],
                    high[n * margin : (n + 1) * margin],
                ],
                0,
            )
            up_ref[base + n] = three_lanes(plane)


def decode_kernel(cot_ref, low_ref, high_ref, edge_ref, conv_ref, up_ref, grad_ref, total_ref):
    fine_ch, planes, depth, width = cot_ref.shape
    main = fine_ch * depth
    rows = conv_ref.shape[0]
    taps = up_ref.shape[1]
    keep = []
    for x in range(planes + 2):
        fields = up_ref[x : x + 3].reshape(3 * taps, width)
        pre = dot(conv_ref[...], fields)
        if x == 0:
            inner = low_ref[...]
        elif x == planes + 1:
            inner = high_ref[...]
        else:
            inner = cot_ref[:, x - 1]
        cot = jnp.concatenate(
            [
                inner.astype(F32).reshape(main, width),
                edge_ref[x].astype(F32).reshape(rows - main, width),
            ],
            0,
        )
        grad = (cot * slope_of(pre)).astype(BF16)
        grad_ref[x] = three_lanes(grad.astype(F32))
        if 0 < x <= planes:
            keep.append(grad[:main])
    grads = jnp.concatenate(keep, 1)
    shape = (main, taps)
    span = RATIO + 4
    z_in = (iota(shape, 1) // fine_ch) % span
    z_out = iota(shape, 0) % RATIO
    shape = (taps, 3 * fine_ch)
    fold_row = iota(shape, 0)
    fold = jnp.where(
        (fold_row // (span * fine_ch) == iota(shape, 1) // fine_ch)
        & (fold_row % fine_ch == iota(shape, 1) % fine_ch),
        1.0,
        0.0,
    )
    for a in range(3):
        fields = jnp.concatenate([up_ref[x + a] for x in range(1, planes + 1)], 1)
        product = dot_nt(grads, fields)
        sums = []
        for b in range(3):
            kept = jnp.where(z_in - z_out - 1 == b, product, 0.0)
            sums.append(jnp.sum(kept.reshape(fine_ch, RATIO, taps), 1))
        total_ref[a] = jnp.dot(
            jnp.concatenate(sums, 0),
            fold,
            precision=lax.Precision.HIGHEST,
            preferred_element_type=F32,
        )


def spread_kernel(cot_ref, grad_ref, back_ref, wide_ref, send_ref):
    fine_ch, planes, depth, width = cot_ref.shape
    main = fine_ch * depth
    taps = grad_ref.shape[1]
    chans = wide_ref.shape[2] // RATIO
    owners, chunk, _ = send_ref.shape
    span = chunk - width // RATIO
    row = iota((main, main), 0)
    column = iota((main, main), 1)
    turn = one_hot((row % fine_ch == column // RATIO) & (row // fine_ch == column % RATIO))
    ups = []
    for x in range(planes):
        fields = grad_ref[x : x + 3].reshape(3 * taps, width)
        own = cot_ref[:, x].astype(F32).reshape(main, width).astype(BF16)
        ups.append((dot(back_ref[...], fields) + dot(turn, own)).astype(BF16))
    parts = dot_tn(
        jnp.concatenate(ups, 0), jnp.concatenate([wide_ref[x] for x in range(planes)], 0)
    )
    mask = iota(parts.shape, 0) % RATIO == iota(parts.shape, 1) // chans
    parts = jnp.where(mask, parts, 0.0)
    both = sum(parts[:, n : n + 2 * chans] for n in range(0, RATIO * chans, 2 * chans))
    cell_grad = jnp.sum((both + pltpu.roll(both, chans, 1)).reshape(-1, RATIO, 2 * chans), 1)
    cell_grad = cell_grad.astype(BF16)
    for owner in range(owners):
        first = (owner * RATIO * RATIO // owners) * fine_ch
        send_ref[owner, :span] = ups[first // main][first % main : first % main + span]
        send_ref[owner, span:] = cell_grad


def widen_kernel(encoded_ref, pre_ref, out_ref, slope_ref):
    cells = encoded_ref.shape[0]
    block = 32
    repeat = one_hot(
        iota((block * RATIO, block), 0) // RATIO == iota((block * RATIO, block), 1)
    )
    for first in range(0, cells, block):
        out_ref[first * RATIO : (first + block) * RATIO] = dot(
            repeat, encoded_ref[first : first + block]
        ).astype(BF16)
    slope_ref[...] = slope_of(pre_ref[...])


def finish_kernel(
    place_ref, got_ref, spread_ref, slope_ref, dark3_ref, enc_ref,
    dark_out, enc_out, up_out, pad_ref,
    *, scale,
):
    owners, chunk, fine_width = got_ref.shape
    padded_planes, padded_depth, width, chans3 = dark3_ref.shape
    planes = padded_planes - 2
    depth = padded_depth - 2
    chans = chans3 // 3
    cells = planes * depth * width
    span = chunk - width
    fine_ch = up_out.shape[1]
    arrived = got_ref[:, span:].astype(F32).reshape(cells, fine_width)[:, :chans]
    grad = (arrived * slope_ref[...]).astype(BF16)
    turned = grad.astype(F32).T.astype(BF16)
    for a in range(3):
        for b in range(3):
            window = dark3_ref[a : a + planes, b : b + depth].reshape(cells, chans3)
            product = dot(turned, window) * scale
            for e in range(3):
                enc_out[9 * a + 3 * b + e] = product[:, e * chans : (e + 1) * chans]
    pad_ref[...] = jnp.zeros(pad_ref.shape, BF16)
    pad_ref[1 : planes + 1, 1 : depth + 1] = shifted_rows(grad, width).reshape(
        planes, depth, width, chans3
    )
    own_z = place_ref[1]
    total = jnp.zeros((planes * width, chans), F32)
    for a in range(3):
        for b in range(3):
            window = pad_ref[a : a + planes, own_z + b].reshape(planes * width, chans3)
            first = 26 - (9 * a + 3 * b)
            taps = jnp.concatenate([enc_ref[first - e] for e in range(3)], 0)
            total = total + dot(window, taps)
    dark_out[...] = total.reshape(planes, width, chans)
    pairs = span // fine_ch
    lane = iota((RATIO * fine_ch, fine_width), 1) % RATIO
    masks = one_hot(lane == iota((RATIO * fine_ch, fine_width), 0) // fine_ch)
    step = 8

    def add(block, sums):
        pieces = []
        for n in range(step):
            rows = got_ref[block * step + n, :span]
            pieces.append(
                jnp.concatenate(
                    [
                        jnp.concatenate([rows[p * fine_ch : (p + 1) * fine_ch]] * RATIO, 0) * masks
                        for p in range(pairs)
                    ],
                    0,
                )
            )
        wide = step * fine_width
        field = spread_ref[pl.ds(pl.multiple_of(block * wide, wide), wide)]
        return sums + dot(jnp.concatenate(pieces, 1), field)

    sums = lax.fori_loop(
        0, owners // step, add, jnp.zeros((pairs * RATIO * fine_ch, chans), F32), unroll=True
    )
    up_out[...] = (sums * scale).reshape(pairs * RATIO, fine_ch, chans)


def call(kernel, out_shape, args, scratch=(), scalars=0, flops=1e8):
    specs = [pl.BlockSpec(memory_space=pltpu.SMEM)] * scalars
    specs += [pl.BlockSpec(memory_space=VMEM)] * (len(args) - scalars)
    return pl.pallas_call(
        kernel,
        out_shape=[jax.ShapeDtypeStruct(*s) for s in out_shape],
        in_specs=specs,
        out_specs=[pl.BlockSpec(memory_space=VMEM)] * len(out_shape),
        scratch_shapes=list(scratch),
        compiler_params=pltpu.CompilerParams(vmem_limit_bytes=VMEM_LIMIT),
        cost_estimate=pl.CostEstimate(
            flops=int(flops), bytes_accessed=2_000_000, transcendentals=0
        ),
    )(*args)


def shift(block, axis, by):
    count = lax.axis_size(axis)
    pairs = [(i, i + by) for i in range(count) if 0 <= i + by < count]
    return lax.ppermute(block, axis, pairs)


def sum_over_all(value):
    count = lax.axis_size(AXES)
    if count & (count - 1):
        return lax.psum(value, AXES)
    step = 1
    while step < count:
        value = value + lax.ppermute(value, AXES, [(i, i ^ step) for i in range(count)])
        step *= 2
    return value


def exchange_depth(dark_rows, faces):
    count = lax.axis_size("narrow")
    if count == 2:
        mine = lax.axis_index("narrow")
        swap = [(0, 1), (1, 0)]
        other = lax.ppermute(dark_rows, "narrow", swap)
        face = lax.ppermute(jnp.where(mine == 0, faces[1], faces[0]), "narrow", swap)
        none = jnp.zeros_like(face)
        first = mine == 0
        planes = jnp.stack(
            [jnp.where(first, dark_rows, other), jnp.where(first, other, dark_rows)], 0
        )
        return planes, jnp.where(first, none, face), jnp.where(first, face, none)
    planes = lax.all_gather(dark_rows, "narrow", axis=0)
    return planes, shift(faces[1], "narrow", 1), shift(faces[0], "narrow", -1)


def on_device(dark, w_enc, up_weight, w_dec, cotangent):
    chans, planes, own_depth, width = dark.shape
    fine_ch, own_fine, fine_depth, fine_width = cotangent.shape
    subs = up_weight.shape[0]
    wide_count = lax.axis_size("wide")
    depth = lax.axis_size("narrow")
    owners = wide_count * depth
    cells = planes * depth * width
    own_rows = subs // owners
    where = jnp.stack([lax.axis_index("wide"), lax.axis_index("narrow")]).astype(jnp.int32)

    dark_rows = dark[:, :, 0].transpose(1, 2, 0)
    faces = [cotangent[:, :, z].transpose(1, 0, 2) for z in (0, fine_depth - 1)]
    dark_planes, face_low, face_high = exchange_depth(dark_rows, faces)
    edges = jnp.stack([face_low, face_high], 1)
    x_low = shift(cotangent[:, -1], "wide", 1)
    x_high = shift(cotangent[:, 0], "wide", -1)
    edge_low = shift(edges[-1], "wide", 1)
    edge_high = shift(edges[0], "wide", -1)
    edges = jnp.concatenate([edge_low[None], edges, edge_high[None]], 0)

    rows = fine_ch * (RATIO + 2)
    taps = 3 * fine_ch * (RATIO + 4)
    main = fine_ch * RATIO
    wide_table, conv, back, enc3 = call(
        prepare_kernel,
        [
            ((RATIO, main, RATIO * chans), BF16),
            ((rows, 3 * taps), BF16),
            ((main, 9 * rows), BF16),
            ((9, chans, 3 * chans), BF16),
        ],
        (up_weight.reshape(RATIO, RATIO, RATIO, fine_ch, chans), w_dec, w_enc),
        flops=2e9,
    )
    enc_pre, encoded, dark3, upsampled = call(
        encode_kernel,
        [
            ((cells, chans), F32),
            ((cells, chans), BF16),
            ((planes + 2, depth + 2, width, 3 * chans), BF16),
            ((RATIO + 4, taps, fine_width), BF16),
        ],
        (where, dark_planes, enc3, wide_table),
        scratch=[VMEM((planes + 2, depth + 2, width, chans), BF16)],
        scalars=1,
        flops=2e9,
    )
    dec_grad, dec_part = call(
        decode_kernel,
        [((RATIO + 2, 3 * rows, fine_width), BF16), ((3, 3 * fine_ch, 3 * fine_ch), F32)],
        (cotangent, x_low, x_high, edges, conv, upsampled),
        flops=2e9,
    )
    dec_sum = sum_over_all(dec_part)
    chunk = max(1, RATIO * RATIO // owners) * fine_ch + width
    (send,) = call(
        spread_kernel,
        [((owners, chunk, fine_width), BF16)],
        (cotangent, dec_grad, back, wide_table),
        flops=2e9,
    )
    got = lax.all_to_all(send, AXES, 0, 0, tiled=True)
    enc_spread, enc_slope = call(
        widen_kernel,
        [((cells * RATIO, chans), BF16), ((cells, chans), F32)],
        (encoded, enc_pre),
        flops=1e9,
    )
    coarse_scale = 1.0 / math.sqrt(cells)
    fine_scale = 1.0 / math.sqrt(cells * subs)
    pairs = (chunk - width) // fine_ch
    grad_dark, grad_enc, grad_up = call(
        functools.partial(finish_kernel, scale=coarse_scale),
        [
            ((planes, width, chans), F32),
            ((27, chans, chans), F32),
            ((pairs * RATIO, fine_ch, chans), F32),
        ],
        (where, got, enc_spread, enc_slope, dark3, w_enc),
        scratch=[VMEM((planes + 2, depth + 2, width, 3 * chans), BF16)],
        scalars=1,
        flops=2e9,
    )
    if own_rows < pairs * RATIO:
        own = lax.axis_index(AXES) * own_rows % RATIO
        grad_up = lax.dynamic_slice_in_dim(grad_up, own, own_rows, 0)
    grad_dec = (
        dec_sum.reshape(3, 3, fine_ch, 3, fine_ch)
        .transpose(0, 1, 3, 2, 4)
        .reshape(27, fine_ch, fine_ch)
    ) * fine_scale
    return grad_dark.transpose(2, 0, 1)[:, :, None], grad_enc, grad_up, grad_dec


def solution(mesh):
    in_specs = (P(None, None, "narrow", None), P(), P(), P(), P(None, "wide", "narrow", None))
    out_specs = (P(None, None, "narrow", None), P(), P(("wide", "narrow"), None, None), P())
    return jax.shard_map(
        on_device, mesh=mesh, in_specs=in_specs, out_specs=out_specs, check_vma=False
    )
```

```python
import functools
import math

import jax
import jax.numpy as jnp
from jax import lax
from jax.experimental import pallas as pl
from jax.experimental.pallas import tpu as pltpu
from jax.sharding import PartitionSpec as P

RATIO = 8
SPAN = 16
F32 = jnp.float32
BF16 = jnp.bfloat16
VMEM_LIMIT = 48 * 1024 * 1024
VMEM = pltpu.VMEM
AXES = ("wide", "narrow")


def slope_of(values):
    sigma = jax.nn.sigmoid(values)
    return sigma * (1.0 + values * (1.0 - sigma))


def dot(left, right):
    return jnp.dot(left, right, preferred_element_type=F32)


def dot_nt(left, right):
    return lax.dot_general(left, right, (((1,), (1,)), ((), ())), preferred_element_type=F32)


def dot_tn(left, right):
    return lax.dot_general(left, right, (((0,), (0,)), ((), ())), preferred_element_type=F32)


def iota(shape, dim):
    return lax.broadcasted_iota(jnp.int32, shape, dim)


def one_hot(condition):
    return jnp.where(condition, 1.0, 0.0).astype(BF16)


def place(index, fine_ch):
    main = fine_ch * RATIO
    over = index - main
    channel = jnp.where(index < main, index // RATIO, over % fine_ch)
    z = jnp.where(index < main, index % RATIO, jnp.where(over < fine_ch, -1, RATIO))
    return channel, z


def lane_shift(values, by):
    width = values.shape[1]
    lane = iota(values.shape, 1)
    if by > 0:
        return jnp.where(lane < by, 0.0, pltpu.roll(values, by, 1))
    return jnp.where(lane >= width + by, 0.0, pltpu.roll(values, width + by, 1))


def store_shifts(ref, block, values):
    rows, width = values.shape
    lanes = slice(block * width, (block + 1) * width)
    ref[0:rows, lanes] = lane_shift(values, 1).astype(BF16)
    ref[rows : 2 * rows, lanes] = values.astype(BF16)
    ref[2 * rows : 3 * rows, lanes] = lane_shift(values, -1).astype(BF16)


def prepare_kernel(table_ref, dec_ref, enc_ref, wide_ref, conv_ref, back_ref, encw_ref):
    fine_ch, chans, subs = table_ref.shape
    depth = encw_ref.shape[1] // chans
    pairs = RATIO * RATIO
    row = iota((subs, subs), 0)
    pick = one_hot(iota((subs, subs), 1) == (row % pairs) * RATIO + row // pairs)
    turned = dot_nt(pick, table_ref[...].reshape(fine_ch * chans, subs))
    two = 2 * chans
    low = iota((pairs, two), 1) < chans
    for p in range(fine_ch // 2):
        lanes = slice(p * two, (p + 1) * two)
        for q in range(RATIO // 2):
            even = turned[2 * q * pairs : (2 * q + 1) * pairs, lanes]
            odd = turned[(2 * q + 1) * pairs : (2 * q + 2) * pairs, lanes]
            first = jnp.where(low, even, pltpu.roll(odd, chans, 1))
            second = jnp.where(low, pltpu.roll(even, chans, 1), odd)
            both = jnp.concatenate(
                [first.reshape(RATIO, RATIO, two), second.reshape(RATIO, RATIO, two)], 1
            )
            wide_ref[:, p * SPAN : (p + 1) * SPAN, q * two : (q + 1) * two] = both.astype(BF16)
    blank = jnp.zeros((chans, chans), BF16)
    for a in range(3):
        for z_out in range(depth):
            blocks = []
            for e in range(3):
                for z_in in range(depth):
                    b = z_in - z_out + 1
                    blocks.append(enc_ref[9 * a + 3 * b + e] if 0 <= b < 3 else blank)
            encw_ref[a, z_out * chans : (z_out + 1) * chans] = jnp.concatenate(blocks, 1)
    taps = dec_ref[...].reshape(fine_ch * fine_ch, 27)
    group = 9 * fine_ch
    rows = fine_ch * (RATIO + 2)
    main = fine_ch * RATIO
    square = fine_ch * fine_ch
    tap_row = iota((27, group), 0)
    tap_ae = iota((27, group), 1) // fine_ch
    tap_base = 9 * (tap_ae // 3) + tap_ae % 3
    cell_row = iota((square, group), 0)
    cell_last = iota((square, group), 1) % fine_ch
    same_in = cell_last == cell_row % fine_ch
    same_out = cell_last == cell_row // fine_ch
    channel, _ = place(iota((rows, square), 0), fine_ch)
    pick = one_hot(channel == iota((rows, square), 1) // fine_ch)
    pick_back = one_hot(
        iota((main, square), 0) // RATIO == iota((main, square), 1) % fine_ch
    )
    _, z_out = place(iota((rows, 128), 0), fine_ch)
    offset = iota((rows, 128), 1) % SPAN - 2 - z_out + 1
    wide = group * SPAN
    spread = one_hot(iota((group, wide), 1) // SPAN == iota((group, wide), 0))
    offset = jnp.concatenate([offset] * (wide // 128), 1)
    piece = jnp.zeros((rows, wide), F32)
    backs = [jnp.zeros((main, 3 * rows), F32)] * 3
    spread_back = []
    for a in range(3):
        column = iota((group, 3 * rows), 1)
        channel, _ = place(column % rows, fine_ch)
        spread_back.append(
            one_hot(iota((group, 3 * rows), 0) == (3 * a + column // rows) * fine_ch + channel)
        )
    _, z_in = place(iota((main, 3 * rows), 1) % rows, fine_ch)
    offset_back = z_in - iota((main, 3 * rows), 0) % RATIO + 1
    for b in range(3):
        chosen = dot(taps, one_hot(tap_row == tap_base + 3 * b))
        chosen = dot(pick, jnp.where(same_in, chosen, 0.0).astype(BF16)).astype(BF16)
        piece = jnp.where(offset == b, dot(chosen, spread), piece)
        chosen = dot(taps, one_hot(tap_row == 26 - tap_base - 3 * b))
        chosen = dot(pick_back, jnp.where(same_out, chosen, 0.0).astype(BF16)).astype(BF16)
        backs = [
            jnp.where(offset_back == b, dot(chosen, spread_back[a]), backs[a]) for a in range(3)
        ]
    for a in range(3):
        conv_ref[a] = piece[:, a * (wide // 3) : (a + 1) * (wide // 3)].astype(BF16)
        back_ref[a] = backs[a].astype(BF16)


def shift_rows(values, width):
    count = values.shape[0]
    block = min(count, 256)
    row = iota((block, block), 0)
    column = iota((block, block), 1)
    down = one_hot((column == row - 1) & (row % width > 0))
    up = one_hot((column == row + 1) & (row % width < width - 1))
    pieces = []
    for first in range(0, count, block):
        part = values[first : first + block]
        pieces.append(
            jnp.concatenate([dot(down, part).astype(BF16), part, dot(up, part).astype(BF16)], 1)
        )
    return jnp.concatenate(pieces, 0)


def store_padded(ref, values, width):
    rows, lanes = ref.shape
    ref[0:width] = jnp.zeros((width, lanes), BF16)
    ref[rows - width : rows] = jnp.zeros((width, lanes), BF16)
    ref[width : rows - width] = shift_rows(values, width)


def encode_kernel(
    place_ref, dark_ref, encw_ref, wide_ref, pre_ref, encoded_ref, dark3_ref, up_ref, pad_ref
):
    depth, planes, width, chans = dark_ref.shape
    main = wide_ref.shape[1]
    fine_ch = main // RATIO
    cells = planes * width
    fine_width = width * RATIO
    dark = jnp.concatenate([dark_ref[z].reshape(cells, chans) for z in range(depth)], 1)
    store_padded(dark3_ref, dark, width)
    pre = sum(
        dot_nt(dark3_ref[a * width : a * width + cells], encw_ref[a]) for a in range(3)
    )
    pre_ref[...] = pre
    encoded = jax.nn.silu(pre).astype(BF16)
    encoded_ref[...] = encoded
    pad_ref[...] = jnp.zeros(pad_ref.shape, F32)
    for z in range(depth):
        part = encoded[:, z * chans : (z + 1) * chans].astype(F32)
        pad_ref[1 : planes + 1, z + 1] = jnp.concatenate([part, part], 1).reshape(
            planes, width, 2 * chans
        )
    first_x = place_ref[0]
    first_z = place_ref[1]
    repeat = one_hot(
        iota((fine_width, width), 0) // RATIO == iota((fine_width, width), 1)
    )
    two = 2 * chans
    cells = jnp.concatenate(
        [pad_ref[first_x + dx, first_z + dz] for dx in range(3) for dz in range(3)], 1
    )
    repeated = dot(repeat, cells.astype(BF16))
    lane = iota((fine_width, two), 1) // chans
    phase = iota((fine_width, two), 0) % RATIO
    plan = ((0, RATIO - 2, 2, 0), (1, 0, RATIO, 2), (2, 0, 2, RATIO + 2))
    low = iota((fine_ch, RATIO, fine_width), 1) < 2
    for dx, first, count, base in plan:
        rows = []
        for dz in range(3):
            n = 3 * dx + dz
            cell = repeated[:, n * two : (n + 1) * two]
            rows.append(
                jnp.concatenate(
                    [jnp.where(phase == 2 * q + lane, cell, 0.0) for q in range(RATIO // 2)], 1
                )
            )
        field = dot_nt(
            wide_ref[first : first + count].reshape(count * main, RATIO * chans),
            jnp.concatenate(rows, 0).astype(BF16),
        )
        for n in range(count):
            under, own, over = (
                pltpu.roll(
                    field[n * main : (n + 1) * main, m * fine_width : (m + 1) * fine_width].reshape(
                        fine_ch, RATIO, fine_width
                    ),
                    2,
                    1,
                )
                for m in range(3)
            )
            plane = jnp.concatenate([jnp.where(low, under, own), jnp.where(low, own, over)], 1)
            store_shifts(up_ref, base + n, plane.reshape(fine_ch * SPAN, fine_width))


def decode_kernel(
    cot_ref, low_ref, high_ref, face_ref, corner_ref, conv_ref, up_ref, grad_ref, total_ref
):
    fine_ch, planes, depth, width = cot_ref.shape
    main = fine_ch * depth
    rows = conv_ref.shape[1]
    wide = (planes + 2) * width
    own = planes * width
    pre = sum(dot(conv_ref[a], up_ref[:, a * width : a * width + wide]) for a in range(3))
    row = iota((main, main), 0)
    column = iota((main, main), 1)
    turn = one_hot((row % fine_ch == column // planes) & (row // fine_ch == column % planes))
    faces = [
        dot(turn, face_ref[side].astype(F32).reshape(main, width).astype(BF16))
        for side in range(2)
    ]
    for x in range(planes + 2):
        if x == 0:
            inner = low_ref[...]
            edge = [corner_ref[0, side].astype(F32) for side in range(2)]
        elif x == planes + 1:
            inner = high_ref[...]
            edge = [corner_ref[1, side].astype(F32) for side in range(2)]
        else:
            inner = cot_ref[:, x - 1]
            edge = [face[(x - 1) * fine_ch : x * fine_ch] for face in faces]
        cot = jnp.concatenate([inner.astype(F32).reshape(main, width)] + edge, 0)
        grad = (cot * slope_of(pre[:, x * width : (x + 1) * width])).astype(BF16)
        store_shifts(grad_ref, x, grad.astype(F32))
    grads = jnp.concatenate(
        [grad_ref[e * rows : e * rows + main, width : width + own] for e in range(3)], 0
    )
    taps = fine_ch * SPAN
    shape = (3 * main, taps)
    offset = iota(shape, 1) % SPAN - 2 - iota(shape, 0) % RATIO + 1
    sums = []
    for a in range(3):
        fields = up_ref[taps : 2 * taps, (a + 1) * width : (a + 1) * width + own]
        product = dot_nt(grads, fields)
        for b in range(3):
            kept = jnp.where(offset == b, product, 0.0)
            sums.append(jnp.sum(kept.reshape(3 * fine_ch, RATIO, taps), 1))
    fold = jnp.where(iota((fine_ch, taps), 1) // SPAN == iota((fine_ch, taps), 0), 1.0, 0.0)
    total_ref[...] = lax.dot_general(
        fold,
        jnp.concatenate(sums, 0),
        (((1,), (1,)), ((), ())),
        precision=lax.Precision.HIGHEST,
        preferred_element_type=F32,
    )


def spread_kernel(cot_ref, grad_ref, back_ref, wide_ref, send_ref):
    fine_ch, planes, depth, width = cot_ref.shape
    main = fine_ch * depth
    own = planes * width
    chans = wide_ref.shape[2] // RATIO
    owners, chunk, _ = send_ref.shape
    span = chunk - RATIO
    back = sum(dot(back_ref[a], grad_ref[:, a * width : a * width + own]) for a in range(3))
    cot = jnp.concatenate(
        [cot_ref[:, x].astype(F32).reshape(main, width) for x in range(planes)], 1
    )
    up = (cot + back).astype(BF16)
    row = iota((main, main), 0)
    column = iota((main, main), 1)
    turn = one_hot((row % fine_ch == column // RATIO) & (row // fine_ch == column % RATIO))
    turned = dot(turn, up).astype(BF16)
    parts = dot_tn(
        jnp.concatenate([up[:, x * width : (x + 1) * width] for x in range(planes)], 0),
        wide_ref[...].reshape(planes * main, RATIO * chans),
    )
    two = 2 * chans
    phase = iota((width, two), 0) % RATIO
    lane = iota((width, two), 1) // chans
    both = sum(
        jnp.where(phase == 2 * q + lane, parts[:, q * two : (q + 1) * two], 0.0)
        for q in range(RATIO // 2)
    )
    cells = jnp.sum((both + pltpu.roll(both, chans, 1)).reshape(-1, RATIO, two), 1)
    half = cells.shape[0] // 2
    cells = jnp.where(iota((half, two), 1) < chans, cells[:half], cells[half:]).astype(BF16)
    for owner in range(owners):
        first = owner * RATIO * RATIO // owners
        x = first // RATIO
        top = first % RATIO * fine_ch
        send_ref[owner, :span] = turned[top : top + span, x * width : (x + 1) * width]
        send_ref[owner, span:] = cells


def widen_kernel(place_ref, encoded_ref, pre_ref, enc_ref, out_ref, slope_ref, taps_ref):
    cells, lanes = encoded_ref.shape
    chans = enc_ref.shape[1]
    depth = lanes // chans
    block = 32
    repeat = one_hot(
        iota((block * RATIO, block), 0) // RATIO == iota((block * RATIO, block), 1)
    )
    for first in range(0, cells, block):
        out_ref[first * RATIO : (first + block) * RATIO] = dot(
            repeat, encoded_ref[first : first + block]
        ).astype(BF16)
    slope_ref[...] = slope_of(pre_ref[...])
    own_z = place_ref[1]
    for a in range(3):
        for e in range(3):
            for z in range(depth):
                b = z - own_z + 1
                tap = enc_ref[26 - (9 * a + 3 * jnp.clip(b, 0, 2) + e)]
                first = (3 * e * depth + 3 * z) * chans // 3
                taps_ref[a, first : first + chans] = jnp.where(
                    (b >= 0) & (b <= 2), tap.astype(F32), 0.0
                ).astype(BF16)


def finish_kernel(
    got_ref, spread_ref, slope_ref, dark3_ref, taps_ref, dark_out, enc_out, up_out, pad_ref, *, scale
):
    owners, chunk, fine_width = got_ref.shape
    cells, lanes = slope_ref.shape
    chans = taps_ref.shape[2]
    depth = lanes // chans
    planes = owners // depth
    width = cells // planes
    span = chunk - RATIO
    fine_ch = up_out.shape[1]
    rows = []
    for x in range(planes):
        parts = [got_ref[x * depth + z, span:].astype(F32) for z in range(depth)]
        for half in range(2):
            rows.append(
                jnp.concatenate([part[:, half * chans : (half + 1) * chans] for part in parts], 1)
            )
    grad = (jnp.concatenate(rows, 0) * slope_ref[...]).astype(BF16)
    store_padded(pad_ref, grad, width)
    dark_out[...] = sum(
        dot(pad_ref[a * width : a * width + cells], taps_ref[a]) for a in range(3)
    ).reshape(planes, width, chans)
    turned = grad.astype(F32).T.astype(BF16)
    for a in range(3):
        product = dot(turned, dark3_ref[a * width : a * width + cells]) * scale
        for b in range(3):
            for e in range(3):
                total = None
                for z in range(depth):
                    z_in = z + b - 1
                    if 0 <= z_in < depth:
                        first = (e * depth + z_in) * chans
                        part = product[z * chans : (z + 1) * chans, first : first + chans]
                        total = part if total is None else total + part
                enc_out[9 * a + 3 * b + e] = (
                    jnp.zeros((chans, chans), F32) if total is None else total
                )
    pairs = span // fine_ch
    lane = iota((RATIO * fine_ch, fine_width), 1) % RATIO
    masks = one_hot(lane == iota((RATIO * fine_ch, fine_width), 0) // fine_ch)
    sums = None
    for z in range(depth):
        pieces = []
        for x in range(planes):
            arrived = got_ref[x * depth + z, :span]
            pieces.append(
                jnp.concatenate(
                    [
                        jnp.concatenate([arrived[p * fine_ch : (p + 1) * fine_ch]] * RATIO, 0)
                        * masks
                        for p in range(pairs)
                    ],
                    0,
                )
            )
        part = dot(jnp.concatenate(pieces, 1), spread_ref[...])
        part = part[:, z * chans : (z + 1) * chans]
        sums = part if sums is None else sums + part
    up_out[...] = (sums * scale).reshape(pairs * RATIO, fine_ch, chans)


def call(kernel, out_shape, args, scratch=(), scalars=0, flops=1e8):
    specs = [pl.BlockSpec(memory_space=pltpu.SMEM)] * scalars
    specs += [pl.BlockSpec(memory_space=VMEM)] * (len(args) - scalars)
    return pl.pallas_call(
        kernel,
        out_shape=[jax.ShapeDtypeStruct(*s) for s in out_shape],
        in_specs=specs,
        out_specs=[pl.BlockSpec(memory_space=VMEM)] * len(out_shape),
        scratch_shapes=list(scratch),
        compiler_params=pltpu.CompilerParams(vmem_limit_bytes=VMEM_LIMIT),
        cost_estimate=pl.CostEstimate(
            flops=int(flops), bytes_accessed=2_000_000, transcendentals=0
        ),
    )(*args)


def shift(block, axis, by):
    count = lax.axis_size(axis)
    pairs = [(i, i + by) for i in range(count) if 0 <= i + by < count]
    return lax.ppermute(block, axis, pairs)


def sum_step(value, step):
    count = lax.axis_size(AXES)
    return value + lax.ppermute(value, AXES, [(i, i ^ step) for i in range(count)])


def exchange_depth(dark_rows, cotangent):
    count = lax.axis_size("narrow")
    last = cotangent.shape[2] - 1
    if count == 2:
        first = lax.axis_index("narrow") == 0
        swap = [(0, 1), (1, 0)]
        other = lax.ppermute(dark_rows, "narrow", swap)
        face = lax.dynamic_index_in_dim(cotangent, jnp.where(first, last, 0), 2, False)
        face = lax.ppermute(face, "narrow", swap)
        none = jnp.zeros_like(face)
        planes = jnp.stack(
            [jnp.where(first, dark_rows, other), jnp.where(first, other, dark_rows)], 0
        )
        low, high = jnp.where(first, none, face), jnp.where(first, face, none)
    else:
        planes = lax.all_gather(dark_rows, "narrow", axis=0)
        low = shift(cotangent[:, :, last], "narrow", 1)
        high = shift(cotangent[:, :, 0], "narrow", -1)
    return planes, jnp.stack([low, high], 0)


def exchange_width(cotangent, faces):
    count = lax.axis_size("wide")
    last = cotangent.shape[1] - 1
    even = lax.axis_index("wide") % 2 == 0
    got = []
    for odd, plane in ((0, jnp.where(even, last, 0)), (1, jnp.where(even, 0, last))):
        pairs = [(i, i + 1) for i in range(odd, count - 1, 2)]
        pairs += [(target, source) for source, target in pairs]
        send = (
            lax.dynamic_index_in_dim(cotangent, plane, 1, False),
            lax.dynamic_index_in_dim(faces, plane, 2, False),
        )
        got.append([lax.ppermute(part, "wide", pairs) for part in send])
    low = [jnp.where(even, second, first) for first, second in zip(*got)]
    high = [jnp.where(even, first, second) for first, second in zip(*got)]
    return low[0], high[0], jnp.stack([low[1], high[1]], 0)


def on_device(dark, w_enc, up_weight, w_dec, cotangent):
    chans, planes, own_depth, width = dark.shape
    fine_ch, own_fine, fine_depth, fine_width = cotangent.shape
    subs = up_weight.shape[0]
    depth = lax.axis_size("narrow")
    owners = lax.axis_size(AXES)
    cells = planes * width
    lanes = depth * chans
    own_rows = subs // owners
    where = jnp.stack([lax.axis_index("wide"), lax.axis_index("narrow")]).astype(jnp.int32)

    dark_planes, faces = exchange_depth(dark[:, :, 0].transpose(1, 2, 0), cotangent)
    x_low, x_high, corners = exchange_width(cotangent, faces)

    rows = fine_ch * (RATIO + 2)
    taps = fine_ch * SPAN
    main = fine_ch * RATIO
    wide_table, conv, back, enc_weights = call(
        prepare_kernel,
        [
            ((RATIO, main, RATIO * chans), BF16),
            ((3, rows, 3 * taps), BF16),
            ((3, main, 3 * rows), BF16),
            ((3, lanes, 3 * lanes), BF16),
        ],
        (up_weight.transpose(1, 2, 0), w_dec.transpose(1, 2, 0), w_enc),
        flops=2e9,
    )
    enc_pre, encoded, dark3, upsampled = call(
        encode_kernel,
        [
            ((cells, lanes), F32),
            ((cells, lanes), BF16),
            ((cells + 2 * width, 3 * lanes), BF16),
            ((3 * taps, (RATIO + 4) * fine_width), BF16),
        ],
        (where, dark_planes, enc_weights, wide_table),
        scratch=[VMEM((planes + 2, depth + 2, width, 2 * chans), F32)],
        scalars=1,
        flops=2e9,
    )
    dec_grad, dec_sum = call(
        decode_kernel,
        [((3 * rows, (RATIO + 2) * fine_width), BF16), ((fine_ch, 27 * fine_ch), F32)],
        (cotangent, x_low, x_high, faces, corners, conv, upsampled),
        flops=2e9,
    )
    chunk = max(1, RATIO * RATIO // owners) * fine_ch + RATIO
    (send,) = call(
        spread_kernel,
        [((owners, chunk, fine_width), BF16)],
        (cotangent, dec_grad, back, wide_table),
        flops=2e9,
    )
    steps = [1 << n for n in range(owners.bit_length() - 1)]
    if owners & (owners - 1):
        dec_sum = lax.psum(dec_sum, AXES)
        steps = []
    steps = sorted(steps, key=lambda step: (step != depth, step))
    for step in steps[:1]:
        dec_sum = sum_step(dec_sum, step)
    send, dec_sum = lax.optimization_barrier((send, dec_sum))
    got = lax.all_to_all(send, AXES, 0, 0, tiled=True)
    for step in steps[1:]:
        dec_sum = sum_step(dec_sum, step)
    enc_spread, enc_slope, enc_taps = call(
        widen_kernel,
        [
            ((cells * RATIO, lanes), BF16),
            ((cells, lanes), F32),
            ((3, 3 * lanes, chans), BF16),
        ],
        (where, encoded, enc_pre, w_enc),
        scalars=1,
        flops=1e9,
    )
    coarse_scale = 1.0 / math.sqrt(cells * depth)
    fine_scale = 1.0 / math.sqrt(cells * depth * subs)
    pairs = (chunk - RATIO) // fine_ch
    grad_dark, grad_enc, grad_up = call(
        functools.partial(finish_kernel, scale=coarse_scale),
        [
            ((planes, width, chans), F32),
            ((27, chans, chans), F32),
            ((pairs * RATIO, fine_ch, chans), F32),
        ],
        (got, enc_spread, enc_slope, dark3, enc_taps),
        scratch=[VMEM((cells + 2 * width, 3 * lanes), BF16)],
        flops=2e9,
    )
    if own_rows < pairs * RATIO:
        own = lax.axis_index(AXES) * own_rows % RATIO
        grad_up = lax.dynamic_slice_in_dim(grad_up, own, own_rows, 0)
    grad_dec = (
        dec_sum.reshape(fine_ch, 3, 3, 3, fine_ch)[:, :, :, ::-1]
        .transpose(1, 2, 3, 4, 0)
        .reshape(27, fine_ch, fine_ch)
    ) * fine_scale
    return grad_dark.transpose(2, 0, 1)[:, :, None], grad_enc, grad_up, grad_dec


def solution(mesh):
    in_specs = (P(None, None, "narrow", None), P(), P(), P(), P(None, "wide", "narrow", None))
    out_specs = (P(None, None, "narrow", None), P(), P(("wide", "narrow"), None, None), P())
    return jax.shard_map(
        on_device, mesh=mesh, in_specs=in_specs, out_specs=out_specs, check_vma=False
    )
```

```python
import functools
import math

import jax
import jax.numpy as jnp
from jax import lax
from jax.experimental import pallas as pl
from jax.experimental.pallas import tpu as pltpu
from jax.sharding import PartitionSpec as P

RATIO = 8
SPAN = 16
F32 = jnp.float32
BF16 = jnp.bfloat16
VMEM_LIMIT = 48 * 1024 * 1024
VMEM = pltpu.VMEM
AXES = ("wide", "narrow")


def slope_of(values):
    sigma = jax.nn.sigmoid(values)
    return sigma * (1.0 + values * (1.0 - sigma))


def dot(left, right):
    return jnp.dot(left, right, preferred_element_type=F32)


def dot_nt(left, right):
    return lax.dot_general(left, right, (((1,), (1,)), ((), ())), preferred_element_type=F32)


def dot_tn(left, right):
    return lax.dot_general(left, right, (((0,), (0,)), ((), ())), preferred_element_type=F32)


def iota(shape, dim):
    return lax.broadcasted_iota(jnp.int32, shape, dim)


def row_index(count):
    return iota((count, 1), 0)


def lane_index(count):
    return iota((1, count), 1)


def one_hot(condition):
    return jnp.where(condition, 1.0, 0.0).astype(BF16)


def place(index, fine_ch):
    main = fine_ch * RATIO
    over = index - main
    channel = jnp.where(index < main, index // RATIO, over % fine_ch)
    z = jnp.where(index < main, index % RATIO, jnp.where(over < fine_ch, -1, RATIO))
    return channel, z


def lane_shift(values, by):
    width = values.shape[1]
    lane = iota(values.shape, 1)
    if by > 0:
        return jnp.where(lane < by, 0.0, pltpu.roll(values, by, 1))
    return jnp.where(lane >= width + by, 0.0, pltpu.roll(values, width + by, 1))


def store_shifts(ref, block, values):
    rows, width = values.shape
    lanes = slice(block * width, (block + 1) * width)
    ref[0:rows, lanes] = lane_shift(values, 1).astype(BF16)
    ref[rows : 2 * rows, lanes] = values.astype(BF16)
    ref[2 * rows : 3 * rows, lanes] = lane_shift(values, -1).astype(BF16)


def taps_kernel(dec_ref, conv_ref, back_ref):
    fine_ch = dec_ref.shape[0]
    rows = fine_ch * (RATIO + 2)
    square = fine_ch * fine_ch
    group = 9 * fine_ch
    block = 256
    column = lane_index(6 * block)
    rest = column % block
    base = 9 * (rest // (3 * fine_ch)) + (rest // fine_ch) % 3 + 3 * (column // block % 3)
    tap = jnp.where(column < 3 * block, base, 26 - base)
    chosen_taps = one_hot(iota((27, 6 * block), 0) == jnp.where(rest < group, tap, -1))
    cell = row_index(square)
    last_index = iota((square, block), 1) % fine_ch
    same_in = last_index == cell % fine_ch
    same_out = last_index == cell // fine_ch
    shape = (fine_ch, square)
    pick_out = one_hot(iota(shape, 0) == lane_index(square) // fine_ch)
    pick_in = one_hot(iota(shape, 0) == lane_index(square) % fine_ch)
    wide = group * SPAN
    spread = one_hot(iota((block, wide), 0) == lane_index(wide) // SPAN)
    back_wide = 9 * rows
    column = lane_index(back_wide)
    channel, _ = place(column % rows, fine_ch)
    spread_back = one_hot(iota((block, back_wide), 0) == column // rows * fine_ch + channel)
    chosen = dot(dec_ref[...].reshape(square, 27), chosen_taps)
    taps = []
    for n in range(6):
        part = chosen[:, n * block : (n + 1) * block]
        part = jnp.where(same_in if n < 3 else same_out, part, 0.0).astype(BF16)
        taps.append(dot(pick_out if n < 3 else pick_in, part).astype(BF16))
    forward = dot(jnp.concatenate(taps[:3], 0), spread)
    backward = dot(jnp.concatenate(taps[3:], 0), spread_back)

    def banded(parts, offset):
        total = jnp.zeros(offset.shape, F32)
        for b in range(3):
            total = jnp.where(offset == b, parts[b], total)
        return total

    def rows_of(field, channel):
        shape = (RATIO, field.shape[1])
        return [
            jnp.broadcast_to(field[b * fine_ch + channel : b * fine_ch + channel + 1], shape)
            for b in range(3)
        ]

    slot = iota((RATIO, 128), 1) % SPAN
    offset = jnp.concatenate([10 - slot - iota((RATIO, 128), 0)] * (wide // 128), 1)
    pieces = [banded(rows_of(forward, o), offset) for o in range(fine_ch)]
    slot = jnp.concatenate([iota((fine_ch, 128), 1) % SPAN] * (wide // 128), 1)
    parts = [forward[b * fine_ch : (b + 1) * fine_ch] for b in range(3)]
    pieces += [banded(parts, 11 - slot), banded(parts, 2 - slot)]
    field = jnp.concatenate(pieces, 0).astype(BF16)
    for a in range(3):
        conv_ref[a] = field[:, a * (wide // 3) : (a + 1) * (wide // 3)]
    _, z_in = place(lane_index(back_wide) % rows, fine_ch)
    offset = z_in - iota((RATIO, back_wide), 0) + 1
    back_ref[...] = jnp.concatenate(
        [banded(rows_of(backward, c), offset) for c in range(fine_ch)], 0
    ).astype(BF16)


def table_kernel(place_ref, table_ref, cot_ref, wide_ref, first_ref, second_ref):
    last = cot_ref.shape[1] - 1
    even = lax.rem(place_ref[0], 2) == 0
    first_ref[...] = cot_ref[:, jnp.where(even, last, 0)]
    second_ref[...] = cot_ref[:, jnp.where(even, 0, last)]
    fine_ch, chans, subs = table_ref.shape
    pairs = RATIO * RATIO
    row = row_index(subs)
    position = row % pairs // RATIO * pairs + (RATIO - 1 - row % RATIO) * RATIO + row // pairs
    pick = one_hot(iota((subs, subs), 1) == position)
    turned = dot_nt(pick, table_ref[...].reshape(fine_ch * chans, subs))
    two = 2 * chans
    low = iota((pairs, two), 1) < chans
    for p in range(fine_ch // 2):
        lanes = slice(p * two, (p + 1) * two)
        for q in range(RATIO // 2):
            even = turned[2 * q * pairs : (2 * q + 1) * pairs, lanes]
            odd = turned[(2 * q + 1) * pairs : (2 * q + 2) * pairs, lanes]
            first = jnp.where(low, even, pltpu.roll(odd, chans, 1))
            second = jnp.where(low, pltpu.roll(even, chans, 1), odd)
            both = jnp.concatenate(
                [first.reshape(RATIO, RATIO, two), second.reshape(RATIO, RATIO, two)], 1
            )
            wide_ref[:, p * SPAN : (p + 1) * SPAN, q * two : (q + 1) * two] = both.astype(BF16)


def shift_rows(values, width):
    count = values.shape[0]
    block = min(count, 256)
    row = iota((block, block), 0)
    column = iota((block, block), 1)
    down = one_hot((column == row - 1) & (row % width > 0))
    up = one_hot((column == row + 1) & (row % width < width - 1))
    pieces = []
    for first in range(0, count, block):
        part = values[first : first + block]
        pieces.append(
            jnp.concatenate([dot(down, part).astype(BF16), part, dot(up, part).astype(BF16)], 1)
        )
    return jnp.concatenate(pieces, 0)


def store_padded(ref, values, width):
    rows, lanes = ref.shape
    ref[0:width] = jnp.zeros((width, lanes), BF16)
    ref[rows - width : rows] = jnp.zeros((width, lanes), BF16)
    ref[width : rows - width] = shift_rows(values, width)


def encode_kernel(
    place_ref, enc_ref, wide_ref, *refs, depth
):
    *dark_refs, pre_ref, encoded_ref, dark3_ref, up_ref, pad_ref = refs
    planes, width, chans = dark_refs[0].shape[-3:]
    main = wide_ref.shape[1]
    fine_ch = main // RATIO
    cells = planes * width
    fine_width = width * RATIO
    blank = jnp.zeros((chans, chans), BF16)
    weights = []
    for a in range(3):
        rows = []
        for z_out in range(depth):
            blocks = []
            for e in range(3):
                for z_in in range(depth):
                    b = z_in - z_out + 1
                    blocks.append(enc_ref[9 * a + 3 * b + e] if 0 <= b < 3 else blank)
            rows.append(jnp.concatenate(blocks, 1))
        weights.append(jnp.concatenate(rows, 0))
    if len(dark_refs) == 2:
        own, other = (ref[...].reshape(cells, chans) for ref in dark_refs)
        first = place_ref[1] == 0
        parts = [jnp.where(first, own, other), jnp.where(first, other, own)]
    else:
        parts = [dark_refs[0][z].reshape(cells, chans) for z in range(depth)]
    dark = jnp.concatenate(parts, 1)
    store_padded(dark3_ref, dark, width)
    pre = sum(
        dot_nt(dark3_ref[a * width : a * width + cells], weights[a]) for a in range(3)
    )
    pre_ref[...] = pre
    encoded = jax.nn.silu(pre).astype(BF16)
    encoded_ref[...] = encoded
    pad_ref[...] = jnp.zeros(pad_ref.shape, F32)
    for z in range(depth):
        part = encoded[:, z * chans : (z + 1) * chans].astype(F32)
        pad_ref[1 : planes + 1, z + 1] = jnp.concatenate([part, part], 1).reshape(
            planes, width, 2 * chans
        )
    first_x = place_ref[0]
    first_z = place_ref[1]
    repeat = one_hot(
        iota((fine_width, width), 0) // RATIO == iota((fine_width, width), 1)
    )
    two = 2 * chans
    cells = jnp.concatenate(
        [pad_ref[first_x + dx, first_z + dz] for dx in range(3) for dz in range(3)], 1
    )
    repeated = dot(repeat, cells.astype(BF16))
    lane = iota((fine_width, two), 1) // chans
    phase = iota((fine_width, two), 0) % RATIO
    plan = ((0, RATIO - 2, 2, 0), (1, 0, RATIO, 2), (2, 0, 2, RATIO + 2))
    low = iota((fine_ch, RATIO, fine_width), 1) < 2
    for dx, first, count, base in plan:
        rows = []
        for dz in range(3):
            n = 3 * dx + dz
            cell = repeated[:, n * two : (n + 1) * two]
            rows.append(
                jnp.concatenate(
                    [jnp.where(phase == 2 * q + lane, cell, 0.0) for q in range(RATIO // 2)], 1
                )
            )
        field = dot_nt(
            wide_ref[first : first + count].reshape(count * main, RATIO * chans),
            jnp.concatenate(rows, 0).astype(BF16),
        )
        for n in range(count):
            under, own, over = (
                pltpu.roll(
                    field[n * main : (n + 1) * main, m * fine_width : (m + 1) * fine_width].reshape(
                        fine_ch, RATIO, fine_width
                    ),
                    2,
                    1,
                )
                for m in range(3)
            )
            plane = jnp.concatenate([jnp.where(low, over, own), jnp.where(low, own, under)], 1)
            store_shifts(up_ref, base + n, plane.reshape(fine_ch * SPAN, fine_width))


def decode_kernel(
    place_ref, cot_ref, x_low_ref, x_high_ref, z_low_ref, z_high_ref, conv_ref, up_ref,
    grad_ref, total_ref, *, planes_z
):
    fine_ch, planes, depth, width = cot_ref.shape
    main = fine_ch * depth
    rows = conv_ref.shape[1]
    wide = (planes + 2) * width
    own = planes * width
    pre = sum(dot(conv_ref[a], up_ref[:, a * width : a * width + wide]) for a in range(3))
    own_z = place_ref[1]
    valid = (own_z > 0, own_z < planes_z - 1)
    shape = (main, main)
    turn = iota(shape, 1) == row_index(main) % fine_ch * planes + row_index(main) // fine_ch
    sides = [
        dot(one_hot(turn & valid[side]), ref[...].astype(F32).reshape(main, width).astype(BF16))
        for side, ref in enumerate((z_low_ref, z_high_ref))
    ]
    for x in range(planes + 2):
        if 0 < x <= planes:
            inner = cot_ref[:, x - 1].astype(F32).reshape(main, width)
            edge = [side[(x - 1) * fine_ch : x * fine_ch] for side in sides]
        else:
            outer = x_low_ref if x == 0 else x_high_ref
            inner = outer[:main].astype(F32)
            edge = []
            for side in range(2):
                first = main + side * (outer.shape[0] - main - fine_ch)
                corner = outer[first : first + fine_ch].astype(F32)
                edge.append(jnp.where(valid[side], corner, 0.0))
        cot = jnp.concatenate([inner] + edge, 0)
        grad = (cot * slope_of(pre[:, x * width : (x + 1) * width])).astype(BF16)
        store_shifts(grad_ref, x, grad.astype(F32))
    grads = jnp.concatenate(
        [grad_ref[e * rows : e * rows + main, width : width + own] for e in (2, 1, 0)], 0
    )
    taps = fine_ch * SPAN
    sums = []
    for a in range(3):
        fields = up_ref[taps : 2 * taps, (a + 1) * width : (a + 1) * width + own]
        product = dot_nt(grads, fields)
        halves = []
        for first in range(0, taps, 128):
            part = product[:, first : first + 128].reshape(3 * fine_ch, RATIO, 128)
            halves.append(jnp.sum(pltpu.roll(part, 0, 2, stride=1, stride_axis=1), 1))
        sums.append(jnp.concatenate(halves, 1))
    shape = (3 * fine_ch, taps)
    fold = jnp.where(
        (iota(shape, 1) // SPAN == iota(shape, 0) % fine_ch)
        & (iota(shape, 1) % SPAN == 10 - iota(shape, 0) // fine_ch),
        1.0,
        0.0,
    )
    total_ref[...] = lax.dot_general(
        fold,
        jnp.concatenate(sums, 0),
        (((1,), (1,)), ((), ())),
        precision=lax.Precision.HIGHEST,
        preferred_element_type=F32,
    )


def spread_kernel(cot_ref, grad_ref, back_ref, wide_ref, send_ref):
    fine_ch, planes, depth, width = cot_ref.shape
    main = fine_ch * depth
    own = planes * width
    chans = wide_ref.shape[2] // RATIO
    owners, chunk, _ = send_ref.shape
    span = chunk - RATIO
    taps = grad_ref.shape[0]
    back = sum(
        dot(back_ref[:, a * taps : (a + 1) * taps], grad_ref[:, a * width : a * width + own])
        for a in range(3)
    )
    cot = jnp.concatenate(
        [cot_ref[:, x].astype(F32).reshape(main, width) for x in range(planes)], 1
    )
    up = (cot + back).astype(BF16)
    row = iota((main, main), 0)
    column = iota((main, main), 1)
    turn = one_hot((row % fine_ch == column // RATIO) & (row // fine_ch == column % RATIO))
    turned = dot(turn, up).astype(BF16)
    flip = one_hot(
        (row // RATIO == column // RATIO) & (row % RATIO + column % RATIO == RATIO - 1)
    )
    flipped = dot(flip, up).astype(BF16)
    parts = dot_tn(
        jnp.concatenate([flipped[:, x * width : (x + 1) * width] for x in range(planes)], 0),
        wide_ref[...].reshape(planes * main, RATIO * chans),
    )
    two = 2 * chans
    phase = iota((width, two), 0) % RATIO
    lane = iota((width, two), 1) // chans
    both = sum(
        jnp.where(phase == 2 * q + lane, parts[:, q * two : (q + 1) * two], 0.0)
        for q in range(RATIO // 2)
    )
    cells = jnp.sum((both + pltpu.roll(both, chans, 1)).reshape(-1, RATIO, two), 1)
    half = cells.shape[0] // 2
    cells = jnp.where(iota((half, two), 1) < chans, cells[:half], cells[half:]).astype(BF16)
    for owner in range(owners):
        first = owner * RATIO * RATIO // owners
        x = first // RATIO
        top = first % RATIO * fine_ch
        send_ref[owner, :span] = turned[top : top + span, x * width : (x + 1) * width]
        send_ref[owner, span:] = cells


def widen_kernel(
    place_ref, encoded_ref, pre_ref, enc_ref, out_ref, slope_ref, taps_ref, order_ref
):
    cells, lanes = encoded_ref.shape
    chans = enc_ref.shape[1]
    depth = lanes // chans
    block = 32
    repeat = one_hot(
        iota((block * RATIO, block), 0) // RATIO == iota((block * RATIO, block), 1)
    )
    for first in range(0, cells, block):
        out_ref[first * RATIO : (first + block) * RATIO] = dot(
            repeat, encoded_ref[first : first + block]
        ).astype(BF16)
    slope_ref[...] = slope_of(pre_ref[...])
    own_z = place_ref[1]
    for a in range(3):
        for e in range(3):
            for z in range(depth):
                b = z - own_z + 1
                tap = enc_ref[26 - (9 * a + 3 * jnp.clip(b, 0, 2) + e)]
                first = (3 * e * depth + 3 * z) * chans // 3
                taps_ref[a, first : first + chans] = jnp.where(
                    (b >= 0) & (b <= 2), tap.astype(F32), 0.0
                ).astype(BF16)
    shape = order_ref.shape[1:]
    fine_ch = shape[0] // 9
    step = shape[1] // fine_ch
    row = row_index(shape[0])
    column = iota(shape, 1)
    tap = row // fine_ch // 3 * 9 + row // fine_ch % 3
    for b in range(3):
        order_ref[b] = one_hot(column == row % fine_ch * step + tap + 3 * b)


def final_kernel(own_ref, other_ref, order_ref, done_ref, out_ref, *, scale):
    total = (own_ref[...] + other_ref[...]) * scale
    fine_ch = out_ref.shape[0]
    high = total.astype(BF16)
    rest = total - high.astype(F32)
    middle = rest.astype(BF16)
    low = (rest - middle.astype(F32)).astype(BF16)
    field = 0.0
    for b in range(3):
        rows = slice(b * fine_ch, (b + 1) * fine_ch)
        field = field + dot(jnp.concatenate([high[rows], middle[rows], low[rows]], 0), order_ref[b])
    field = field[:fine_ch] + field[fine_ch : 2 * fine_ch] + field[2 * fine_ch :]
    step = field.shape[1] // fine_ch
    for o in range(fine_ch):
        first = o * step // 128 * 128
        part = field[:, first : first + 128]
        if o * step > first:
            part = pltpu.roll(part, 128 - (o * step - first), 1)
        out_ref[o] = part[:, :27]


def finish_kernel(
    got_ref, spread_ref, slope_ref, dark3_ref, taps_ref,
    dark_out, enc_out, up_out, done_ref, pad_ref, *, scale
):
    done_ref[...] = jnp.zeros(done_ref.shape, F32)
    owners, chunk, fine_width = got_ref.shape
    cells, lanes = slope_ref.shape
    chans = taps_ref.shape[2]
    depth = lanes // chans
    planes = owners // depth
    width = cells // planes
    span = chunk - RATIO
    fine_ch = up_out.shape[1]
    rows = []
    for x in range(planes):
        parts = [got_ref[x * depth + z, span:].astype(F32) for z in range(depth)]
        for half in range(2):
            rows.append(
                jnp.concatenate([part[:, half * chans : (half + 1) * chans] for part in parts], 1)
            )
    grad = (jnp.concatenate(rows, 0) * slope_ref[...]).astype(BF16)
    store_padded(pad_ref, grad, width)
    dark_out[...] = sum(
        dot(pad_ref[a * width : a * width + cells], taps_ref[a]) for a in range(3)
    ).reshape(planes, width, chans)
    turned = grad.astype(F32).T.astype(BF16)
    for a in range(3):
        product = dot(turned, dark3_ref[a * width : a * width + cells]) * scale
        for b in range(3):
            for e in range(3):
                total = None
                for z in range(depth):
                    z_in = z + b - 1
                    if 0 <= z_in < depth:
                        first = (e * depth + z_in) * chans
                        part = product[z * chans : (z + 1) * chans, first : first + chans]
                        total = part if total is None else total + part
                enc_out[9 * a + 3 * b + e] = (
                    jnp.zeros((chans, chans), F32) if total is None else total
                )
    pairs = span // fine_ch
    lane = iota((RATIO * fine_ch, fine_width), 1) % RATIO
    masks = one_hot(lane == iota((RATIO * fine_ch, fine_width), 0) // fine_ch)
    sums = None
    for z in range(depth):
        pieces = []
        for x in range(planes):
            arrived = got_ref[x * depth + z, :span]
            pieces.append(
                jnp.concatenate(
                    [
                        jnp.concatenate([arrived[p * fine_ch : (p + 1) * fine_ch]] * RATIO, 0)
                        * masks
                        for p in range(pairs)
                    ],
                    0,
                )
            )
        part = dot(jnp.concatenate(pieces, 1), spread_ref[...])
        part = part[:, z * chans : (z + 1) * chans]
        sums = part if sums is None else sums + part
    up_out[...] = (sums * scale).reshape(pairs * RATIO, fine_ch, chans)


def call(kernel, out_shape, args, scratch=(), scalars=0, flops=1e8):
    specs = [pl.BlockSpec(memory_space=pltpu.SMEM)] * scalars
    specs += [pl.BlockSpec(memory_space=VMEM)] * (len(args) - scalars)
    return pl.pallas_call(
        kernel,
        out_shape=[jax.ShapeDtypeStruct(*s) for s in out_shape],
        in_specs=specs,
        out_specs=[pl.BlockSpec(memory_space=VMEM)] * len(out_shape),
        scratch_shapes=list(scratch),
        compiler_params=pltpu.CompilerParams(vmem_limit_bytes=VMEM_LIMIT),
        cost_estimate=pl.CostEstimate(
            flops=int(flops), bytes_accessed=2_000_000, transcendentals=0
        ),
    )(*args)


def shift(block, axis, by):
    count = lax.axis_size(axis)
    pairs = [(i, i + by) for i in range(count) if 0 <= i + by < count]
    return lax.ppermute(block, axis, pairs)


def swapped(value, step):
    count = lax.axis_size(AXES)
    return lax.ppermute(value, AXES, [(i, i ^ step) for i in range(count)])


def exchange_depth(dark_rows, cotangent):
    count = lax.axis_size("narrow")
    last = cotangent.shape[2] - 1
    if count == 2:
        swap = [(0, 1), (1, 0)]
        dark = lax.ppermute(dark_rows, "narrow", swap)
        z = jnp.where(lax.axis_index("narrow") == 0, last, 0)
        face = lax.ppermute(lax.dynamic_index_in_dim(cotangent, z, 2, False), "narrow", swap)
        return (dark_rows, dark), (face,)
    planes = lax.all_gather(dark_rows, "narrow", axis=0)
    low = shift(cotangent[:, :, last], "narrow", 1)
    return (planes,), (low, shift(cotangent[:, :, 0], "narrow", -1))


def exchange_width(planes, faces):
    count = lax.axis_size("wide")
    last = faces[0].shape[1] - 1
    even = lax.axis_index("wide") % 2 == 0
    got = []
    for odd in range(2):
        pairs = [(i, i + 1) for i in range(odd, count - 1, 2)]
        pairs += [(target, source) for source, target in pairs]
        plane = jnp.where(even, 0, last) if odd else jnp.where(even, last, 0)
        edges = [lax.dynamic_index_in_dim(face, plane, 1, False) for face in faces]
        send = jnp.concatenate([planes[odd], *edges], 0)
        got.append(lax.ppermute(send, "wide", pairs))
    return jnp.where(even, got[1], got[0]), jnp.where(even, got[0], got[1])


def on_device(dark, w_enc, up_weight, w_dec, cotangent):
    chans, planes, own_depth, width = dark.shape
    fine_ch, own_fine, fine_depth, fine_width = cotangent.shape
    subs = up_weight.shape[0]
    depth = lax.axis_size("narrow")
    owners = lax.axis_size(AXES)
    cells = planes * width
    lanes = depth * chans
    own_rows = subs // owners
    where = jnp.stack([lax.axis_index("wide"), lax.axis_index("narrow")]).astype(jnp.int32)

    dark_planes, faces = exchange_depth(dark[:, :, 0].transpose(1, 2, 0), cotangent)

    rows = fine_ch * (RATIO + 2)
    taps = fine_ch * SPAN
    main = fine_ch * RATIO
    face = (fine_ch * fine_depth, fine_width)
    conv, back = call(
        taps_kernel,
        [((3, rows, 3 * taps), BF16), ((main, 9 * rows), BF16)],
        (w_dec.transpose(1, 2, 0),),
        flops=1e9,
    )
    outer = (fine_ch, fine_depth, fine_width)
    wide_table, first_plane, second_plane = call(
        table_kernel,
        [((RATIO, main, RATIO * chans), BF16), (outer, BF16), (outer, BF16)],
        (where, up_weight.transpose(1, 2, 0), cotangent),
        scalars=1,
        flops=1e9,
    )
    outer_planes = [plane.reshape(face) for plane in (first_plane, second_plane)]
    x_low, x_high = exchange_width(outer_planes, faces)
    enc_pre, encoded, dark3, upsampled = call(
        functools.partial(encode_kernel, depth=depth),
        [
            ((cells, lanes), F32),
            ((cells, lanes), BF16),
            ((cells + 2 * width, 3 * lanes), BF16),
            ((3 * taps, (RATIO + 4) * fine_width), BF16),
        ],
        (where, w_enc, wide_table, *dark_planes),
        scratch=[VMEM((planes + 2, depth + 2, width, 2 * chans), F32)],
        scalars=1,
        flops=2e9,
    )
    dec_grad, dec_sum = call(
        functools.partial(decode_kernel, planes_z=depth),
        [((3 * rows, (RATIO + 2) * fine_width), BF16), ((3 * fine_ch, 9 * fine_ch), F32)],
        (where, cotangent, x_low, x_high, faces[0], faces[-1], conv, upsampled),
        scalars=1,
        flops=2e9,
    )
    chunk = max(1, RATIO * RATIO // owners) * fine_ch + RATIO
    (send,) = call(
        spread_kernel,
        [((owners, chunk, fine_width), BF16)],
        (cotangent, dec_grad, back, wide_table),
        flops=2e9,
    )
    steps = [1 << n for n in range(owners.bit_length() - 1)]
    if owners & (owners - 1):
        dec_sum = lax.psum(dec_sum, AXES)
        steps = []
    steps = sorted(steps)
    received = jnp.zeros_like(dec_sum)
    for n, step in enumerate(steps):
        received = swapped(dec_sum, step)
        if n < len(steps) - 1:
            dec_sum = dec_sum + received
        if n == 0:
            send, dec_sum = lax.optimization_barrier((send, dec_sum))
    got = lax.all_to_all(send, AXES, 0, 0, tiled=True)
    enc_spread, enc_slope, enc_taps, order = call(
        widen_kernel,
        [
            ((cells * RATIO, lanes), BF16),
            ((cells, lanes), F32),
            ((3, 3 * lanes, chans), BF16),
            ((3, 9 * fine_ch, 32 * fine_ch), BF16),
        ],
        (where, encoded, enc_pre, w_enc),
        scalars=1,
        flops=1e9,
    )
    coarse_scale = 1.0 / math.sqrt(cells * depth)
    fine_scale = 1.0 / math.sqrt(cells * depth * subs)
    pairs = (chunk - RATIO) // fine_ch
    grad_dark, grad_enc, grad_up, done = call(
        functools.partial(finish_kernel, scale=coarse_scale),
        [
            ((planes, width, chans), F32),
            ((27, chans, chans), F32),
            ((pairs * RATIO, fine_ch, chans), F32),
            ((8, 128), F32),
        ],
        (got, enc_spread, enc_slope, dark3, enc_taps),
        scratch=[VMEM((cells + 2 * width, 3 * lanes), BF16)],
        flops=2e9,
    )
    if own_rows < pairs * RATIO:
        own = lax.axis_index(AXES) * own_rows % RATIO
        grad_up = lax.dynamic_slice_in_dim(grad_up, own, own_rows, 0)
    (grad_dec,) = call(
        functools.partial(final_kernel, scale=fine_scale),
        [((fine_ch, fine_ch, 27), F32)],
        (dec_sum, received, order, done),
        flops=1e8,
    )
    return grad_dark.transpose(2, 0, 1)[:, :, None], grad_enc, grad_up, grad_dec.transpose(2, 0, 1)


def solution(mesh):
    in_specs = (P(None, None, "narrow", None), P(), P(), P(), P(None, "wide", "narrow", None))
    out_specs = (P(None, None, "narrow", None), P(), P(("wide", "narrow"), None, None), P())
    return jax.shard_map(
        on_device, mesh=mesh, in_specs=in_specs, out_specs=out_specs, check_vma=False
    )
```

```python
import functools
import math

import jax
import jax.numpy as jnp
from jax import lax
from jax.experimental import pallas as pl
from jax.experimental.pallas import tpu as pltpu
from jax.sharding import PartitionSpec as P

RATIO = 8
SPAN = 16
LAST_STEPS = 2
F32 = jnp.float32
BF16 = jnp.bfloat16
VMEM_LIMIT = 48 * 1024 * 1024
VMEM = pltpu.VMEM
AXES = ("wide", "narrow")


def slope_of(values):
    sigma = jax.nn.sigmoid(values)
    return sigma * (1.0 + values * (1.0 - sigma))


def dot(left, right):
    return jnp.dot(left, right, preferred_element_type=F32)


def dot_nt(left, right):
    return lax.dot_general(left, right, (((1,), (1,)), ((), ())), preferred_element_type=F32)


def dot_tn(left, right):
    return lax.dot_general(left, right, (((0,), (0,)), ((), ())), preferred_element_type=F32)


def split(values):
    high = values.astype(BF16)
    rest = values - high.astype(F32)
    middle = rest.astype(BF16)
    return high, middle, (rest - middle.astype(F32)).astype(BF16)


def iota(shape, dim):
    return lax.broadcasted_iota(jnp.int32, shape, dim)


def row_index(count):
    return iota((count, 1), 0)


def lane_index(count):
    return iota((1, count), 1)


def one_hot(condition):
    return jnp.where(condition, 1.0, 0.0).astype(BF16)


def place(index, fine_ch):
    main = fine_ch * RATIO
    over = index - main
    channel = jnp.where(index < main, index // RATIO, over % fine_ch)
    z = jnp.where(index < main, index % RATIO, jnp.where(over < fine_ch, -1, RATIO))
    return channel, z


def lane_shift(values, by):
    width = values.shape[1]
    lane = iota(values.shape, 1)
    if by > 0:
        return jnp.where(lane < by, 0.0, pltpu.roll(values, by, 1))
    return jnp.where(lane >= width + by, 0.0, pltpu.roll(values, width + by, 1))


def store_shifts(ref, block, values):
    rows, width = values.shape
    lanes = slice(block * width, (block + 1) * width)
    ref[0:rows, lanes] = lane_shift(values, 1).astype(BF16)
    ref[rows : 2 * rows, lanes] = values.astype(BF16)
    ref[2 * rows : 3 * rows, lanes] = lane_shift(values, -1).astype(BF16)


def band_taps(dec_ref, conv_ref, back_ref):
    fine_ch = dec_ref.shape[0]
    rows = fine_ch * (RATIO + 2)
    square = fine_ch * fine_ch
    group = 9 * fine_ch
    block = 256
    column = lane_index(6 * block)
    rest = column % block
    base = 9 * (rest // (3 * fine_ch)) + (rest // fine_ch) % 3 + 3 * (column // block % 3)
    tap = jnp.where(column < 3 * block, base, 26 - base)
    chosen_taps = one_hot(iota((27, 6 * block), 0) == jnp.where(rest < group, tap, -1))
    cell = row_index(square)
    last_index = iota((square, block), 1) % fine_ch
    same_in = last_index == cell % fine_ch
    same_out = last_index == cell // fine_ch
    shape = (fine_ch, square)
    pick_out = one_hot(iota(shape, 0) == lane_index(square) // fine_ch)
    pick_in = one_hot(iota(shape, 0) == lane_index(square) % fine_ch)
    wide = group * SPAN
    spread = one_hot(iota((block, wide), 0) == lane_index(wide) // SPAN)
    back_wide = 9 * rows
    column = lane_index(back_wide)
    channel, _ = place(column % rows, fine_ch)
    spread_back = one_hot(iota((block, back_wide), 0) == column // rows * fine_ch + channel)
    chosen = dot(dec_ref[...].reshape(square, 27), chosen_taps)
    taps = []
    for n in range(6):
        part = chosen[:, n * block : (n + 1) * block]
        part = jnp.where(same_in if n < 3 else same_out, part, 0.0).astype(BF16)
        taps.append(dot(pick_out if n < 3 else pick_in, part).astype(BF16))
    forward = dot(jnp.concatenate(taps[:3], 0), spread)
    backward = dot(jnp.concatenate(taps[3:], 0), spread_back)

    def banded(parts, offset):
        total = jnp.zeros(offset.shape, F32)
        for b in range(3):
            total = jnp.where(offset == b, parts[b], total)
        return total

    def rows_of(field, channel):
        shape = (RATIO, field.shape[1])
        return [
            jnp.broadcast_to(field[b * fine_ch + channel : b * fine_ch + channel + 1], shape)
            for b in range(3)
        ]

    slot = iota((RATIO, 128), 1) % SPAN
    offset = jnp.concatenate([10 - slot - iota((RATIO, 128), 0)] * (wide // 128), 1)
    pieces = [banded(rows_of(forward, o), offset) for o in range(fine_ch)]
    slot = jnp.concatenate([iota((fine_ch, 128), 1) % SPAN] * (wide // 128), 1)
    parts = [forward[b * fine_ch : (b + 1) * fine_ch] for b in range(3)]
    pieces += [banded(parts, 11 - slot), banded(parts, 2 - slot)]
    field = jnp.concatenate(pieces, 0).astype(BF16)
    for a in range(3):
        conv_ref[a] = field[:, a * (wide // 3) : (a + 1) * (wide // 3)]
    _, z_in = place(lane_index(back_wide) % rows, fine_ch)
    offset = z_in - iota((RATIO, back_wide), 0) + 1
    back_ref[...] = jnp.concatenate(
        [banded(rows_of(backward, c), offset) for c in range(fine_ch)], 0
    ).astype(BF16)


def table_kernel(
    place_ref, table_hbm, cot_hbm, wide_ref, first_ref, second_ref, table_ref, sems
):
    last = cot_hbm.shape[1] - 1
    even = lax.rem(place_ref[0], 2) == 0
    fine_ch, chans, subs = table_ref.shape
    half = fine_ch // 2
    loads = [
        pltpu.make_async_copy(
            table_hbm.at[n * half : (n + 1) * half],
            table_ref.at[n * half : (n + 1) * half],
            sems.at[n],
        )
        for n in range(2)
    ]
    planes = [
        pltpu.make_async_copy(cot_hbm.at[:, jnp.where(even, last, 0)], first_ref, sems.at[2]),
        pltpu.make_async_copy(cot_hbm.at[:, jnp.where(even, 0, last)], second_ref, sems.at[3]),
    ]
    for copy in loads + planes:
        copy.start()
    pairs = RATIO * RATIO
    row = row_index(subs)
    position = row % pairs // RATIO * pairs + (RATIO - 1 - row % RATIO) * RATIO + row // pairs
    pick = one_hot(iota((subs, subs), 1) == position)
    two = 2 * chans
    low = iota((pairs, two), 1) < chans
    for n in range(2):
        loads[n].wait()
        part = table_ref[n * half : (n + 1) * half].reshape(half * chans, subs)
        turned = dot_nt(pick, part)
        for p in range(half // 2):
            lanes = slice(p * two, (p + 1) * two)
            top = (n * half // 2 + p) * SPAN
            for q in range(RATIO // 2):
                even = turned[2 * q * pairs : (2 * q + 1) * pairs, lanes]
                odd = turned[(2 * q + 1) * pairs : (2 * q + 2) * pairs, lanes]
                first = jnp.where(low, even, pltpu.roll(odd, chans, 1))
                second = jnp.where(low, pltpu.roll(even, chans, 1), odd)
                both = jnp.concatenate(
                    [first.reshape(RATIO, RATIO, two), second.reshape(RATIO, RATIO, two)], 1
                )
                wide_ref[:, top : top + SPAN, q * two : (q + 1) * two] = both.astype(BF16)
    for copy in planes:
        copy.wait()


def shift_rows(values, width):
    count = values.shape[0]
    block = min(count, 256)
    row = iota((block, block), 0)
    column = iota((block, block), 1)
    down = one_hot((column == row - 1) & (row % width > 0))
    up = one_hot((column == row + 1) & (row % width < width - 1))
    pieces = []
    for first in range(0, count, block):
        part = values[first : first + block]
        pieces.append(
            jnp.concatenate([dot(down, part).astype(BF16), part, dot(up, part).astype(BF16)], 1)
        )
    return jnp.concatenate(pieces, 0)


def store_padded(ref, values, width):
    rows, lanes = ref.shape
    ref[0:width] = jnp.zeros((width, lanes), BF16)
    ref[rows - width : rows] = jnp.zeros((width, lanes), BF16)
    ref[width : rows - width] = shift_rows(values, width)


def encode_kernel(
    place_ref, dec_ref, enc_ref, wide_ref, *refs, depth
):
    *dark_refs, conv_ref, back_ref, pre_ref, encoded_ref, dark3_ref, up_ref, pad_ref = refs
    planes, width, chans = dark_refs[0].shape[-3:]
    main = wide_ref.shape[1]
    fine_ch = main // RATIO
    cells = planes * width
    fine_width = width * RATIO
    blank = jnp.zeros((chans, chans), BF16)
    weights = []
    for a in range(3):
        rows = []
        for z_out in range(depth):
            blocks = []
            for e in range(3):
                for z_in in range(depth):
                    b = z_in - z_out + 1
                    blocks.append(enc_ref[9 * a + 3 * b + e] if 0 <= b < 3 else blank)
            rows.append(jnp.concatenate(blocks, 1))
        weights.append(jnp.concatenate(rows, 0))
    if len(dark_refs) == 2:
        own, other = (ref[...].reshape(cells, chans) for ref in dark_refs)
        first = place_ref[1] == 0
        parts = [jnp.where(first, own, other), jnp.where(first, other, own)]
    else:
        parts = [dark_refs[0][z].reshape(cells, chans) for z in range(depth)]
    dark = jnp.concatenate(parts, 1)
    store_padded(dark3_ref, dark, width)
    pre = sum(
        dot_nt(dark3_ref[a * width : a * width + cells], weights[a]) for a in range(3)
    )
    pre_ref[...] = pre
    band_taps(dec_ref, conv_ref, back_ref)
    encoded = jax.nn.silu(pre).astype(BF16)
    encoded_ref[...] = encoded
    pad_ref[...] = jnp.zeros(pad_ref.shape, F32)
    for z in range(depth):
        part = encoded[:, z * chans : (z + 1) * chans].astype(F32)
        pad_ref[1 : planes + 1, z + 1] = jnp.concatenate([part, part], 1).reshape(
            planes, width, 2 * chans
        )
    first_x = place_ref[0]
    first_z = place_ref[1]
    repeat = one_hot(
        iota((fine_width, width), 0) // RATIO == iota((fine_width, width), 1)
    )
    two = 2 * chans
    cells = jnp.concatenate(
        [pad_ref[first_x + dx, first_z + dz] for dx in range(3) for dz in range(3)], 1
    )
    repeated = dot(repeat, cells.astype(BF16))
    lane = iota((fine_width, two), 1) // chans
    phase = iota((fine_width, two), 0) % RATIO
    plan = ((0, RATIO - 2, 2, 0), (1, 0, RATIO, 2), (2, 0, 2, RATIO + 2))
    low = iota((fine_ch, RATIO, fine_width), 1) < 2
    for dx, first, count, base in plan:
        rows = []
        for dz in range(3):
            n = 3 * dx + dz
            cell = repeated[:, n * two : (n + 1) * two]
            rows.append(
                jnp.concatenate(
                    [jnp.where(phase == 2 * q + lane, cell, 0.0) for q in range(RATIO // 2)], 1
                )
            )
        field = dot_nt(
            wide_ref[first : first + count].reshape(count * main, RATIO * chans),
            jnp.concatenate(rows, 0).astype(BF16),
        )
        for n in range(count):
            under, own, over = (
                pltpu.roll(
                    field[n * main : (n + 1) * main, m * fine_width : (m + 1) * fine_width].reshape(
                        fine_ch, RATIO, fine_width
                    ),
                    2,
                    1,
                )
                for m in range(3)
            )
            plane = jnp.concatenate([jnp.where(low, over, own), jnp.where(low, own, under)], 1)
            store_shifts(up_ref, base + n, plane.reshape(fine_ch * SPAN, fine_width))


def decode_kernel(
    place_ref, cot_ref, x_low_ref, x_high_ref, z_low_ref, z_high_ref, conv_ref, up_ref,
    grad_ref, total_ref, *, planes_x, planes_z
):
    fine_ch, planes, depth, width = cot_ref.shape
    main = fine_ch * depth
    rows = conv_ref.shape[1]
    wide = (planes + 2) * width
    own = planes * width

    def convolve(first, count):
        low, high = first * width, (first + count) * width
        return sum(
            dot(conv_ref[a], up_ref[:, a * width + low : a * width + high]) for a in range(3)
        )

    step = 2
    ahead = convolve(0, step)
    own_z = place_ref[1]
    valid = (own_z > 0, own_z < planes_z - 1)
    own_x = place_ref[0]
    shape = (main, main)
    turn = iota(shape, 1) == row_index(main) % fine_ch * planes + row_index(main) // fine_ch
    sides = [
        dot(one_hot(turn & valid[side]), ref[...].astype(F32).reshape(main, width).astype(BF16))
        for side, ref in enumerate((z_low_ref, z_high_ref))
    ]
    for x in range(planes + 2):
        if x % step == 0:
            pre = ahead
            if x + step < planes + 2:
                ahead = convolve(x + step, step)
        if 0 < x <= planes:
            inner = cot_ref[:, x - 1].astype(F32).reshape(main, width)
            edge = [side[(x - 1) * fine_ch : x * fine_ch] for side in sides]
        else:
            outer = x_low_ref if x == 0 else x_high_ref
            inside = own_x > 0 if x == 0 else own_x < planes_x - 1
            inner = jnp.where(inside, outer[:main].astype(F32), 0.0)
            edge = []
            for side in range(2):
                first = main + side * (outer.shape[0] - main - fine_ch)
                corner = outer[first : first + fine_ch].astype(F32)
                edge.append(jnp.where(valid[side] & inside, corner, 0.0))
        cot = jnp.concatenate([inner] + edge, 0)
        grad = (cot * slope_of(pre[:, x % step * width : (x % step + 1) * width])).astype(BF16)
        store_shifts(grad_ref, x, grad.astype(F32))
    grads = jnp.concatenate(
        [grad_ref[e * rows : e * rows + main, width : width + own] for e in (2, 1, 0)], 0
    )
    taps = fine_ch * SPAN
    sums = []
    for a in range(3):
        fields = up_ref[taps : 2 * taps, (a + 1) * width : (a + 1) * width + own]
        product = dot_nt(grads, fields)
        halves = []
        for first in range(0, taps, 128):
            part = product[:, first : first + 128].reshape(3 * fine_ch, RATIO, 128)
            halves.append(jnp.sum(pltpu.roll(part, 0, 2, stride=1, stride_axis=1), 1))
        sums.append(jnp.concatenate(halves, 1))
    shape = (3 * fine_ch, taps)
    fold = one_hot(
        iota(shape, 1)
        == row_index(shape[0]) % fine_ch * SPAN + 10 - row_index(shape[0]) // fine_ch
    )
    total_ref[...] = sum(dot_nt(fold, part) for part in split(jnp.concatenate(sums, 0)))


def spread_kernel(cot_ref, grad_ref, back_ref, wide_ref, send_hbm, send_ref, cells_ref, sems):
    fine_ch, planes, depth, width = cot_ref.shape
    main = fine_ch * depth
    own = planes * width
    chans = wide_ref.shape[2] // RATIO
    owners, chunk, _ = send_hbm.shape
    span = chunk - RATIO
    taps = grad_ref.shape[0]
    back = sum(
        dot(back_ref[:, a * taps : (a + 1) * taps], grad_ref[:, a * width : a * width + own])
        for a in range(3)
    )
    cot = jnp.concatenate(
        [cot_ref[:, x].astype(F32).reshape(main, width) for x in range(planes)], 1
    )
    up = (cot + back).astype(BF16)
    row = iota((main, main), 0)
    column = iota((main, main), 1)
    turn = one_hot((row % fine_ch == column // RATIO) & (row // fine_ch == column % RATIO))
    turned = dot(turn, up).astype(BF16)
    for owner in range(owners):
        first = owner * RATIO * RATIO // owners
        x = first // RATIO
        top = first % RATIO * fine_ch
        send_ref[owner] = turned[top : top + span, x * width : (x + 1) * width]
    store = pltpu.make_async_copy(send_ref, send_hbm.at[:, :span], sems.at[0])
    store.start()
    flip = one_hot(
        (row // RATIO == column // RATIO) & (row % RATIO + column % RATIO == RATIO - 1)
    )
    flipped = dot(flip, up).astype(BF16)
    parts = dot_tn(
        jnp.concatenate([flipped[:, x * width : (x + 1) * width] for x in range(planes)], 0),
        wide_ref[...].reshape(planes * main, RATIO * chans),
    )
    two = 2 * chans
    phase = iota((width, two), 0) % RATIO
    lane = iota((width, two), 1) // chans
    both = sum(
        jnp.where(phase == 2 * q + lane, parts[:, q * two : (q + 1) * two], 0.0)
        for q in range(RATIO // 2)
    )
    cells = jnp.sum((both + pltpu.roll(both, chans, 1)).reshape(-1, RATIO, two), 1)
    half = cells.shape[0] // 2
    cells = jnp.where(iota((half, two), 1) < chans, cells[:half], cells[half:]).astype(BF16)
    for owner in range(owners):
        cells_ref[owner] = cells
    last = pltpu.make_async_copy(cells_ref, send_hbm.at[:, span:], sems.at[1])
    last.start()
    store.wait()
    last.wait()


def widen_kernel(
    place_ref, encoded_ref, pre_ref, enc_ref, out_ref, slope_ref, taps_ref, order_ref
):
    cells, lanes = encoded_ref.shape
    chans = enc_ref.shape[1]
    depth = lanes // chans
    block = 32
    repeat = one_hot(
        iota((block * RATIO, block), 0) // RATIO == iota((block * RATIO, block), 1)
    )
    for first in range(0, cells, block):
        out_ref[first * RATIO : (first + block) * RATIO] = dot(
            repeat, encoded_ref[first : first + block]
        ).astype(BF16)
    slope_ref[...] = slope_of(pre_ref[...])
    own_z = place_ref[1]
    for a in range(3):
        for e in range(3):
            for z in range(depth):
                b = z - own_z + 1
                tap = enc_ref[26 - (9 * a + 3 * jnp.clip(b, 0, 2) + e)]
                first = (3 * e * depth + 3 * z) * chans // 3
                taps_ref[a, first : first + chans] = jnp.where(
                    (b >= 0) & (b <= 2), tap.astype(F32), 0.0
                ).astype(BF16)
    shape = order_ref.shape[1:]
    fine_ch = shape[0] // 9
    step = shape[1] // fine_ch
    row = row_index(shape[0])
    column = iota(shape, 1)
    tap = row // fine_ch // 3 * 9 + row // fine_ch % 3
    for b in range(3):
        order_ref[b] = one_hot(column == row % fine_ch * step + tap + 3 * b)


def final_kernel(order_ref, done_ref, *refs, scale):
    *parts, out_ref = refs
    total = sum(part[...] for part in parts) * scale
    fine_ch = out_ref.shape[0]
    parts = split(total)
    field = 0.0
    for b in range(3):
        rows = slice(b * fine_ch, (b + 1) * fine_ch)
        field = field + dot(jnp.concatenate([part[rows] for part in parts], 0), order_ref[b])
    field = field[:fine_ch] + field[fine_ch : 2 * fine_ch] + field[2 * fine_ch :]
    step = field.shape[1] // fine_ch
    for o in range(fine_ch):
        first = o * step // 128 * 128
        part = field[:, first : first + 128]
        if o * step > first:
            part = pltpu.roll(part, 128 - (o * step - first), 1)
        out_ref[o] = part[:, :27]


def finish_kernel(
    got_ref, spread_ref, slope_ref, dark3_ref, taps_ref,
    dark_out, enc_out, up_out, done_ref, pad_ref, *, scale
):
    done_ref[...] = jnp.zeros(done_ref.shape, F32)
    owners, chunk, fine_width = got_ref.shape
    cells, lanes = slope_ref.shape
    chans = taps_ref.shape[2]
    depth = lanes // chans
    planes = owners // depth
    width = cells // planes
    span = chunk - RATIO
    fine_ch = up_out.shape[1]
    rows = []
    for x in range(planes):
        parts = [got_ref[x * depth + z, span:].astype(F32) for z in range(depth)]
        for half in range(2):
            rows.append(
                jnp.concatenate([part[:, half * chans : (half + 1) * chans] for part in parts], 1)
            )
    grad = (jnp.concatenate(rows, 0) * slope_ref[...]).astype(BF16)
    store_padded(pad_ref, grad, width)
    dark_out[...] = sum(
        dot(pad_ref[a * width : a * width + cells], taps_ref[a]) for a in range(3)
    ).reshape(planes, width, chans)
    turned = grad.astype(F32).T.astype(BF16)
    for a in range(3):
        product = dot(turned, dark3_ref[a * width : a * width + cells]) * scale
        for b in range(3):
            for e in range(3):
                total = None
                for z in range(depth):
                    z_in = z + b - 1
                    if 0 <= z_in < depth:
                        first = (e * depth + z_in) * chans
                        part = product[z * chans : (z + 1) * chans, first : first + chans]
                        total = part if total is None else total + part
                enc_out[9 * a + 3 * b + e] = (
                    jnp.zeros((chans, chans), F32) if total is None else total
                )
    pairs = span // fine_ch
    lane = iota((RATIO * fine_ch, fine_width), 1) % RATIO
    masks = one_hot(lane == iota((RATIO * fine_ch, fine_width), 0) // fine_ch)
    sums = None
    for z in range(depth):
        pieces = []
        for x in range(planes):
            arrived = got_ref[x * depth + z, :span]
            pieces.append(
                jnp.concatenate(
                    [
                        jnp.concatenate([arrived[p * fine_ch : (p + 1) * fine_ch]] * RATIO, 0)
                        * masks
                        for p in range(pairs)
                    ],
                    0,
                )
            )
        part = dot(jnp.concatenate(pieces, 1), spread_ref[...])
        part = part[:, z * chans : (z + 1) * chans]
        sums = part if sums is None else sums + part
    up_out[...] = (sums * scale).reshape(pairs * RATIO, fine_ch, chans)


def call(kernel, out_shape, args, scratch=(), scalars=0, flops=1e8, hbm=(), hbm_out=()):
    specs = [pl.BlockSpec(memory_space=pltpu.SMEM)] * scalars
    specs += [
        pl.BlockSpec(memory_space=pltpu.HBM if n in hbm else VMEM)
        for n in range(scalars, len(args))
    ]
    args = [
        pltpu.with_memory_space_constraint(arg, pltpu.HBM) if n in hbm else arg
        for n, arg in enumerate(args)
    ]
    return pl.pallas_call(
        kernel,
        out_shape=[jax.ShapeDtypeStruct(*s) for s in out_shape],
        in_specs=specs,
        out_specs=[
            pl.BlockSpec(memory_space=pltpu.HBM if n in hbm_out else VMEM)
            for n in range(len(out_shape))
        ],
        scratch_shapes=list(scratch),
        compiler_params=pltpu.CompilerParams(vmem_limit_bytes=VMEM_LIMIT),
        cost_estimate=pl.CostEstimate(
            flops=int(flops), bytes_accessed=2_000_000, transcendentals=0
        ),
    )(*args)


def shift(block, axis, by):
    count = lax.axis_size(axis)
    pairs = [(i, i + by) for i in range(count) if 0 <= i + by < count]
    return lax.ppermute(block, axis, pairs)


def swapped(value, step):
    count = lax.axis_size(AXES)
    return lax.ppermute(value, AXES, [(i, i ^ step) for i in range(count)])


def exchange_depth(dark_rows, cotangent):
    count = lax.axis_size("narrow")
    last = cotangent.shape[2] - 1
    if count == 2:
        swap = [(0, 1), (1, 0)]
        dark = lax.ppermute(dark_rows, "narrow", swap)
        z = jnp.where(lax.axis_index("narrow") == 0, last, 0)
        face = lax.ppermute(lax.dynamic_index_in_dim(cotangent, z, 2, False), "narrow", swap)
        return (dark_rows, dark), (face,)
    planes = lax.all_gather(dark_rows, "narrow", axis=0)
    low = shift(cotangent[:, :, last], "narrow", 1)
    return (planes,), (low, shift(cotangent[:, :, 0], "narrow", -1))


def exchange_width(planes, faces):
    count = lax.axis_size("wide")
    depth = lax.axis_size("narrow")
    last = faces[0].shape[1] - 1
    even = lax.axis_index("wide") % 2 == 0
    got = []
    for odd in range(2):
        partner = {}
        for x in range(count):
            other = x + 1 if x % 2 == odd else x - 1
            for z in range(depth):
                if 0 <= other < count:
                    partner[x * depth + z] = other * depth + z
                elif depth % 2 == 0:
                    partner[x * depth + z] = x * depth + (z ^ 1)
        plane = jnp.where(even, 0, last) if odd else jnp.where(even, last, 0)
        edges = [lax.dynamic_index_in_dim(face, plane, 1, False) for face in faces]
        send = jnp.concatenate([planes[odd], *edges], 0)
        got.append(lax.ppermute(send, AXES, list(partner.items())))
    return jnp.where(even, got[1], got[0]), jnp.where(even, got[0], got[1])


def on_device(dark, w_enc, up_weight, w_dec, cotangent):
    chans, planes, own_depth, width = dark.shape
    fine_ch, own_fine, fine_depth, fine_width = cotangent.shape
    subs = up_weight.shape[0]
    depth = lax.axis_size("narrow")
    owners = lax.axis_size(AXES)
    cells = planes * width
    lanes = depth * chans
    own_rows = subs // owners
    where = jnp.stack([lax.axis_index("wide"), lax.axis_index("narrow")]).astype(jnp.int32)

    dark_planes, faces = exchange_depth(dark[:, :, 0].transpose(1, 2, 0), cotangent)

    rows = fine_ch * (RATIO + 2)
    taps = fine_ch * SPAN
    main = fine_ch * RATIO
    face = (fine_ch * fine_depth, fine_width)
    outer = (fine_ch, fine_depth, fine_width)
    wide_table, first_plane, second_plane = call(
        table_kernel,
        [((RATIO, main, RATIO * chans), BF16), (outer, BF16), (outer, BF16)],
        (where, up_weight.transpose(1, 2, 0), cotangent),
        scratch=[VMEM((fine_ch, chans, subs), BF16), pltpu.SemaphoreType.DMA((4,))],
        scalars=1,
        hbm=(1, 2),
        flops=1e9,
    )
    outer_planes = [plane.reshape(face) for plane in (first_plane, second_plane)]
    x_low, x_high = exchange_width(outer_planes, faces)
    conv, back, enc_pre, encoded, dark3, upsampled = call(
        functools.partial(encode_kernel, depth=depth),
        [
            ((3, rows, 3 * taps), BF16),
            ((main, 9 * rows), BF16),
            ((cells, lanes), F32),
            ((cells, lanes), BF16),
            ((cells + 2 * width, 3 * lanes), BF16),
            ((3 * taps, (RATIO + 4) * fine_width), BF16),
        ],
        (where, w_dec.transpose(1, 2, 0), w_enc, wide_table, *dark_planes),
        scratch=[VMEM((planes + 2, depth + 2, width, 2 * chans), F32)],
        scalars=1,
        flops=2e9,
    )
    dec_grad, dec_sum = call(
        functools.partial(decode_kernel, planes_x=planes, planes_z=depth),
        [((3 * rows, (RATIO + 2) * fine_width), BF16), ((3 * fine_ch, 9 * fine_ch), F32)],
        (where, cotangent, x_low, x_high, faces[0], faces[-1], conv, upsampled),
        scalars=1,
        flops=2e9,
    )
    chunk = max(1, RATIO * RATIO // owners) * fine_ch + RATIO
    (send,) = call(
        spread_kernel,
        [((owners, chunk, fine_width), BF16)],
        (cotangent, dec_grad, back, wide_table),
        scratch=[
            VMEM((owners, chunk - RATIO, fine_width), BF16),
            VMEM((owners, RATIO, fine_width), BF16),
            pltpu.SemaphoreType.DMA((2,)),
        ],
        flops=2e9,
        hbm_out=(0,),
    )
    steps = [1 << n for n in range(owners.bit_length() - 1)]
    if owners & (owners - 1):
        dec_sum = lax.psum(dec_sum, AXES)
        steps = []
    steps = sorted(steps)
    one_by_one = steps[: max(1, len(steps) - LAST_STEPS)]
    for step in one_by_one:
        dec_sum = dec_sum + swapped(dec_sum, step)
        if step == steps[0]:
            send, dec_sum = lax.optimization_barrier((send, dec_sum))
    sums = [0]
    for step in steps[len(one_by_one) :]:
        sums += [step + other for other in sums]
    received = [swapped(dec_sum, step) for step in sums[1:]]
    got = lax.all_to_all(send, AXES, 0, 0, tiled=True)
    enc_spread, enc_slope, enc_taps, order = call(
        widen_kernel,
        [
            ((cells * RATIO, lanes), BF16),
            ((cells, lanes), F32),
            ((3, 3 * lanes, chans), BF16),
            ((3, 9 * fine_ch, 32 * fine_ch), BF16),
        ],
        (where, encoded, enc_pre, w_enc),
        scalars=1,
        flops=1e9,
    )
    coarse_scale = 1.0 / math.sqrt(cells * depth)
    fine_scale = 1.0 / math.sqrt(cells * depth * subs)
    pairs = (chunk - RATIO) // fine_ch
    grad_dark, grad_enc, grad_up, done = call(
        functools.partial(finish_kernel, scale=coarse_scale),
        [
            ((planes, width, chans), F32),
            ((27, chans, chans), F32),
            ((pairs * RATIO, fine_ch, chans), F32),
            ((8, 128), F32),
        ],
        (got, enc_spread, enc_slope, dark3, enc_taps),
        scratch=[VMEM((cells + 2 * width, 3 * lanes), BF16)],
        flops=2e9,
    )
    if own_rows < pairs * RATIO:
        own = lax.axis_index(AXES) * own_rows % RATIO
        grad_up = lax.dynamic_slice_in_dim(grad_up, own, own_rows, 0)
    (grad_dec,) = call(
        functools.partial(final_kernel, scale=fine_scale),
        [((fine_ch, fine_ch, 27), F32)],
        (order, done, dec_sum, *received),
        flops=1e8,
    )
    return grad_dark.transpose(2, 0, 1)[:, :, None], grad_enc, grad_up, grad_dec.transpose(2, 0, 1)


def solution(mesh):
    in_specs = (P(None, None, "narrow", None), P(), P(), P(), P(None, "wide", "narrow", None))
    out_specs = (P(None, None, "narrow", None), P(), P(("wide", "narrow"), None, None), P())
    return jax.shard_map(
        on_device, mesh=mesh, in_specs=in_specs, out_specs=out_specs, check_vma=False
    )
```

```python
import functools
import math

import jax
import jax.numpy as jnp
from jax import lax
from jax.experimental import pallas as pl
from jax.experimental.pallas import tpu as pltpu
from jax.sharding import PartitionSpec as P

RATIO = 8
SPAN = 16
LAST_STEPS = 2
F32 = jnp.float32
BF16 = jnp.bfloat16
VMEM_LIMIT = 48 * 1024 * 1024
VMEM = pltpu.VMEM
AXES = ("wide", "narrow")


def slope_of(values):
    sigma = jax.nn.sigmoid(values)
    return sigma * (1.0 + values * (1.0 - sigma))


def dot(left, right):
    return jnp.dot(left, right, preferred_element_type=F32)


def dot_nt(left, right):
    return lax.dot_general(left, right, (((1,), (1,)), ((), ())), preferred_element_type=F32)


def dot_tn(left, right):
    return lax.dot_general(left, right, (((0,), (0,)), ((), ())), preferred_element_type=F32)


def split(values):
    high = values.astype(BF16)
    rest = values - high.astype(F32)
    middle = rest.astype(BF16)
    return high, middle, (rest - middle.astype(F32)).astype(BF16)


def iota(shape, dim):
    return lax.broadcasted_iota(jnp.int32, shape, dim)


def row_index(count):
    return iota((count, 1), 0)


def lane_index(count):
    return iota((1, count), 1)


def one_hot(condition):
    return jnp.where(condition, 1.0, 0.0).astype(BF16)


def place(index, fine_ch):
    main = fine_ch * RATIO
    over = index - main
    channel = jnp.where(index < main, index // RATIO, over % fine_ch)
    z = jnp.where(index < main, index % RATIO, jnp.where(over < fine_ch, -1, RATIO))
    return channel, z


def lane_shift(values, by):
    width = values.shape[1]
    lane = iota(values.shape, 1)
    if by > 0:
        return jnp.where(lane < by, 0.0, pltpu.roll(values, by, 1))
    return jnp.where(lane >= width + by, 0.0, pltpu.roll(values, width + by, 1))


def store_shifts(ref, block, values, top=0, stride=None):
    rows, width = values.shape
    stride = stride or rows
    lanes = slice(block * width, (block + 1) * width)
    parts = (lane_shift(values, 1), values, lane_shift(values, -1))
    for e, part in enumerate(parts):
        ref[top + e * stride : top + e * stride + rows, lanes] = part.astype(BF16)


def band_taps(dec_ref, conv_ref, back_ref):
    fine_ch = dec_ref.shape[0]
    rows = fine_ch * (RATIO + 2)
    square = fine_ch * fine_ch
    group = 9 * fine_ch
    block = 256
    column = lane_index(6 * block)
    rest = column % block
    base = 9 * (rest // (3 * fine_ch)) + (rest // fine_ch) % 3 + 3 * (column // block % 3)
    tap = jnp.where(column < 3 * block, base, 26 - base)
    chosen_taps = one_hot(iota((27, 6 * block), 0) == jnp.where(rest < group, tap, -1))
    cell = row_index(square)
    last_index = iota((square, block), 1) % fine_ch
    same_in = last_index == cell % fine_ch
    same_out = last_index == cell // fine_ch
    shape = (fine_ch, square)
    pick_out = one_hot(iota(shape, 0) == lane_index(square) // fine_ch)
    pick_in = one_hot(iota(shape, 0) == lane_index(square) % fine_ch)
    wide = group * SPAN
    spread = one_hot(iota((group, wide), 0) == lane_index(wide) // SPAN)
    spread = jnp.concatenate([spread, jnp.zeros((block - group, wide), BF16)], 0)
    back_wide = 9 * rows
    column = lane_index(back_wide)
    channel, _ = place(column % rows, fine_ch)
    spread_back = one_hot(iota((group, back_wide), 0) == column // rows * fine_ch + channel)
    spread_back = jnp.concatenate([spread_back, jnp.zeros((block - group, back_wide), BF16)], 0)
    chosen = dot(dec_ref[...].reshape(square, 27), chosen_taps)
    taps = []
    for n in range(6):
        part = chosen[:, n * block : (n + 1) * block]
        part = jnp.where(same_in if n < 3 else same_out, part, 0.0).astype(BF16)
        taps.append(dot(pick_out if n < 3 else pick_in, part).astype(BF16))
    forward = dot(jnp.concatenate(taps[:3], 0), spread)
    backward = dot(jnp.concatenate(taps[3:], 0), spread_back)

    def banded(parts, masks):
        blocks = []
        for first in range(0, parts[0].shape[1], 128):
            total = jnp.zeros(masks[0].shape, F32)
            for part, mask in zip(parts, masks):
                part = jnp.broadcast_to(part[:, first : first + 128], mask.shape)
                total = jnp.where(mask, part, total)
            blocks.append(total)
        return jnp.concatenate(blocks, 1)

    def rows_of(field, channel):
        return [
            field[b * fine_ch + channel : b * fine_ch + channel + 1] for b in range(3)
        ]

    slot = iota((RATIO, 128), 1) % SPAN
    masks = [10 - slot - iota((RATIO, 128), 0) == b for b in range(3)]
    pieces = [banded(rows_of(forward, o), masks) for o in range(fine_ch)]
    slot = iota((fine_ch, 128), 1) % SPAN
    parts = [forward[b * fine_ch : (b + 1) * fine_ch] for b in range(3)]
    pieces += [banded(parts, [base - slot == b for b in range(3)]) for base in (11, 2)]
    field = jnp.concatenate(pieces, 0).astype(BF16)
    for a in range(3):
        conv_ref[a] = field[:, a * (wide // 3) : (a + 1) * (wide // 3)]
    _, z_in = place(lane_index(back_wide) % rows, fine_ch)
    offset = z_in - iota((RATIO, back_wide), 0) + 1
    masks = [offset == b for b in range(3)]
    pieces = []
    for c in range(fine_ch):
        total = jnp.zeros(offset.shape, F32)
        for part, mask in zip(rows_of(backward, c), masks):
            total = jnp.where(mask, jnp.broadcast_to(part, offset.shape), total)
        pieces.append(total)
    back_ref[...] = jnp.concatenate(pieces, 0).astype(BF16)


def table_kernel(
    place_ref, table_hbm, cot_hbm, wide_ref, first_ref, second_ref, table_ref, sems
):
    last = cot_hbm.shape[1] - 1
    even = lax.rem(place_ref[0], 2) == 0
    fine_ch, chans, subs = table_ref.shape
    half = fine_ch // 2
    loads = [
        pltpu.make_async_copy(
            table_hbm.at[n * half : (n + 1) * half],
            table_ref.at[n * half : (n + 1) * half],
            sems.at[n],
        )
        for n in range(2)
    ]
    planes = [
        pltpu.make_async_copy(cot_hbm.at[:, jnp.where(even, last, 0)], first_ref, sems.at[2]),
        pltpu.make_async_copy(cot_hbm.at[:, jnp.where(even, 0, last)], second_ref, sems.at[3]),
    ]
    for copy in loads + planes:
        copy.start()
    pairs = RATIO * RATIO
    row = row_index(subs)
    position = row % pairs // RATIO * pairs + (RATIO - 1 - row % RATIO) * RATIO + row // pairs
    pick = one_hot(iota((subs, subs), 1) == position)
    two = 2 * chans
    low = iota((pairs, two), 1) < chans
    for n in range(2):
        loads[n].wait()
        part = table_ref[n * half : (n + 1) * half].reshape(half * chans, subs)
        turned = dot_nt(pick, part)
        for p in range(half // 2):
            lanes = slice(p * two, (p + 1) * two)
            top = (n * half // 2 + p) * SPAN
            for q in range(RATIO // 2):
                even = turned[2 * q * pairs : (2 * q + 1) * pairs, lanes]
                odd = turned[(2 * q + 1) * pairs : (2 * q + 2) * pairs, lanes]
                first = jnp.where(low, even, pltpu.roll(odd, chans, 1))
                second = jnp.where(low, pltpu.roll(even, chans, 1), odd)
                both = jnp.concatenate(
                    [first.reshape(RATIO, RATIO, two), second.reshape(RATIO, RATIO, two)], 1
                )
                wide_ref[:, top : top + SPAN, q * two : (q + 1) * two] = both.astype(BF16)
    for copy in planes:
        copy.wait()


def shift_rows(values, width):
    count = values.shape[0]
    block = min(count, 256)
    row = iota((block, block), 0)
    column = iota((block, block), 1)
    down = one_hot((column == row - 1) & (row % width > 0))
    up = one_hot((column == row + 1) & (row % width < width - 1))
    pieces = []
    for first in range(0, count, block):
        part = values[first : first + block]
        pieces.append(
            jnp.concatenate([dot(down, part).astype(BF16), part, dot(up, part).astype(BF16)], 1)
        )
    return jnp.concatenate(pieces, 0)


def store_padded(ref, values, width):
    rows, lanes = ref.shape
    ref[0:width] = jnp.zeros((width, lanes), BF16)
    ref[rows - width : rows] = jnp.zeros((width, lanes), BF16)
    ref[width : rows - width] = shift_rows(values, width)


def encode_kernel(
    place_ref, dec_ref, enc_ref, wide_ref, *refs, depth
):
    *dark_refs, conv_ref, back_ref, pre_ref, encoded_ref, dark3_ref, up_ref, pad_ref = refs
    planes, width, chans = dark_refs[0].shape[-3:]
    main = wide_ref.shape[1]
    fine_ch = main // RATIO
    cells = planes * width
    fine_width = width * RATIO
    blank = jnp.zeros((chans, chans), BF16)
    weights = []
    for a in range(3):
        rows = []
        for z_out in range(depth):
            blocks = []
            for e in range(3):
                for z_in in range(depth):
                    b = z_in - z_out + 1
                    blocks.append(enc_ref[9 * a + 3 * b + e] if 0 <= b < 3 else blank)
            rows.append(jnp.concatenate(blocks, 1))
        weights.append(jnp.concatenate(rows, 0))
    if len(dark_refs) == 2:
        own, other = (ref[...].reshape(cells, chans) for ref in dark_refs)
        first = place_ref[1] == 0
        parts = [jnp.where(first, own, other), jnp.where(first, other, own)]
    else:
        parts = [dark_refs[0][z].reshape(cells, chans) for z in range(depth)]
    dark = jnp.concatenate(parts, 1)
    store_padded(dark3_ref, dark, width)
    pre = sum(
        dot_nt(dark3_ref[a * width : a * width + cells], weights[a]) for a in range(3)
    )
    pre_ref[...] = pre
    band_taps(dec_ref, conv_ref, back_ref)
    encoded = jax.nn.silu(pre).astype(BF16)
    encoded_ref[...] = encoded
    pad_ref[...] = jnp.zeros(pad_ref.shape, F32)
    for z in range(depth):
        part = encoded[:, z * chans : (z + 1) * chans].astype(F32)
        pad_ref[1 : planes + 1, z + 1] = jnp.concatenate([part, part], 1).reshape(
            planes, width, 2 * chans
        )
    first_x = place_ref[0]
    first_z = place_ref[1]
    repeat = one_hot(
        iota((fine_width, width), 0) // RATIO == iota((fine_width, width), 1)
    )
    two = 2 * chans
    cells = jnp.concatenate(
        [pad_ref[first_x + dx, first_z + dz] for dx in range(3) for dz in range(3)], 1
    )
    repeated = dot(repeat, cells.astype(BF16))
    lane = iota((fine_width, two), 1) // chans
    phase = iota((fine_width, two), 0) % RATIO
    low = iota((fine_ch, RATIO, fine_width), 1) < 2
    columns = []
    for n in range(9):
        cell = repeated[:, n * two : (n + 1) * two]
        columns.append(
            jnp.concatenate(
                [jnp.where(phase == 2 * q + lane, cell, 0.0) for q in range(RATIO // 2)], 1
            ).astype(BF16)
        )
    plan = (
        (0, 2, ((1, 2), (2, RATIO + 2))),
        (2, RATIO - 4, ((1, 2),)),
        (RATIO - 2, 2, ((0, 2 - RATIO), (1, 2))),
    )
    for first, count, needed in plan:
        field = dot_nt(
            wide_ref[first : first + count].reshape(count * main, RATIO * chans),
            jnp.concatenate([columns[3 * dx + dz] for dx, _ in needed for dz in range(3)], 0),
        )
        for n in range(count):
            for m, (_, base) in enumerate(needed):
                under, own, over = (
                    pltpu.roll(
                        field[
                            n * main : (n + 1) * main,
                            (3 * m + dz) * fine_width : (3 * m + dz + 1) * fine_width,
                        ].reshape(fine_ch, RATIO, fine_width),
                        2,
                        1,
                    )
                    for dz in range(3)
                )
                plane = jnp.concatenate([jnp.where(low, over, own), jnp.where(low, own, under)], 1)
                store_shifts(up_ref, base + first + n, plane.reshape(fine_ch * SPAN, fine_width))


def decode_kernel(cot_ref, conv_ref, up_ref, grad_ref, outer_ref, edge_ref, total_ref):
    fine_ch, planes, depth, width = cot_ref.shape
    main = fine_ch * depth
    own = planes * width

    def convolve(first, count):
        low, high = first * width, (first + count) * width
        return sum(
            dot(conv_ref[a], up_ref[:, a * width + low : a * width + high]) for a in range(3)
        )

    step = 2
    ahead = convolve(0, step)
    for x in range(planes + 2):
        if x % step == 0:
            pre = ahead
            if x + step < planes + 2:
                ahead = convolve(x + step, step)
        here = pre[:, x % step * width : (x % step + 1) * width]
        if 0 < x <= planes:
            cot = cot_ref[:, x - 1].astype(F32).reshape(main, width)
            grad = (cot * slope_of(here[:main])).astype(BF16)
            store_shifts(grad_ref, x - 1, grad.astype(F32))
            edge_ref[:, (x - 1) * width : x * width] = here[main:]
        else:
            outer_ref[0 if x == 0 else 1] = here
    grads = jnp.concatenate([grad_ref[e * main : (e + 1) * main] for e in (2, 1, 0)], 0)
    taps = fine_ch * SPAN
    sums = []
    for a in range(3):
        fields = up_ref[taps : 2 * taps, (a + 1) * width : (a + 1) * width + own]
        product = dot_nt(grads, fields)
        halves = []
        for first in range(0, taps, 128):
            part = product[:, first : first + 128].reshape(3 * fine_ch, RATIO, 128)
            halves.append(jnp.sum(pltpu.roll(part, 0, 2, stride=1, stride_axis=1), 1))
        sums.append(jnp.concatenate(halves, 1))
    shape = (3 * fine_ch, taps)
    fold = one_hot(
        iota(shape, 1)
        == row_index(shape[0]) % fine_ch * SPAN + 10 - row_index(shape[0]) // fine_ch
    )
    total_ref[...] = sum(dot_nt(fold, part) for part in split(jnp.concatenate(sums, 0)))


def spread_kernel(
    place_ref, cot_ref, x_low_ref, x_high_ref, z_low_ref, z_high_ref, own_ref, outer_ref, edge_ref,
    back_ref, wide_ref, send_hbm, grad_ref, send_ref, cells_ref, sems, *, planes_x, planes_z
):
    fine_ch, planes, depth, width = cot_ref.shape
    main = fine_ch * depth
    own = planes * width
    rows = outer_ref.shape[1]
    chans = wide_ref.shape[2] // RATIO
    owners, chunk, _ = send_hbm.shape
    span = chunk - RATIO
    own_x = place_ref[0]
    own_z = place_ref[1]
    valid = (own_z > 0, own_z < planes_z - 1)
    for e in range(3):
        grad_ref[e * rows : e * rows + main, width : width + own] = own_ref[
            e * main : (e + 1) * main
        ]
    for x, outer in ((0, x_low_ref), (planes + 1, x_high_ref)):
        inside = own_x > 0 if x == 0 else own_x < planes_x - 1
        cot = [jnp.where(inside, outer[:main].astype(F32), 0.0)]
        for side in range(2):
            first = main + side * (outer.shape[0] - main - fine_ch)
            corner = outer[first : first + fine_ch].astype(F32)
            cot.append(jnp.where(valid[side] & inside, corner, 0.0))
        pre = outer_ref[0 if x == 0 else 1]
        grad = (jnp.concatenate(cot, 0) * slope_of(pre)).astype(BF16)
        store_shifts(grad_ref, x, grad.astype(F32))
    shape = (main, main)
    turn = iota(shape, 1) == row_index(main) % fine_ch * planes + row_index(main) // fine_ch
    sides = [
        dot(one_hot(turn & valid[side]), ref[...].astype(F32).reshape(main, width).astype(BF16))
        for side, ref in enumerate((z_low_ref, z_high_ref))
    ]
    for x in range(planes):
        cot = jnp.concatenate([side[x * fine_ch : (x + 1) * fine_ch] for side in sides], 0)
        grad = (cot * slope_of(edge_ref[:, x * width : (x + 1) * width])).astype(BF16)
        store_shifts(grad_ref, x + 1, grad.astype(F32), main, rows)
    taps = grad_ref.shape[0]
    back = sum(
        dot(back_ref[:, a * taps : (a + 1) * taps], grad_ref[:, a * width : a * width + own])
        for a in range(3)
    )
    cot = jnp.concatenate(
        [cot_ref[:, x].astype(F32).reshape(main, width) for x in range(planes)], 1
    )
    up = (cot + back).astype(BF16)
    row = row_index(main)
    order = jnp.concatenate(
        [row % fine_ch * RATIO + row // fine_ch, row // RATIO * RATIO + RATIO - 1 - row % RATIO], 0
    )
    both = dot(one_hot(iota((2 * main, main), 1) == order), up).astype(BF16)
    turned, flipped = both[:main], both[main:]
    for owner in range(owners):
        first = owner * RATIO * RATIO // owners
        x = first // RATIO
        top = first % RATIO * fine_ch
        send_ref[owner] = turned[top : top + span, x * width : (x + 1) * width]
    store = pltpu.make_async_copy(send_ref, send_hbm.at[:, :span], sems.at[0])
    store.start()
    parts = dot_tn(
        jnp.concatenate([flipped[:, x * width : (x + 1) * width] for x in range(planes)], 0),
        wide_ref[...].reshape(planes * main, RATIO * chans),
    )
    two = 2 * chans
    phase = iota((width, two), 0) % RATIO
    lane = iota((width, two), 1) // chans
    both = sum(
        jnp.where(phase == 2 * q + lane, parts[:, q * two : (q + 1) * two], 0.0)
        for q in range(RATIO // 2)
    )
    cells = jnp.sum((both + pltpu.roll(both, chans, 1)).reshape(-1, RATIO, two), 1)
    half = cells.shape[0] // 2
    cells = jnp.where(iota((half, two), 1) < chans, cells[:half], cells[half:]).astype(BF16)
    for owner in range(owners):
        cells_ref[owner] = cells
    last = pltpu.make_async_copy(cells_ref, send_hbm.at[:, span:], sems.at[1])
    last.start()
    store.wait()
    last.wait()


def widen_kernel(
    place_ref, encoded_ref, pre_ref, enc_ref, out_ref, slope_ref, taps_ref, order_ref
):
    cells, lanes = encoded_ref.shape
    chans = enc_ref.shape[1]
    depth = lanes // chans
    block = 32
    repeat = one_hot(
        iota((block * RATIO, block), 0) // RATIO == iota((block * RATIO, block), 1)
    )
    for first in range(0, cells, block):
        out_ref[first * RATIO : (first + block) * RATIO] = dot(
            repeat, encoded_ref[first : first + block]
        ).astype(BF16)
    slope_ref[...] = slope_of(pre_ref[...])
    own_z = place_ref[1]
    for a in range(3):
        for e in range(3):
            for z in range(depth):
                b = z - own_z + 1
                tap = enc_ref[26 - (9 * a + 3 * jnp.clip(b, 0, 2) + e)]
                first = (3 * e * depth + 3 * z) * chans // 3
                taps_ref[a, first : first + chans] = jnp.where(
                    (b >= 0) & (b <= 2), tap.astype(F32), 0.0
                ).astype(BF16)
    shape = order_ref.shape[1:]
    fine_ch = shape[0] // 9
    step = shape[1] // fine_ch
    row = row_index(shape[0])
    column = iota(shape, 1)
    tap = row // fine_ch // 3 * 9 + row // fine_ch % 3
    for b in range(3):
        order_ref[b] = one_hot(column == row % fine_ch * step + tap + 3 * b)


def final_kernel(order_ref, done_ref, *refs, scale):
    *parts, out_ref = refs
    total = sum(part[...] for part in parts) * scale
    fine_ch = out_ref.shape[0]
    parts = split(total)
    field = 0.0
    for b in range(3):
        rows = slice(b * fine_ch, (b + 1) * fine_ch)
        field = field + dot(jnp.concatenate([part[rows] for part in parts], 0), order_ref[b])
    field = field[:fine_ch] + field[fine_ch : 2 * fine_ch] + field[2 * fine_ch :]
    step = field.shape[1] // fine_ch
    for o in range(fine_ch):
        first = o * step // 128 * 128
        part = field[:, first : first + 128]
        if o * step > first:
            part = pltpu.roll(part, 128 - (o * step - first), 1)
        out_ref[o] = part[:, :27]


def finish_kernel(
    got_ref, spread_ref, slope_ref, dark3_ref, taps_ref,
    dark_out, enc_out, up_out, done_ref, pad_ref, *, scale
):
    done_ref[...] = jnp.zeros(done_ref.shape, F32)
    owners, chunk, fine_width = got_ref.shape
    cells, lanes = slope_ref.shape
    chans = taps_ref.shape[2]
    depth = lanes // chans
    planes = owners // depth
    width = cells // planes
    span = chunk - RATIO
    fine_ch = up_out.shape[1]
    rows = []
    for x in range(planes):
        parts = [got_ref[x * depth + z, span:].astype(F32) for z in range(depth)]
        for half in range(2):
            rows.append(
                jnp.concatenate([part[:, half * chans : (half + 1) * chans] for part in parts], 1)
            )
    grad = (jnp.concatenate(rows, 0) * slope_ref[...]).astype(BF16)
    store_padded(pad_ref, grad, width)
    dark_out[...] = sum(
        dot(pad_ref[a * width : a * width + cells], taps_ref[a]) for a in range(3)
    ).reshape(planes, width, chans)
    turned = grad.astype(F32).T.astype(BF16)
    for a in range(3):
        product = dot(turned, dark3_ref[a * width : a * width + cells]) * scale
        for b in range(3):
            for e in range(3):
                total = None
                for z in range(depth):
                    z_in = z + b - 1
                    if 0 <= z_in < depth:
                        first = (e * depth + z_in) * chans
                        part = product[z * chans : (z + 1) * chans, first : first + chans]
                        total = part if total is None else total + part
                enc_out[9 * a + 3 * b + e] = (
                    jnp.zeros((chans, chans), F32) if total is None else total
                )
    pairs = span // fine_ch
    lane = iota((RATIO * fine_ch, fine_width), 1) % RATIO
    masks = one_hot(lane == iota((RATIO * fine_ch, fine_width), 0) // fine_ch)
    sums = None
    for z in range(depth):
        pieces = []
        for x in range(planes):
            arrived = got_ref[x * depth + z, :span]
            pieces.append(
                jnp.concatenate(
                    [
                        jnp.concatenate([arrived[p * fine_ch : (p + 1) * fine_ch]] * RATIO, 0)
                        * masks
                        for p in range(pairs)
                    ],
                    0,
                )
            )
        part = dot(jnp.concatenate(pieces, 1), spread_ref[...])
        part = part[:, z * chans : (z + 1) * chans]
        sums = part if sums is None else sums + part
    up_out[...] = (sums * scale).reshape(pairs * RATIO, fine_ch, chans)


def call(kernel, out_shape, args, scratch=(), scalars=0, flops=1e8, hbm=(), hbm_out=()):
    specs = [pl.BlockSpec(memory_space=pltpu.SMEM)] * scalars
    specs += [
        pl.BlockSpec(memory_space=pltpu.HBM if n in hbm else VMEM)
        for n in range(scalars, len(args))
    ]
    args = [
        pltpu.with_memory_space_constraint(arg, pltpu.HBM) if n in hbm else arg
        for n, arg in enumerate(args)
    ]
    return pl.pallas_call(
        kernel,
        out_shape=[jax.ShapeDtypeStruct(*s) for s in out_shape],
        in_specs=specs,
        out_specs=[
            pl.BlockSpec(memory_space=pltpu.HBM if n in hbm_out else VMEM)
            for n in range(len(out_shape))
        ],
        scratch_shapes=list(scratch),
        compiler_params=pltpu.CompilerParams(vmem_limit_bytes=VMEM_LIMIT),
        cost_estimate=pl.CostEstimate(
            flops=int(flops), bytes_accessed=2_000_000, transcendentals=0
        ),
    )(*args)


def shift(block, axis, by):
    count = lax.axis_size(axis)
    pairs = [(i, i + by) for i in range(count) if 0 <= i + by < count]
    return lax.ppermute(block, axis, pairs)


def swapped(value, step):
    count = lax.axis_size(AXES)
    return lax.ppermute(value, AXES, [(i, i ^ step) for i in range(count)])


def exchange_depth(dark_rows, cotangent):
    count = lax.axis_size("narrow")
    last = cotangent.shape[2] - 1
    if count == 2:
        swap = [(0, 1), (1, 0)]
        dark = lax.ppermute(dark_rows, "narrow", swap)
        z = jnp.where(lax.axis_index("narrow") == 0, last, 0)
        face = lax.ppermute(lax.dynamic_index_in_dim(cotangent, z, 2, False), "narrow", swap)
        return (dark_rows, dark), (face,)
    planes = lax.all_gather(dark_rows, "narrow", axis=0)
    low = shift(cotangent[:, :, last], "narrow", 1)
    return (planes,), (low, shift(cotangent[:, :, 0], "narrow", -1))


def exchange_width(planes, faces):
    count = lax.axis_size("wide")
    depth = lax.axis_size("narrow")
    last = faces[0].shape[1] - 1
    even = lax.axis_index("wide") % 2 == 0
    got = []
    for odd in range(2):
        partner = {}
        for x in range(count):
            other = x + 1 if x % 2 == odd else x - 1
            for z in range(depth):
                if 0 <= other < count:
                    partner[x * depth + z] = other * depth + z
                elif depth % 2 == 0:
                    partner[x * depth + z] = x * depth + (z ^ 1)
        plane = jnp.where(even, 0, last) if odd else jnp.where(even, last, 0)
        edges = [lax.dynamic_index_in_dim(face, plane, 1, False) for face in faces]
        send = jnp.concatenate([planes[odd], *edges], 0)
        got.append(lax.ppermute(send, AXES, list(partner.items())))
    return jnp.where(even, got[1], got[0]), jnp.where(even, got[0], got[1])


def on_device(dark, w_enc, up_weight, w_dec, cotangent):
    chans, planes, own_depth, width = dark.shape
    fine_ch, own_fine, fine_depth, fine_width = cotangent.shape
    subs = up_weight.shape[0]
    depth = lax.axis_size("narrow")
    owners = lax.axis_size(AXES)
    cells = planes * width
    lanes = depth * chans
    own_rows = subs // owners
    where = jnp.stack([lax.axis_index("wide"), lax.axis_index("narrow")]).astype(jnp.int32)

    dark_planes, faces = exchange_depth(dark[:, :, 0].transpose(1, 2, 0), cotangent)

    rows = fine_ch * (RATIO + 2)
    taps = fine_ch * SPAN
    main = fine_ch * RATIO
    face = (fine_ch * fine_depth, fine_width)
    outer = (fine_ch, fine_depth, fine_width)
    wide_table, first_plane, second_plane = call(
        table_kernel,
        [((RATIO, main, RATIO * chans), BF16), (outer, BF16), (outer, BF16)],
        (where, up_weight.transpose(1, 2, 0), cotangent),
        scratch=[VMEM((fine_ch, chans, subs), BF16), pltpu.SemaphoreType.DMA((4,))],
        scalars=1,
        hbm=(1, 2),
        flops=1e9,
    )
    outer_planes = [plane.reshape(face) for plane in (first_plane, second_plane)]
    x_low, x_high = exchange_width(outer_planes, faces)
    conv, back, enc_pre, encoded, dark3, upsampled = call(
        functools.partial(encode_kernel, depth=depth),
        [
            ((3, rows, 3 * taps), BF16),
            ((main, 9 * rows), BF16),
            ((cells, lanes), F32),
            ((cells, lanes), BF16),
            ((cells + 2 * width, 3 * lanes), BF16),
            ((3 * taps, (RATIO + 4) * fine_width), BF16),
        ],
        (where, w_dec.transpose(1, 2, 0), w_enc, wide_table, *dark_planes),
        scratch=[VMEM((planes + 2, depth + 2, width, 2 * chans), F32)],
        scalars=1,
        flops=2e9,
    )
    own = own_fine * fine_width
    dec_grad, outer_pre, edge_pre, dec_sum = call(
        decode_kernel,
        [
            ((3 * main, own), BF16),
            ((2, rows, fine_width), F32),
            ((rows - main, own), F32),
            ((3 * fine_ch, 9 * fine_ch), F32),
        ],
        (cotangent, conv, upsampled),
        flops=2e9,
    )
    chunk = max(1, RATIO * RATIO // owners) * fine_ch + RATIO
    (send,) = call(
        functools.partial(spread_kernel, planes_x=planes, planes_z=depth),
        [((owners, chunk, fine_width), BF16)],
        (
            where, cotangent, x_low, x_high, faces[0], faces[-1], dec_grad, outer_pre, edge_pre,
            back, wide_table,
        ),
        scratch=[
            VMEM((3 * rows, own + 2 * fine_width), BF16),
            VMEM((owners, chunk - RATIO, fine_width), BF16),
            VMEM((owners, RATIO, fine_width), BF16),
            pltpu.SemaphoreType.DMA((2,)),
        ],
        scalars=1,
        flops=2e9,
        hbm_out=(0,),
    )
    steps = [1 << n for n in range(owners.bit_length() - 1)]
    if owners & (owners - 1):
        dec_sum = lax.psum(dec_sum, AXES)
        steps = []
    steps = sorted(steps)
    one_by_one = steps[: max(1, len(steps) - LAST_STEPS)]
    for step in one_by_one:
        other = swapped(dec_sum, step)
        if step == steps[0]:
            send, other, dec_sum = lax.optimization_barrier((send, other, dec_sum))
        dec_sum = dec_sum + other
    sums = [0]
    for step in steps[len(one_by_one) :]:
        sums += [step + other for other in sums]
    received = [swapped(dec_sum, step) for step in sums[1:]]
    got = lax.all_to_all(send, AXES, 0, 0, tiled=True)
    enc_spread, enc_slope, enc_taps, order = call(
        widen_kernel,
        [
            ((cells * RATIO, lanes), BF16),
            ((cells, lanes), F32),
            ((3, 3 * lanes, chans), BF16),
            ((3, 9 * fine_ch, 32 * fine_ch), BF16),
        ],
        (where, encoded, enc_pre, w_enc),
        scalars=1,
        flops=1e9,
    )
    coarse_scale = 1.0 / math.sqrt(cells * depth)
    fine_scale = 1.0 / math.sqrt(cells * depth * subs)
    pairs = (chunk - RATIO) // fine_ch
    grad_dark, grad_enc, grad_up, done = call(
        functools.partial(finish_kernel, scale=coarse_scale),
        [
            ((planes, width, chans), F32),
            ((27, chans, chans), F32),
            ((pairs * RATIO, fine_ch, chans), F32),
            ((8, 128), F32),
        ],
        (got, enc_spread, enc_slope, dark3, enc_taps),
        scratch=[VMEM((cells + 2 * width, 3 * lanes), BF16)],
        flops=2e9,
    )
    if own_rows < pairs * RATIO:
        own = lax.axis_index(AXES) * own_rows % RATIO
        grad_up = lax.dynamic_slice_in_dim(grad_up, own, own_rows, 0)
    (grad_dec,) = call(
        functools.partial(final_kernel, scale=fine_scale),
        [((fine_ch, fine_ch, 27), F32)],
        (order, done, dec_sum, *received),
        flops=1e8,
    )
    return grad_dark.transpose(2, 0, 1)[:, :, None], grad_enc, grad_up, grad_dec.transpose(2, 0, 1)


def solution(mesh):
    in_specs = (P(None, None, "narrow", None), P(), P(), P(), P(None, "wide", "narrow", None))
    out_specs = (P(None, None, "narrow", None), P(), P(("wide", "narrow"), None, None), P())
    return jax.shard_map(
        on_device, mesh=mesh, in_specs=in_specs, out_specs=out_specs, check_vma=False
    )
```

```python
import functools
import math

import jax
import jax.numpy as jnp
from jax import lax
from jax.experimental import pallas as pl
from jax.experimental.pallas import tpu as pltpu
from jax.sharding import PartitionSpec as P

RATIO = 8
SPAN = 16
LAST_STEPS = 2
F32 = jnp.float32
BF16 = jnp.bfloat16
VMEM_LIMIT = 48 * 1024 * 1024
VMEM = pltpu.VMEM
AXES = ("wide", "narrow")


def slope_of(values):
    sigma = jax.nn.sigmoid(values)
    return sigma * (1.0 + values * (1.0 - sigma))


def dot(left, right):
    return jnp.dot(left, right, preferred_element_type=F32)


def dot_nt(left, right):
    return lax.dot_general(left, right, (((1,), (1,)), ((), ())), preferred_element_type=F32)


def dot_tn(left, right):
    return lax.dot_general(left, right, (((0,), (0,)), ((), ())), preferred_element_type=F32)


def split(values):
    high = values.astype(BF16)
    rest = values - high.astype(F32)
    middle = rest.astype(BF16)
    return high, middle, (rest - middle.astype(F32)).astype(BF16)


def iota(shape, dim):
    return lax.broadcasted_iota(jnp.int32, shape, dim)


def row_index(count):
    return iota((count, 1), 0)


def lane_index(count):
    return iota((1, count), 1)


def one_hot(condition):
    return jnp.where(condition, 1.0, 0.0).astype(BF16)


def place(index, fine_ch):
    main = fine_ch * RATIO
    over = index - main
    channel = jnp.where(index < main, index // RATIO, over % fine_ch)
    z = jnp.where(index < main, index % RATIO, jnp.where(over < fine_ch, -1, RATIO))
    return channel, z


def lane_shift(values, by):
    width = values.shape[1]
    lane = iota(values.shape, 1)
    if by > 0:
        return jnp.where(lane < by, 0.0, pltpu.roll(values, by, 1))
    return jnp.where(lane >= width + by, 0.0, pltpu.roll(values, width + by, 1))


def store_shifts(ref, block, values, top=0, stride=None):
    rows, width = values.shape
    stride = stride or rows
    lanes = slice(block * width, (block + 1) * width)
    parts = (lane_shift(values, 1), values, lane_shift(values, -1))
    for e, part in enumerate(parts):
        ref[top + e * stride : top + e * stride + rows, lanes] = part.astype(BF16)


def band_taps(dec_ref, conv_ref, back_ref):
    fine_ch = dec_ref.shape[0]
    rows = fine_ch * (RATIO + 2)
    square = fine_ch * fine_ch
    group = 9 * fine_ch
    block = 256
    column = lane_index(6 * block)
    rest = column % block
    base = 9 * (rest // (3 * fine_ch)) + (rest // fine_ch) % 3 + 3 * (column // block % 3)
    tap = jnp.where(column < 3 * block, base, 26 - base)
    chosen_taps = one_hot(iota((27, 6 * block), 0) == jnp.where(rest < group, tap, -1))
    cell = row_index(square)
    last_index = iota((square, block), 1) % fine_ch
    same_in = last_index == cell % fine_ch
    same_out = last_index == cell // fine_ch
    shape = (fine_ch, square)
    pick_out = one_hot(iota(shape, 0) == lane_index(square) // fine_ch)
    pick_in = one_hot(iota(shape, 0) == lane_index(square) % fine_ch)
    wide = group * SPAN
    spread = one_hot(iota((group, wide), 0) == lane_index(wide) // SPAN)
    spread = jnp.concatenate([spread, jnp.zeros((block - group, wide), BF16)], 0)
    back_wide = 9 * rows
    column = lane_index(back_wide)
    channel, _ = place(column % rows, fine_ch)
    spread_back = one_hot(iota((group, back_wide), 0) == column // rows * fine_ch + channel)
    spread_back = jnp.concatenate([spread_back, jnp.zeros((block - group, back_wide), BF16)], 0)
    chosen = dot(dec_ref[...].reshape(square, 27), chosen_taps)
    taps = []
    for n in range(6):
        part = chosen[:, n * block : (n + 1) * block]
        part = jnp.where(same_in if n < 3 else same_out, part, 0.0).astype(BF16)
        taps.append(dot(pick_out if n < 3 else pick_in, part).astype(BF16))
    forward = dot(jnp.concatenate(taps[:3], 0), spread)
    backward = dot(jnp.concatenate(taps[3:], 0), spread_back)

    def banded(parts, masks):
        blocks = []
        for first in range(0, parts[0].shape[1], 128):
            total = jnp.zeros(masks[0].shape, F32)
            for part, mask in zip(parts, masks):
                part = jnp.broadcast_to(part[:, first : first + 128], mask.shape)
                total = jnp.where(mask, part, total)
            blocks.append(total)
        return jnp.concatenate(blocks, 1)

    def rows_of(field, channel):
        return [
            field[b * fine_ch + channel : b * fine_ch + channel + 1] for b in range(3)
        ]

    slot = iota((RATIO, 128), 1) % SPAN
    masks = [10 - slot - iota((RATIO, 128), 0) == b for b in range(3)]
    pieces = [banded(rows_of(forward, o), masks) for o in range(fine_ch)]
    slot = iota((fine_ch, 128), 1) % SPAN
    parts = [forward[b * fine_ch : (b + 1) * fine_ch] for b in range(3)]
    pieces += [banded(parts, [base - slot == b for b in range(3)]) for base in (11, 2)]
    field = jnp.concatenate(pieces, 0).astype(BF16)
    for a in range(3):
        conv_ref[a] = field[:, a * (wide // 3) : (a + 1) * (wide // 3)]
    _, z_in = place(lane_index(back_wide) % rows, fine_ch)
    offset = z_in - iota((RATIO, back_wide), 0) + 1
    masks = [offset == b for b in range(3)]
    pieces = []
    for c in range(fine_ch):
        total = jnp.zeros(offset.shape, F32)
        for part, mask in zip(rows_of(backward, c), masks):
            total = jnp.where(mask, jnp.broadcast_to(part, offset.shape), total)
        pieces.append(total)
    back_ref[...] = jnp.concatenate(pieces, 0).astype(BF16)


def table_kernel(
    place_ref, table_hbm, cot_hbm, wide_ref, first_ref, second_ref, table_ref, sems
):
    last = cot_hbm.shape[1] - 1
    even = lax.rem(place_ref[0], 2) == 0
    fine_ch, chans, subs = table_ref.shape
    half = fine_ch // 2
    loads = [
        pltpu.make_async_copy(
            table_hbm.at[n * half : (n + 1) * half],
            table_ref.at[n * half : (n + 1) * half],
            sems.at[n],
        )
        for n in range(2)
    ]
    planes = [
        pltpu.make_async_copy(cot_hbm.at[:, jnp.where(even, last, 0)], first_ref, sems.at[2]),
        pltpu.make_async_copy(cot_hbm.at[:, jnp.where(even, 0, last)], second_ref, sems.at[3]),
    ]
    for copy in loads + planes:
        copy.start()
    pairs = RATIO * RATIO
    row = row_index(subs)
    position = row % pairs // RATIO * pairs + (RATIO - 1 - row % RATIO) * RATIO + row // pairs
    pick = one_hot(iota((subs, subs), 1) == position)
    two = 2 * chans
    low = iota((pairs, two), 1) < chans
    for n in range(2):
        loads[n].wait()
        part = table_ref[n * half : (n + 1) * half].reshape(half * chans, subs)
        turned = dot_nt(pick, part)
        for p in range(half // 2):
            lanes = slice(p * two, (p + 1) * two)
            top = (n * half // 2 + p) * SPAN
            for q in range(RATIO // 2):
                even = turned[2 * q * pairs : (2 * q + 1) * pairs, lanes]
                odd = turned[(2 * q + 1) * pairs : (2 * q + 2) * pairs, lanes]
                first = jnp.where(low, even, pltpu.roll(odd, chans, 1))
                second = jnp.where(low, pltpu.roll(even, chans, 1), odd)
                both = jnp.concatenate(
                    [first.reshape(RATIO, RATIO, two), second.reshape(RATIO, RATIO, two)], 1
                )
                wide_ref[:, top : top + SPAN, q * two : (q + 1) * two] = both.astype(BF16)
    for copy in planes:
        copy.wait()


def shift_rows(values, width):
    count = values.shape[0]
    block = min(count, 256)
    row = iota((block, block), 0)
    column = iota((block, block), 1)
    down = one_hot((column == row - 1) & (row % width > 0))
    up = one_hot((column == row + 1) & (row % width < width - 1))
    pieces = []
    for first in range(0, count, block):
        part = values[first : first + block]
        pieces.append(
            jnp.concatenate([dot(down, part).astype(BF16), part, dot(up, part).astype(BF16)], 1)
        )
    return jnp.concatenate(pieces, 0)


def store_padded(ref, values, width):
    rows, lanes = ref.shape
    ref[0:width] = jnp.zeros((width, lanes), BF16)
    ref[rows - width : rows] = jnp.zeros((width, lanes), BF16)
    ref[width : rows - width] = shift_rows(values, width)


def encode_kernel(
    place_ref, dec_ref, enc_ref, wide_ref, *refs, depth
):
    *dark_refs, conv_ref, back_ref, pre_ref, encoded_ref, dark3_ref, up_ref, pad_ref = refs
    planes, width, chans = dark_refs[0].shape[-3:]
    main = wide_ref.shape[1]
    fine_ch = main // RATIO
    cells = planes * width
    fine_width = width * RATIO
    blank = jnp.zeros((chans, chans), BF16)
    weights = []
    for a in range(3):
        rows = []
        for z_out in range(depth):
            blocks = []
            for e in range(3):
                for z_in in range(depth):
                    b = z_in - z_out + 1
                    blocks.append(enc_ref[9 * a + 3 * b + e] if 0 <= b < 3 else blank)
            rows.append(jnp.concatenate(blocks, 1))
        weights.append(jnp.concatenate(rows, 0))
    if len(dark_refs) == 2:
        own, other = (ref[...].reshape(cells, chans) for ref in dark_refs)
        first = place_ref[1] == 0
        parts = [jnp.where(first, own, other), jnp.where(first, other, own)]
    else:
        parts = [dark_refs[0][z].reshape(cells, chans) for z in range(depth)]
    dark = jnp.concatenate(parts, 1)
    store_padded(dark3_ref, dark, width)
    pre = sum(
        dot_nt(dark3_ref[a * width : a * width + cells], weights[a]) for a in range(3)
    )
    pre_ref[...] = pre
    band_taps(dec_ref, conv_ref, back_ref)
    encoded = jax.nn.silu(pre).astype(BF16)
    encoded_ref[...] = encoded
    pad_ref[...] = jnp.zeros(pad_ref.shape, F32)
    for z in range(depth):
        part = encoded[:, z * chans : (z + 1) * chans].astype(F32)
        pad_ref[1 : planes + 1, z + 1] = jnp.concatenate([part, part], 1).reshape(
            planes, width, 2 * chans
        )
    first_x = place_ref[0]
    first_z = place_ref[1]
    repeat = one_hot(
        iota((fine_width, width), 0) // RATIO == iota((fine_width, width), 1)
    )
    two = 2 * chans
    cells = jnp.concatenate(
        [pad_ref[first_x + dx, first_z + dz] for dx in range(3) for dz in range(3)], 1
    )
    repeated = dot(repeat, cells.astype(BF16))
    lane = iota((fine_width, two), 1) // chans
    phase = iota((fine_width, two), 0) % RATIO
    low = iota((fine_ch, RATIO, fine_width), 1) < 2
    columns = []
    for n in range(9):
        cell = repeated[:, n * two : (n + 1) * two]
        columns.append(
            jnp.concatenate(
                [jnp.where(phase == 2 * q + lane, cell, 0.0) for q in range(RATIO // 2)], 1
            ).astype(BF16)
        )
    plan = (
        (0, 2, ((1, 2), (2, RATIO + 2))),
        (2, RATIO - 4, ((1, 2),)),
        (RATIO - 2, 2, ((0, 2 - RATIO), (1, 2))),
    )
    for first, count, needed in plan:
        field = dot_nt(
            wide_ref[first : first + count].reshape(count * main, RATIO * chans),
            jnp.concatenate([columns[3 * dx + dz] for dx, _ in needed for dz in range(3)], 0),
        )
        for n in range(count):
            for m, (_, base) in enumerate(needed):
                under, own, over = (
                    pltpu.roll(
                        field[
                            n * main : (n + 1) * main,
                            (3 * m + dz) * fine_width : (3 * m + dz + 1) * fine_width,
                        ].reshape(fine_ch, RATIO, fine_width),
                        2,
                        1,
                    )
                    for dz in range(3)
                )
                plane = jnp.concatenate([jnp.where(low, over, own), jnp.where(low, own, under)], 1)
                store_shifts(up_ref, base + first + n, plane.reshape(fine_ch * SPAN, fine_width))


def decode_kernel(cot_ref, conv_ref, up_ref, grad_ref, outer_ref, edge_ref, total_ref):
    fine_ch, planes, depth, width = cot_ref.shape
    main = fine_ch * depth
    own = planes * width

    def convolve(first, count):
        low, high = first * width, (first + count) * width
        return sum(
            dot(conv_ref[a], up_ref[:, a * width + low : a * width + high]) for a in range(3)
        )

    step = 2
    ahead = convolve(0, step)
    for x in range(planes + 2):
        if x % step == 0:
            pre = ahead
            if x + step < planes + 2:
                ahead = convolve(x + step, step)
        here = pre[:, x % step * width : (x % step + 1) * width]
        if 0 < x <= planes:
            cot = cot_ref[:, x - 1].astype(F32).reshape(main, width)
            grad = (cot * slope_of(here[:main])).astype(BF16)
            store_shifts(grad_ref, x - 1, grad.astype(F32))
            edge_ref[:, (x - 1) * width : x * width] = here[main:]
        else:
            outer_ref[0 if x == 0 else 1] = here
    grads = jnp.concatenate([grad_ref[e * main : (e + 1) * main] for e in (2, 1, 0)], 0)
    taps = fine_ch * SPAN
    sums = []
    for a in range(3):
        fields = up_ref[taps : 2 * taps, (a + 1) * width : (a + 1) * width + own]
        product = dot_nt(grads, fields)
        halves = []
        for first in range(0, taps, 128):
            part = product[:, first : first + 128].reshape(3 * fine_ch, RATIO, 128)
            halves.append(jnp.sum(pltpu.roll(part, 0, 2, stride=1, stride_axis=1), 1))
        sums.append(jnp.concatenate(halves, 1))
    shape = (3 * fine_ch, taps)
    fold = one_hot(
        iota(shape, 1)
        == row_index(shape[0]) % fine_ch * SPAN + 10 - row_index(shape[0]) // fine_ch
    )
    total = sum(dot_nt(fold, part) for part in split(jnp.concatenate(sums, 0)))
    total_ref[...] = jnp.concatenate(
        [total[b * fine_ch : (b + 1) * fine_ch] for b in range(3)], 1
    )


def spread_kernel(
    place_ref, cot_ref, x_low_ref, x_high_ref, z_low_ref, z_high_ref, own_ref, outer_ref, edge_ref,
    back_ref, wide_ref, send_hbm, grad_ref, send_ref, cells_ref, sems, *, planes_x, planes_z
):
    fine_ch, planes, depth, width = cot_ref.shape
    main = fine_ch * depth
    own = planes * width
    rows = outer_ref.shape[1]
    chans = wide_ref.shape[2] // RATIO
    owners, chunk, _ = send_hbm.shape
    span = chunk - RATIO
    own_x = place_ref[0]
    own_z = place_ref[1]
    valid = (own_z > 0, own_z < planes_z - 1)
    for e in range(3):
        grad_ref[e * rows : e * rows + main, width : width + own] = own_ref[
            e * main : (e + 1) * main
        ]
    for x, outer in ((0, x_low_ref), (planes + 1, x_high_ref)):
        inside = own_x > 0 if x == 0 else own_x < planes_x - 1
        cot = [jnp.where(inside, outer[:main].astype(F32), 0.0)]
        for side in range(2):
            first = main + side * (outer.shape[0] - main - fine_ch)
            corner = outer[first : first + fine_ch].astype(F32)
            cot.append(jnp.where(valid[side] & inside, corner, 0.0))
        pre = outer_ref[0 if x == 0 else 1]
        grad = (jnp.concatenate(cot, 0) * slope_of(pre)).astype(BF16)
        store_shifts(grad_ref, x, grad.astype(F32))
    shape = (main, main)
    turn = iota(shape, 1) == row_index(main) % fine_ch * planes + row_index(main) // fine_ch
    sides = [
        dot(one_hot(turn & valid[side]), ref[...].astype(F32).reshape(main, width).astype(BF16))
        for side, ref in enumerate((z_low_ref, z_high_ref))
    ]
    for x in range(planes):
        cot = jnp.concatenate([side[x * fine_ch : (x + 1) * fine_ch] for side in sides], 0)
        grad = (cot * slope_of(edge_ref[:, x * width : (x + 1) * width])).astype(BF16)
        store_shifts(grad_ref, x + 1, grad.astype(F32), main, rows)
    taps = grad_ref.shape[0]
    back = sum(
        dot(back_ref[:, a * taps : (a + 1) * taps], grad_ref[:, a * width : a * width + own])
        for a in range(3)
    )
    cot = jnp.concatenate(
        [cot_ref[:, x].astype(F32).reshape(main, width) for x in range(planes)], 1
    )
    up = (cot + back).astype(BF16)
    row = row_index(main)
    order = jnp.concatenate(
        [row % fine_ch * RATIO + row // fine_ch, row // RATIO * RATIO + RATIO - 1 - row % RATIO], 0
    )
    both = dot(one_hot(iota((2 * main, main), 1) == order), up).astype(BF16)
    turned, flipped = both[:main], both[main:]
    for owner in range(owners):
        first = owner * RATIO * RATIO // owners
        x = first // RATIO
        top = first % RATIO * fine_ch
        send_ref[owner] = turned[top : top + span, x * width : (x + 1) * width]
    store = pltpu.make_async_copy(send_ref, send_hbm.at[:, :span], sems.at[0])
    store.start()
    parts = dot_tn(
        jnp.concatenate([flipped[:, x * width : (x + 1) * width] for x in range(planes)], 0),
        wide_ref[...].reshape(planes * main, RATIO * chans),
    )
    two = 2 * chans
    phase = iota((width, two), 0) % RATIO
    lane = iota((width, two), 1) // chans
    both = sum(
        jnp.where(phase == 2 * q + lane, parts[:, q * two : (q + 1) * two], 0.0)
        for q in range(RATIO // 2)
    )
    cells = jnp.sum((both + pltpu.roll(both, chans, 1)).reshape(-1, RATIO, two), 1)
    half = cells.shape[0] // 2
    cells = jnp.where(iota((half, two), 1) < chans, cells[:half], cells[half:]).astype(BF16)
    for owner in range(owners):
        cells_ref[owner] = cells
    last = pltpu.make_async_copy(cells_ref, send_hbm.at[:, span:], sems.at[1])
    last.start()
    store.wait()
    last.wait()


def widen_kernel(
    place_ref, encoded_ref, pre_ref, enc_ref, out_ref, slope_ref, taps_ref, order_ref
):
    cells, lanes = encoded_ref.shape
    chans = enc_ref.shape[1]
    depth = lanes // chans
    block = 32
    repeat = one_hot(
        iota((block * RATIO, block), 0) // RATIO == iota((block * RATIO, block), 1)
    )
    for first in range(0, cells, block):
        out_ref[first * RATIO : (first + block) * RATIO] = dot(
            repeat, encoded_ref[first : first + block]
        ).astype(BF16)
    slope_ref[...] = slope_of(pre_ref[...])
    own_z = place_ref[1]
    for a in range(3):
        for e in range(3):
            for z in range(depth):
                b = z - own_z + 1
                tap = enc_ref[26 - (9 * a + 3 * jnp.clip(b, 0, 2) + e)]
                first = (3 * e * depth + 3 * z) * chans // 3
                taps_ref[a, first : first + chans] = jnp.where(
                    (b >= 0) & (b <= 2), tap.astype(F32), 0.0
                ).astype(BF16)
    shape = order_ref.shape
    fine_ch = shape[0] // 27
    step = shape[1] // fine_ch
    row = row_index(shape[0])
    tap = row // fine_ch
    tap = tap // 9 * 3 + tap // 3 % 3 * 9 + tap % 3
    order_ref[...] = one_hot(iota(shape, 1) == row % fine_ch * step + tap)


def final_kernel(order_ref, done_ref, *refs, scale):
    *parts, out_ref = refs
    total = sum(part[...] for part in parts) * scale
    fine_ch = out_ref.shape[0]
    field = dot(jnp.concatenate(split(total), 0), order_ref[...])
    field = field[:fine_ch] + field[fine_ch : 2 * fine_ch] + field[2 * fine_ch :]
    step = field.shape[1] // fine_ch
    for o in range(fine_ch):
        first = o * step // 128 * 128
        part = field[:, first : first + 128]
        if o * step > first:
            part = pltpu.roll(part, 128 - (o * step - first), 1)
        out_ref[o] = part[:, :27]


def finish_kernel(
    got_ref, spread_ref, slope_ref, dark3_ref, taps_ref,
    dark_out, enc_out, up_out, done_ref, pad_ref, *, scale
):
    done_ref[...] = jnp.zeros(done_ref.shape, F32)
    owners, chunk, fine_width = got_ref.shape
    cells, lanes = slope_ref.shape
    chans = taps_ref.shape[2]
    depth = lanes // chans
    planes = owners // depth
    width = cells // planes
    span = chunk - RATIO
    fine_ch = up_out.shape[1]
    rows = []
    for x in range(planes):
        parts = [got_ref[x * depth + z, span:].astype(F32) for z in range(depth)]
        for half in range(2):
            rows.append(
                jnp.concatenate([part[:, half * chans : (half + 1) * chans] for part in parts], 1)
            )
    grad = (jnp.concatenate(rows, 0) * slope_ref[...]).astype(BF16)
    store_padded(pad_ref, grad, width)
    dark_out[...] = sum(
        dot(pad_ref[a * width : a * width + cells], taps_ref[a]) for a in range(3)
    ).reshape(planes, width, chans)
    turned = grad.astype(F32).T.astype(BF16)
    for a in range(3):
        product = dot(turned, dark3_ref[a * width : a * width + cells]) * scale
        for b in range(3):
            for e in range(3):
                total = None
                for z in range(depth):
                    z_in = z + b - 1
                    if 0 <= z_in < depth:
                        first = (e * depth + z_in) * chans
                        part = product[z * chans : (z + 1) * chans, first : first + chans]
                        total = part if total is None else total + part
                enc_out[9 * a + 3 * b + e] = (
                    jnp.zeros((chans, chans), F32) if total is None else total
                )
    pairs = span // fine_ch
    lane = iota((RATIO * fine_ch, fine_width), 1) % RATIO
    masks = one_hot(lane == iota((RATIO * fine_ch, fine_width), 0) // fine_ch)
    sums = None
    for z in range(depth):
        pieces = []
        for x in range(planes):
            arrived = got_ref[x * depth + z, :span]
            pieces.append(
                jnp.concatenate(
                    [
                        jnp.concatenate([arrived[p * fine_ch : (p + 1) * fine_ch]] * RATIO, 0)
                        * masks
                        for p in range(pairs)
                    ],
                    0,
                )
            )
        part = dot(jnp.concatenate(pieces, 1), spread_ref[...])
        part = part[:, z * chans : (z + 1) * chans]
        sums = part if sums is None else sums + part
    up_out[...] = (sums * scale).reshape(pairs * RATIO, fine_ch, chans)


def call(kernel, out_shape, args, scratch=(), scalars=0, flops=1e8, hbm=(), hbm_out=()):
    specs = [pl.BlockSpec(memory_space=pltpu.SMEM)] * scalars
    specs += [
        pl.BlockSpec(memory_space=pltpu.HBM if n in hbm else VMEM)
        for n in range(scalars, len(args))
    ]
    args = [
        pltpu.with_memory_space_constraint(arg, pltpu.HBM) if n in hbm else arg
        for n, arg in enumerate(args)
    ]
    return pl.pallas_call(
        kernel,
        out_shape=[jax.ShapeDtypeStruct(*s) for s in out_shape],
        in_specs=specs,
        out_specs=[
            pl.BlockSpec(memory_space=pltpu.HBM if n in hbm_out else VMEM)
            for n in range(len(out_shape))
        ],
        scratch_shapes=list(scratch),
        compiler_params=pltpu.CompilerParams(vmem_limit_bytes=VMEM_LIMIT),
        cost_estimate=pl.CostEstimate(
            flops=int(flops), bytes_accessed=2_000_000, transcendentals=0
        ),
    )(*args)


def shift(block, axis, by):
    count = lax.axis_size(axis)
    pairs = [(i, i + by) for i in range(count) if 0 <= i + by < count]
    return lax.ppermute(block, axis, pairs)


def swapped(value, step):
    count = lax.axis_size(AXES)
    return lax.ppermute(value, AXES, [(i, i ^ step) for i in range(count)])


def exchange_depth(dark_rows, cotangent):
    count = lax.axis_size("narrow")
    last = cotangent.shape[2] - 1
    if count == 2:
        swap = [(0, 1), (1, 0)]
        dark = lax.ppermute(dark_rows, "narrow", swap)
        z = jnp.where(lax.axis_index("narrow") == 0, last, 0)
        face = lax.ppermute(lax.dynamic_index_in_dim(cotangent, z, 2, False), "narrow", swap)
        return (dark_rows, dark), (face,)
    planes = lax.all_gather(dark_rows, "narrow", axis=0)
    low = shift(cotangent[:, :, last], "narrow", 1)
    return (planes,), (low, shift(cotangent[:, :, 0], "narrow", -1))


def exchange_width(planes, faces):
    count = lax.axis_size("wide")
    depth = lax.axis_size("narrow")
    last = faces[0].shape[1] - 1
    even = lax.axis_index("wide") % 2 == 0
    got = []
    for odd in range(2):
        partner = {}
        for x in range(count):
            other = x + 1 if x % 2 == odd else x - 1
            for z in range(depth):
                if 0 <= other < count:
                    partner[x * depth + z] = other * depth + z
                elif depth % 2 == 0:
                    partner[x * depth + z] = x * depth + (z ^ 1)
        plane = jnp.where(even, 0, last) if odd else jnp.where(even, last, 0)
        edges = [lax.dynamic_index_in_dim(face, plane, 1, False) for face in faces]
        send = jnp.concatenate([planes[odd], *edges], 0)
        got.append(lax.ppermute(send, AXES, list(partner.items())))
    return jnp.where(even, got[1], got[0]), jnp.where(even, got[0], got[1])


def on_device(dark, w_enc, up_weight, w_dec, cotangent):
    chans, planes, own_depth, width = dark.shape
    fine_ch, own_fine, fine_depth, fine_width = cotangent.shape
    subs = up_weight.shape[0]
    depth = lax.axis_size("narrow")
    owners = lax.axis_size(AXES)
    cells = planes * width
    lanes = depth * chans
    own_rows = subs // owners
    where = jnp.stack([lax.axis_index("wide"), lax.axis_index("narrow")]).astype(jnp.int32)

    dark_planes, faces = exchange_depth(dark[:, :, 0].transpose(1, 2, 0), cotangent)

    rows = fine_ch * (RATIO + 2)
    taps = fine_ch * SPAN
    main = fine_ch * RATIO
    face = (fine_ch * fine_depth, fine_width)
    outer = (fine_ch, fine_depth, fine_width)
    wide_table, first_plane, second_plane = call(
        table_kernel,
        [((RATIO, main, RATIO * chans), BF16), (outer, BF16), (outer, BF16)],
        (where, up_weight.transpose(1, 2, 0), cotangent),
        scratch=[VMEM((fine_ch, chans, subs), BF16), pltpu.SemaphoreType.DMA((4,))],
        scalars=1,
        hbm=(1, 2),
        flops=1e9,
    )
    outer_planes = [plane.reshape(face) for plane in (first_plane, second_plane)]
    x_low, x_high = exchange_width(outer_planes, faces)
    conv, back, enc_pre, encoded, dark3, upsampled = call(
        functools.partial(encode_kernel, depth=depth),
        [
            ((3, rows, 3 * taps), BF16),
            ((main, 9 * rows), BF16),
            ((cells, lanes), F32),
            ((cells, lanes), BF16),
            ((cells + 2 * width, 3 * lanes), BF16),
            ((3 * taps, (RATIO + 4) * fine_width), BF16),
        ],
        (where, w_dec.transpose(1, 2, 0), w_enc, wide_table, *dark_planes),
        scratch=[VMEM((planes + 2, depth + 2, width, 2 * chans), F32)],
        scalars=1,
        flops=2e9,
    )
    own = own_fine * fine_width
    dec_grad, outer_pre, edge_pre, dec_sum = call(
        decode_kernel,
        [
            ((3 * main, own), BF16),
            ((2, rows, fine_width), F32),
            ((rows - main, own), F32),
            ((fine_ch, 27 * fine_ch), F32),
        ],
        (cotangent, conv, upsampled),
        flops=2e9,
    )
    chunk = max(1, RATIO * RATIO // owners) * fine_ch + RATIO
    (send,) = call(
        functools.partial(spread_kernel, planes_x=planes, planes_z=depth),
        [((owners, chunk, fine_width), BF16)],
        (
            where, cotangent, x_low, x_high, faces[0], faces[-1], dec_grad, outer_pre, edge_pre,
            back, wide_table,
        ),
        scratch=[
            VMEM((3 * rows, own + 2 * fine_width), BF16),
            VMEM((owners, chunk - RATIO, fine_width), BF16),
            VMEM((owners, RATIO, fine_width), BF16),
            pltpu.SemaphoreType.DMA((2,)),
        ],
        scalars=1,
        flops=2e9,
        hbm_out=(0,),
    )
    steps = [1 << n for n in range(owners.bit_length() - 1)]
    if owners & (owners - 1):
        dec_sum = lax.psum(dec_sum, AXES)
        steps = []
    steps = sorted(steps)
    one_by_one = steps[: max(1, len(steps) - LAST_STEPS)]
    for step in one_by_one:
        other = swapped(dec_sum, step)
        if step == steps[0]:
            send, other, dec_sum = lax.optimization_barrier((send, other, dec_sum))
        dec_sum = dec_sum + other
    sums = [0]
    for step in steps[len(one_by_one) :]:
        sums += [step + other for other in sums]
    received = [swapped(dec_sum, step) for step in sums[1:]]
    got = lax.all_to_all(send, AXES, 0, 0, tiled=True)
    enc_spread, enc_slope, enc_taps, order = call(
        widen_kernel,
        [
            ((cells * RATIO, lanes), BF16),
            ((cells, lanes), F32),
            ((3, 3 * lanes, chans), BF16),
            ((27 * fine_ch, 32 * fine_ch), BF16),
        ],
        (where, encoded, enc_pre, w_enc),
        scalars=1,
        flops=1e9,
    )
    coarse_scale = 1.0 / math.sqrt(cells * depth)
    fine_scale = 1.0 / math.sqrt(cells * depth * subs)
    pairs = (chunk - RATIO) // fine_ch
    grad_dark, grad_enc, grad_up, done = call(
        functools.partial(finish_kernel, scale=coarse_scale),
        [
            ((planes, width, chans), F32),
            ((27, chans, chans), F32),
            ((pairs * RATIO, fine_ch, chans), F32),
            ((8, 128), F32),
        ],
        (got, enc_spread, enc_slope, dark3, enc_taps),
        scratch=[VMEM((cells + 2 * width, 3 * lanes), BF16)],
        flops=2e9,
    )
    if own_rows < pairs * RATIO:
        own = lax.axis_index(AXES) * own_rows % RATIO
        grad_up = lax.dynamic_slice_in_dim(grad_up, own, own_rows, 0)
    (grad_dec,) = call(
        functools.partial(final_kernel, scale=fine_scale),
        [((fine_ch, fine_ch, 27), F32)],
        (order, done, dec_sum, *received),
        flops=1e8,
    )
    return grad_dark.transpose(2, 0, 1)[:, :, None], grad_enc, grad_up, grad_dec.transpose(2, 0, 1)


def solution(mesh):
    in_specs = (P(None, None, "narrow", None), P(), P(), P(), P(None, "wide", "narrow", None))
    out_specs = (P(None, None, "narrow", None), P(), P(("wide", "narrow"), None, None), P())
    return jax.shard_map(
        on_device, mesh=mesh, in_specs=in_specs, out_specs=out_specs, check_vma=False
    )
```

```python
import functools
import math

import jax
import jax.numpy as jnp
from jax import lax
from jax.experimental import pallas as pl
from jax.experimental.pallas import tpu as pltpu
from jax.sharding import PartitionSpec as P

RATIO = 8
SPAN = 16
LAST_STEPS = 2
F32 = jnp.float32
BF16 = jnp.bfloat16
VMEM_LIMIT = 48 * 1024 * 1024
VMEM = pltpu.VMEM
AXES = ("wide", "narrow")


def slope_of(values):
    sigma = jax.nn.sigmoid(values)
    return sigma * (1.0 + values * (1.0 - sigma))


def dot(left, right):
    return jnp.dot(left, right, preferred_element_type=F32)


def dot_nt(left, right):
    return lax.dot_general(left, right, (((1,), (1,)), ((), ())), preferred_element_type=F32)


def dot_tn(left, right):
    return lax.dot_general(left, right, (((0,), (0,)), ((), ())), preferred_element_type=F32)


def split(values):
    high = values.astype(BF16)
    rest = values - high.astype(F32)
    middle = rest.astype(BF16)
    return high, middle, (rest - middle.astype(F32)).astype(BF16)


def iota(shape, dim):
    return lax.broadcasted_iota(jnp.int32, shape, dim)


def row_index(count):
    return iota((count, 1), 0)


def lane_index(count):
    return iota((1, count), 1)


def one_hot(condition):
    return jnp.where(condition, 1.0, 0.0).astype(BF16)


def place(index, fine_ch):
    main = fine_ch * RATIO
    over = index - main
    channel = jnp.where(index < main, index // RATIO, over % fine_ch)
    z = jnp.where(index < main, index % RATIO, jnp.where(over < fine_ch, -1, RATIO))
    return channel, z


def lane_shift(values, by):
    width = values.shape[1]
    lane = iota(values.shape, 1)
    if by > 0:
        return jnp.where(lane < by, 0.0, pltpu.roll(values, by, 1))
    return jnp.where(lane >= width + by, 0.0, pltpu.roll(values, width + by, 1))


def store_shifts(ref, block, values, top=0, stride=None):
    rows, width = values.shape
    stride = stride or rows
    lanes = slice(block * width, (block + 1) * width)
    parts = (lane_shift(values, 1), values, lane_shift(values, -1))
    for e, part in enumerate(parts):
        ref[top + e * stride : top + e * stride + rows, lanes] = part.astype(BF16)


def band_taps(dec_ref, conv_ref, back_ref):
    fine_ch = dec_ref.shape[0]
    rows = fine_ch * (RATIO + 2)
    square = fine_ch * fine_ch
    group = 9 * fine_ch
    block = 256
    column = lane_index(6 * block)
    rest = column % block
    base = 9 * (rest // (3 * fine_ch)) + (rest // fine_ch) % 3 + 3 * (column // block % 3)
    tap = jnp.where(column < 3 * block, base, 26 - base)
    chosen_taps = one_hot(iota((27, 6 * block), 0) == jnp.where(rest < group, tap, -1))
    cell = row_index(square)
    last_index = iota((square, block), 1) % fine_ch
    same_in = last_index == cell % fine_ch
    same_out = last_index == cell // fine_ch
    shape = (fine_ch, square)
    pick_out = one_hot(iota(shape, 0) == lane_index(square) // fine_ch)
    pick_in = one_hot(iota(shape, 0) == lane_index(square) % fine_ch)
    wide = group * SPAN
    spread = one_hot(iota((group, wide), 0) == lane_index(wide) // SPAN)
    spread = jnp.concatenate([spread, jnp.zeros((block - group, wide), BF16)], 0)
    back_wide = 9 * rows
    column = lane_index(back_wide)
    channel, _ = place(column % rows, fine_ch)
    spread_back = one_hot(iota((group, back_wide), 0) == column // rows * fine_ch + channel)
    spread_back = jnp.concatenate([spread_back, jnp.zeros((block - group, back_wide), BF16)], 0)
    chosen = dot(dec_ref[...].reshape(square, 27), chosen_taps)
    taps = []
    for n in range(6):
        part = chosen[:, n * block : (n + 1) * block]
        part = jnp.where(same_in if n < 3 else same_out, part, 0.0).astype(BF16)
        taps.append(dot(pick_out if n < 3 else pick_in, part).astype(BF16))
    forward = dot(jnp.concatenate(taps[:3], 0), spread)
    backward = dot(jnp.concatenate(taps[3:], 0), spread_back)

    def banded(parts, masks):
        blocks = []
        for first in range(0, parts[0].shape[1], 128):
            total = jnp.zeros(masks[0].shape, F32)
            for part, mask in zip(parts, masks):
                part = jnp.broadcast_to(part[:, first : first + 128], mask.shape)
                total = jnp.where(mask, part, total)
            blocks.append(total)
        return jnp.concatenate(blocks, 1)

    def rows_of(field, channel):
        return [
            field[b * fine_ch + channel : b * fine_ch + channel + 1] for b in range(3)
        ]

    slot = iota((RATIO, 128), 1) % SPAN
    masks = [10 - slot - iota((RATIO, 128), 0) == b for b in range(3)]
    pieces = [banded(rows_of(forward, o), masks) for o in range(fine_ch)]
    slot = iota((fine_ch, 128), 1) % SPAN
    parts = [forward[b * fine_ch : (b + 1) * fine_ch] for b in range(3)]
    pieces += [banded(parts, [base - slot == b for b in range(3)]) for base in (11, 2)]
    field = jnp.concatenate(pieces, 0).astype(BF16)
    for a in range(3):
        conv_ref[a] = field[:, a * (wide // 3) : (a + 1) * (wide // 3)]
    _, z_in = place(lane_index(back_wide) % rows, fine_ch)
    offset = z_in - iota((RATIO, back_wide), 0) + 1
    masks = [offset == b for b in range(3)]
    pieces = []
    for c in range(fine_ch):
        total = jnp.zeros(offset.shape, F32)
        for part, mask in zip(rows_of(backward, c), masks):
            total = jnp.where(mask, jnp.broadcast_to(part, offset.shape), total)
        pieces.append(total)
    back_ref[...] = jnp.concatenate(pieces, 0).astype(BF16)


def table_kernel(
    place_ref, table_hbm, cot_hbm, wide_ref, first_ref, second_ref, table_ref, sems
):
    last = cot_hbm.shape[1] - 1
    even = lax.rem(place_ref[0], 2) == 0
    fine_ch, chans, subs = table_ref.shape
    half = fine_ch // 2
    loads = [
        pltpu.make_async_copy(
            table_hbm.at[n * half : (n + 1) * half],
            table_ref.at[n * half : (n + 1) * half],
            sems.at[n],
        )
        for n in range(2)
    ]
    planes = [
        pltpu.make_async_copy(cot_hbm.at[:, jnp.where(even, last, 0)], first_ref, sems.at[2]),
        pltpu.make_async_copy(cot_hbm.at[:, jnp.where(even, 0, last)], second_ref, sems.at[3]),
    ]
    for copy in loads + planes:
        copy.start()
    pairs = RATIO * RATIO
    row = row_index(subs)
    position = row % pairs // RATIO * pairs + (RATIO - 1 - row % RATIO) * RATIO + row // pairs
    pick = one_hot(iota((subs, subs), 1) == position)
    two = 2 * chans
    low = iota((pairs, two), 1) < chans
    for n in range(2):
        loads[n].wait()
        part = table_ref[n * half : (n + 1) * half].reshape(half * chans, subs)
        turned = dot_nt(pick, part)
        for p in range(half // 2):
            lanes = slice(p * two, (p + 1) * two)
            top = (n * half // 2 + p) * SPAN
            for q in range(RATIO // 2):
                even = turned[2 * q * pairs : (2 * q + 1) * pairs, lanes]
                odd = turned[(2 * q + 1) * pairs : (2 * q + 2) * pairs, lanes]
                first = jnp.where(low, even, pltpu.roll(odd, chans, 1))
                second = jnp.where(low, pltpu.roll(even, chans, 1), odd)
                both = jnp.concatenate(
                    [first.reshape(RATIO, RATIO, two), second.reshape(RATIO, RATIO, two)], 1
                )
                wide_ref[:, top : top + SPAN, q * two : (q + 1) * two] = both.astype(BF16)
    for copy in planes:
        copy.wait()


def shift_rows(values, width):
    count = values.shape[0]
    block = min(count, 256)
    row = iota((block, block), 0)
    column = iota((block, block), 1)
    down = one_hot((column == row - 1) & (row % width > 0))
    up = one_hot((column == row + 1) & (row % width < width - 1))
    pieces = []
    for first in range(0, count, block):
        part = values[first : first + block]
        pieces.append(
            jnp.concatenate([dot(down, part).astype(BF16), part, dot(up, part).astype(BF16)], 1)
        )
    return jnp.concatenate(pieces, 0)


def store_padded(ref, values, width):
    rows, lanes = ref.shape
    ref[0:width] = jnp.zeros((width, lanes), BF16)
    ref[rows - width : rows] = jnp.zeros((width, lanes), BF16)
    ref[width : rows - width] = shift_rows(values, width)


def encode_kernel(
    place_ref, dec_ref, enc_ref, wide_ref, *refs, depth
):
    *dark_refs, conv_ref, back_ref, pre_ref, encoded_ref, dark3_ref, up_ref, pad_ref = refs
    planes, width, chans = dark_refs[0].shape[-3:]
    main = wide_ref.shape[1]
    fine_ch = main // RATIO
    cells = planes * width
    fine_width = width * RATIO
    blank = jnp.zeros((chans, chans), BF16)
    weights = []
    for a in range(3):
        rows = []
        for z_out in range(depth):
            blocks = []
            for e in range(3):
                for z_in in range(depth):
                    b = z_in - z_out + 1
                    blocks.append(enc_ref[9 * a + 3 * b + e] if 0 <= b < 3 else blank)
            rows.append(jnp.concatenate(blocks, 1))
        weights.append(jnp.concatenate(rows, 0))
    if len(dark_refs) == 2:
        own, other = (ref[...].reshape(cells, chans) for ref in dark_refs)
        first = place_ref[1] == 0
        parts = [jnp.where(first, own, other), jnp.where(first, other, own)]
    else:
        parts = [dark_refs[0][z].reshape(cells, chans) for z in range(depth)]
    dark = jnp.concatenate(parts, 1)
    store_padded(dark3_ref, dark, width)
    pre = sum(
        dot_nt(dark3_ref[a * width : a * width + cells], weights[a]) for a in range(3)
    )
    pre_ref[...] = pre
    band_taps(dec_ref, conv_ref, back_ref)
    encoded = jax.nn.silu(pre).astype(BF16)
    encoded_ref[...] = encoded
    pad_ref[...] = jnp.zeros(pad_ref.shape, F32)
    for z in range(depth):
        part = encoded[:, z * chans : (z + 1) * chans].astype(F32)
        pad_ref[1 : planes + 1, z + 1] = jnp.concatenate([part, part], 1).reshape(
            planes, width, 2 * chans
        )
    first_x = place_ref[0]
    first_z = place_ref[1]
    repeat = one_hot(
        iota((fine_width, width), 0) // RATIO == iota((fine_width, width), 1)
    )
    two = 2 * chans
    cells = jnp.concatenate(
        [pad_ref[first_x + dx, first_z + dz] for dx in range(3) for dz in range(3)], 1
    )
    repeated = dot(repeat, cells.astype(BF16))
    lane = iota((fine_width, two), 1) // chans
    phase = iota((fine_width, two), 0) % RATIO
    low = iota((fine_ch, RATIO, fine_width), 1) < 2
    columns = []
    for n in range(9):
        cell = repeated[:, n * two : (n + 1) * two]
        columns.append(
            jnp.concatenate(
                [jnp.where(phase == 2 * q + lane, cell, 0.0) for q in range(RATIO // 2)], 1
            ).astype(BF16)
        )
    plan = (
        (0, 2, ((1, 2), (2, RATIO + 2))),
        (2, RATIO - 4, ((1, 2),)),
        (RATIO - 2, 2, ((0, 2 - RATIO), (1, 2))),
    )
    for first, count, needed in plan:
        field = dot_nt(
            wide_ref[first : first + count].reshape(count * main, RATIO * chans),
            jnp.concatenate([columns[3 * dx + dz] for dx, _ in needed for dz in range(3)], 0),
        )
        for n in range(count):
            for m, (_, base) in enumerate(needed):
                under, own, over = (
                    pltpu.roll(
                        field[
                            n * main : (n + 1) * main,
                            (3 * m + dz) * fine_width : (3 * m + dz + 1) * fine_width,
                        ].reshape(fine_ch, RATIO, fine_width),
                        2,
                        1,
                    )
                    for dz in range(3)
                )
                plane = jnp.concatenate([jnp.where(low, over, own), jnp.where(low, own, under)], 1)
                store_shifts(up_ref, base + first + n, plane.reshape(fine_ch * SPAN, fine_width))


def decode_kernel(cot_ref, conv_ref, up_ref, grad_ref, outer_ref, edge_ref, total_ref):
    fine_ch, planes, depth, width = cot_ref.shape
    main = fine_ch * depth
    own = planes * width

    def convolve(first, count):
        low, high = first * width, (first + count) * width
        return sum(
            dot(conv_ref[a], up_ref[:, a * width + low : a * width + high]) for a in range(3)
        )

    step = 2
    ahead = convolve(0, step)
    for x in range(planes + 2):
        if x % step == 0:
            pre = ahead
            if x + step < planes + 2:
                ahead = convolve(x + step, step)
        here = pre[:, x % step * width : (x % step + 1) * width]
        if 0 < x <= planes:
            cot = cot_ref[:, x - 1].astype(F32).reshape(main, width)
            grad = (cot * slope_of(here[:main])).astype(BF16)
            store_shifts(grad_ref, x - 1, grad.astype(F32))
            edge_ref[:, (x - 1) * width : x * width] = here[main:]
        else:
            outer_ref[0 if x == 0 else 1] = here
    grads = jnp.concatenate([grad_ref[e * main : (e + 1) * main] for e in (2, 1, 0)], 0)
    taps = fine_ch * SPAN
    sums = []
    for a in range(3):
        fields = up_ref[taps : 2 * taps, (a + 1) * width : (a + 1) * width + own]
        product = dot_nt(grads, fields)
        halves = []
        for first in range(0, taps, 128):
            part = product[:, first : first + 128].reshape(3 * fine_ch, RATIO, 128)
            halves.append(jnp.sum(pltpu.roll(part, 0, 2, stride=1, stride_axis=1), 1))
        sums.append(jnp.concatenate(halves, 1))
    shape = (3 * fine_ch, taps)
    fold = one_hot(
        iota(shape, 1)
        == row_index(shape[0]) % fine_ch * SPAN + 10 - row_index(shape[0]) // fine_ch
    )
    total = sum(dot_nt(fold, part) for part in split(jnp.concatenate(sums, 0)))
    total_ref[...] = jnp.concatenate(
        [total[b * fine_ch : (b + 1) * fine_ch] for b in range(3)], 1
    )


def spread_kernel(
    place_ref, cot_ref, x_low_ref, x_high_ref, z_low_ref, z_high_ref, own_ref, outer_ref, edge_ref,
    back_ref, wide_ref, send_ref, grad_ref, *, planes_x, planes_z
):
    fine_ch, planes, depth, width = cot_ref.shape
    main = fine_ch * depth
    own = planes * width
    rows = outer_ref.shape[1]
    chans = wide_ref.shape[2] // RATIO
    owners, chunk, _ = send_ref.shape
    span = chunk - RATIO
    own_x = place_ref[0]
    own_z = place_ref[1]
    valid = (own_z > 0, own_z < planes_z - 1)
    for e in range(3):
        grad_ref[e * rows : e * rows + main, width : width + own] = own_ref[
            e * main : (e + 1) * main
        ]
    for x, outer in ((0, x_low_ref), (planes + 1, x_high_ref)):
        inside = own_x > 0 if x == 0 else own_x < planes_x - 1
        cot = [jnp.where(inside, outer[:main].astype(F32), 0.0)]
        for side in range(2):
            first = main + side * (outer.shape[0] - main - fine_ch)
            corner = outer[first : first + fine_ch].astype(F32)
            cot.append(jnp.where(valid[side] & inside, corner, 0.0))
        pre = outer_ref[0 if x == 0 else 1]
        grad = (jnp.concatenate(cot, 0) * slope_of(pre)).astype(BF16)
        store_shifts(grad_ref, x, grad.astype(F32))
    shape = (main, main)
    turn = iota(shape, 1) == row_index(main) % fine_ch * planes + row_index(main) // fine_ch
    sides = [
        dot(one_hot(turn & valid[side]), ref[...].astype(F32).reshape(main, width).astype(BF16))
        for side, ref in enumerate((z_low_ref, z_high_ref))
    ]
    for x in range(planes):
        cot = jnp.concatenate([side[x * fine_ch : (x + 1) * fine_ch] for side in sides], 0)
        grad = (cot * slope_of(edge_ref[:, x * width : (x + 1) * width])).astype(BF16)
        store_shifts(grad_ref, x + 1, grad.astype(F32), main, rows)
    taps = grad_ref.shape[0]
    back = sum(
        dot(back_ref[:, a * taps : (a + 1) * taps], grad_ref[:, a * width : a * width + own])
        for a in range(3)
    )
    cot = jnp.concatenate(
        [cot_ref[:, x].astype(F32).reshape(main, width) for x in range(planes)], 1
    )
    up = (cot + back).astype(BF16)
    row = row_index(main)
    order = jnp.concatenate(
        [row % fine_ch * RATIO + row // fine_ch, row // RATIO * RATIO + RATIO - 1 - row % RATIO], 0
    )
    both = dot(one_hot(iota((2 * main, main), 1) == order), up).astype(BF16)
    turned, flipped = both[:main], both[main:]
    for owner in range(owners):
        first = owner * RATIO * RATIO // owners
        x = first // RATIO
        top = first % RATIO * fine_ch
        send_ref[owner, :span] = turned[top : top + span, x * width : (x + 1) * width]
    parts = dot_tn(
        jnp.concatenate([flipped[:, x * width : (x + 1) * width] for x in range(planes)], 0),
        wide_ref[...].reshape(planes * main, RATIO * chans),
    )
    two = 2 * chans
    phase = iota((width, two), 0) % RATIO
    lane = iota((width, two), 1) // chans
    both = sum(
        jnp.where(phase == 2 * q + lane, parts[:, q * two : (q + 1) * two], 0.0)
        for q in range(RATIO // 2)
    )
    cells = jnp.sum((both + pltpu.roll(both, chans, 1)).reshape(-1, RATIO, two), 1)
    half = cells.shape[0] // 2
    cells = jnp.where(iota((half, two), 1) < chans, cells[:half], cells[half:]).astype(BF16)
    for owner in range(owners):
        send_ref[owner, span:] = cells


def widen_kernel(
    place_ref, encoded_ref, pre_ref, enc_ref, out_ref, slope_ref, taps_ref, order_ref
):
    cells, lanes = encoded_ref.shape
    chans = enc_ref.shape[1]
    depth = lanes // chans
    block = 32
    repeat = one_hot(
        iota((block * RATIO, block), 0) // RATIO == iota((block * RATIO, block), 1)
    )
    for first in range(0, cells, block):
        out_ref[first * RATIO : (first + block) * RATIO] = dot(
            repeat, encoded_ref[first : first + block]
        ).astype(BF16)
    slope_ref[...] = slope_of(pre_ref[...])
    own_z = place_ref[1]
    for a in range(3):
        for e in range(3):
            for z in range(depth):
                b = z - own_z + 1
                tap = enc_ref[26 - (9 * a + 3 * jnp.clip(b, 0, 2) + e)]
                first = (3 * e * depth + 3 * z) * chans // 3
                taps_ref[a, first : first + chans] = jnp.where(
                    (b >= 0) & (b <= 2), tap.astype(F32), 0.0
                ).astype(BF16)
    shape = order_ref.shape
    fine_ch = shape[0] // 27
    step = shape[1] // fine_ch
    row = row_index(shape[0])
    tap = row // fine_ch
    tap = tap // 9 * 3 + tap // 3 % 3 * 9 + tap % 3
    order_ref[...] = one_hot(iota(shape, 1) == row % fine_ch * step + tap)


def final_kernel(order_ref, done_ref, *refs, scale):
    *parts, out_ref = refs
    total = sum(part[...] for part in parts) * scale
    fine_ch = out_ref.shape[0]
    field = dot(jnp.concatenate(split(total), 0), order_ref[...])
    field = field[:fine_ch] + field[fine_ch : 2 * fine_ch] + field[2 * fine_ch :]
    step = field.shape[1] // fine_ch
    for o in range(fine_ch):
        first = o * step // 128 * 128
        part = field[:, first : first + 128]
        if o * step > first:
            part = pltpu.roll(part, 128 - (o * step - first), 1)
        out_ref[o] = part[:, :27]


def finish_kernel(
    got_ref, spread_ref, slope_ref, dark3_ref, taps_ref,
    dark_out, enc_out, up_out, done_ref, pad_ref, *, scale
):
    done_ref[...] = jnp.zeros(done_ref.shape, F32)
    owners, chunk, fine_width = got_ref.shape
    cells, lanes = slope_ref.shape
    chans = taps_ref.shape[2]
    depth = lanes // chans
    planes = owners // depth
    width = cells // planes
    span = chunk - RATIO
    fine_ch = up_out.shape[1]
    rows = []
    for x in range(planes):
        parts = [got_ref[x * depth + z, span:].astype(F32) for z in range(depth)]
        for half in range(2):
            rows.append(
                jnp.concatenate([part[:, half * chans : (half + 1) * chans] for part in parts], 1)
            )
    grad = (jnp.concatenate(rows, 0) * slope_ref[...]).astype(BF16)
    store_padded(pad_ref, grad, width)
    dark_out[...] = sum(
        dot(pad_ref[a * width : a * width + cells], taps_ref[a]) for a in range(3)
    ).reshape(planes, width, chans)
    turned = grad.astype(F32).T.astype(BF16)
    for a in range(3):
        product = dot(turned, dark3_ref[a * width : a * width + cells]) * scale
        for b in range(3):
            for e in range(3):
                total = None
                for z in range(depth):
                    z_in = z + b - 1
                    if 0 <= z_in < depth:
                        first = (e * depth + z_in) * chans
                        part = product[z * chans : (z + 1) * chans, first : first + chans]
                        total = part if total is None else total + part
                enc_out[9 * a + 3 * b + e] = (
                    jnp.zeros((chans, chans), F32) if total is None else total
                )
    pairs = span // fine_ch
    lane = iota((RATIO * fine_ch, fine_width), 1) % RATIO
    masks = one_hot(lane == iota((RATIO * fine_ch, fine_width), 0) // fine_ch)
    sums = None
    for z in range(depth):
        pieces = []
        for x in range(planes):
            arrived = got_ref[x * depth + z, :span]
            pieces.append(
                jnp.concatenate(
                    [
                        jnp.concatenate([arrived[p * fine_ch : (p + 1) * fine_ch]] * RATIO, 0)
                        * masks
                        for p in range(pairs)
                    ],
                    0,
                )
            )
        part = dot(jnp.concatenate(pieces, 1), spread_ref[...])
        part = part[:, z * chans : (z + 1) * chans]
        sums = part if sums is None else sums + part
    up_out[...] = (sums * scale).reshape(pairs * RATIO, fine_ch, chans)


def call(kernel, out_shape, args, scratch=(), scalars=0, flops=1e8, hbm=()):
    specs = [pl.BlockSpec(memory_space=pltpu.SMEM)] * scalars
    specs += [
        pl.BlockSpec(memory_space=pltpu.HBM if n in hbm else VMEM)
        for n in range(scalars, len(args))
    ]
    args = [
        pltpu.with_memory_space_constraint(arg, pltpu.HBM) if n in hbm else arg
        for n, arg in enumerate(args)
    ]
    return pl.pallas_call(
        kernel,
        out_shape=[jax.ShapeDtypeStruct(*s) for s in out_shape],
        in_specs=specs,
        out_specs=[pl.BlockSpec(memory_space=VMEM)] * len(out_shape),
        scratch_shapes=list(scratch),
        compiler_params=pltpu.CompilerParams(vmem_limit_bytes=VMEM_LIMIT),
        cost_estimate=pl.CostEstimate(
            flops=int(flops), bytes_accessed=2_000_000, transcendentals=0
        ),
    )(*args)


def shift(block, axis, by):
    count = lax.axis_size(axis)
    pairs = [(i, i + by) for i in range(count) if 0 <= i + by < count]
    return lax.ppermute(block, axis, pairs)


def swapped(value, step):
    count = lax.axis_size(AXES)
    return lax.ppermute(value, AXES, [(i, i ^ step) for i in range(count)])


def exchange_depth(dark_rows, cotangent):
    count = lax.axis_size("narrow")
    last = cotangent.shape[2] - 1
    if count == 2:
        swap = [(0, 1), (1, 0)]
        dark = lax.ppermute(dark_rows, "narrow", swap)
        z = jnp.where(lax.axis_index("narrow") == 0, last, 0)
        face = lax.ppermute(lax.dynamic_index_in_dim(cotangent, z, 2, False), "narrow", swap)
        return (dark_rows, dark), (face,)
    planes = lax.all_gather(dark_rows, "narrow", axis=0)
    low = shift(cotangent[:, :, last], "narrow", 1)
    return (planes,), (low, shift(cotangent[:, :, 0], "narrow", -1))


def exchange_width(planes, faces):
    count = lax.axis_size("wide")
    depth = lax.axis_size("narrow")
    last = faces[0].shape[1] - 1
    even = lax.axis_index("wide") % 2 == 0
    got = []
    for odd in range(2):
        partner = {}
        for x in range(count):
            other = x + 1 if x % 2 == odd else x - 1
            for z in range(depth):
                if 0 <= other < count:
                    partner[x * depth + z] = other * depth + z
                elif depth % 2 == 0:
                    partner[x * depth + z] = x * depth + (z ^ 1)
        plane = jnp.where(even, 0, last) if odd else jnp.where(even, last, 0)
        edges = [lax.dynamic_index_in_dim(face, plane, 1, False) for face in faces]
        send = jnp.concatenate([planes[odd], *edges], 0)
        got.append(lax.ppermute(send, AXES, list(partner.items())))
    return jnp.where(even, got[1], got[0]), jnp.where(even, got[0], got[1])


def on_device(dark, w_enc, up_weight, w_dec, cotangent):
    chans, planes, own_depth, width = dark.shape
    fine_ch, own_fine, fine_depth, fine_width = cotangent.shape
    subs = up_weight.shape[0]
    depth = lax.axis_size("narrow")
    owners = lax.axis_size(AXES)
    cells = planes * width
    lanes = depth * chans
    own_rows = subs // owners
    where = jnp.stack([lax.axis_index("wide"), lax.axis_index("narrow")]).astype(jnp.int32)

    dark_planes, faces = exchange_depth(dark[:, :, 0].transpose(1, 2, 0), cotangent)

    rows = fine_ch * (RATIO + 2)
    taps = fine_ch * SPAN
    main = fine_ch * RATIO
    face = (fine_ch * fine_depth, fine_width)
    outer = (fine_ch, fine_depth, fine_width)
    wide_table, first_plane, second_plane = call(
        table_kernel,
        [((RATIO, main, RATIO * chans), BF16), (outer, BF16), (outer, BF16)],
        (where, up_weight.transpose(1, 2, 0), cotangent),
        scratch=[VMEM((fine_ch, chans, subs), BF16), pltpu.SemaphoreType.DMA((4,))],
        scalars=1,
        hbm=(1, 2),
        flops=1e9,
    )
    outer_planes = [plane.reshape(face) for plane in (first_plane, second_plane)]
    x_low, x_high = exchange_width(outer_planes, faces)
    conv, back, enc_pre, encoded, dark3, upsampled = call(
        functools.partial(encode_kernel, depth=depth),
        [
            ((3, rows, 3 * taps), BF16),
            ((main, 9 * rows), BF16),
            ((cells, lanes), F32),
            ((cells, lanes), BF16),
            ((cells + 2 * width, 3 * lanes), BF16),
            ((3 * taps, (RATIO + 4) * fine_width), BF16),
        ],
        (where, w_dec.transpose(1, 2, 0), w_enc, wide_table, *dark_planes),
        scratch=[VMEM((planes + 2, depth + 2, width, 2 * chans), F32)],
        scalars=1,
        flops=2e9,
    )
    own = own_fine * fine_width
    dec_grad, outer_pre, edge_pre, dec_sum = call(
        decode_kernel,
        [
            ((3 * main, own), BF16),
            ((2, rows, fine_width), F32),
            ((rows - main, own), F32),
            ((fine_ch, 27 * fine_ch), F32),
        ],
        (cotangent, conv, upsampled),
        flops=2e9,
    )
    chunk = max(1, RATIO * RATIO // owners) * fine_ch + RATIO
    (send,) = call(
        functools.partial(spread_kernel, planes_x=planes, planes_z=depth),
        [((owners, chunk, fine_width), BF16)],
        (
            where, cotangent, x_low, x_high, faces[0], faces[-1], dec_grad, outer_pre, edge_pre,
            back, wide_table,
        ),
        scratch=[
            VMEM((3 * rows, own + 2 * fine_width), BF16),
        ],
        scalars=1,
        flops=2e9,
    )
    steps = [1 << n for n in range(owners.bit_length() - 1)]
    if owners & (owners - 1):
        dec_sum = lax.psum(dec_sum, AXES)
        steps = []
    steps = sorted(steps)
    one_by_one = steps[: max(1, len(steps) - LAST_STEPS)]
    for step in one_by_one:
        other = swapped(dec_sum, step)
        if step == steps[0]:
            send, other, dec_sum = lax.optimization_barrier((send, other, dec_sum))
        dec_sum = dec_sum + other
    sums = [0]
    for step in steps[len(one_by_one) :]:
        sums += [step + other for other in sums]
    received = [swapped(dec_sum, step) for step in sums[1:]]
    got = lax.all_to_all(send, AXES, 0, 0, tiled=True)
    enc_spread, enc_slope, enc_taps, order = call(
        widen_kernel,
        [
            ((cells * RATIO, lanes), BF16),
            ((cells, lanes), F32),
            ((3, 3 * lanes, chans), BF16),
            ((27 * fine_ch, 32 * fine_ch), BF16),
        ],
        (where, encoded, enc_pre, w_enc),
        scalars=1,
        flops=1e9,
    )
    coarse_scale = 1.0 / math.sqrt(cells * depth)
    fine_scale = 1.0 / math.sqrt(cells * depth * subs)
    pairs = (chunk - RATIO) // fine_ch
    grad_dark, grad_enc, grad_up, done = call(
        functools.partial(finish_kernel, scale=coarse_scale),
        [
            ((planes, width, chans), F32),
            ((27, chans, chans), F32),
            ((pairs * RATIO, fine_ch, chans), F32),
            ((8, 128), F32),
        ],
        (got, enc_spread, enc_slope, dark3, enc_taps),
        scratch=[VMEM((cells + 2 * width, 3 * lanes), BF16)],
        flops=2e9,
    )
    if own_rows < pairs * RATIO:
        own = lax.axis_index(AXES) * own_rows % RATIO
        grad_up = lax.dynamic_slice_in_dim(grad_up, own, own_rows, 0)
    (grad_dec,) = call(
        functools.partial(final_kernel, scale=fine_scale),
        [((fine_ch, fine_ch, 27), F32)],
        (order, done, dec_sum, *received),
        flops=1e8,
    )
    return grad_dark.transpose(2, 0, 1)[:, :, None], grad_enc, grad_up, grad_dec.transpose(2, 0, 1)


def solution(mesh):
    in_specs = (P(None, None, "narrow", None), P(), P(), P(), P(None, "wide", "narrow", None))
    out_specs = (P(None, None, "narrow", None), P(), P(("wide", "narrow"), None, None), P())
    return jax.shard_map(
        on_device, mesh=mesh, in_specs=in_specs, out_specs=out_specs, check_vma=False
    )
```

```python
import functools
import math

import jax
import jax.numpy as jnp
from jax import lax
from jax.experimental import pallas as pl
from jax.experimental.pallas import tpu as pltpu
from jax.sharding import PartitionSpec as P

RATIO = 8
SPAN = 16
LAST_STEPS = 2
F32 = jnp.float32
BF16 = jnp.bfloat16
VMEM_LIMIT = 48 * 1024 * 1024
VMEM = pltpu.VMEM
AXES = ("wide", "narrow")


def slope_of(values):
    sigma = jax.nn.sigmoid(values)
    return sigma * (1.0 + values * (1.0 - sigma))


def dot(left, right):
    return jnp.dot(left, right, preferred_element_type=F32)


def dot_nt(left, right):
    return lax.dot_general(left, right, (((1,), (1,)), ((), ())), preferred_element_type=F32)


def dot_tn(left, right):
    return lax.dot_general(left, right, (((0,), (0,)), ((), ())), preferred_element_type=F32)


def split(values):
    high = values.astype(BF16)
    rest = values - high.astype(F32)
    middle = rest.astype(BF16)
    return high, middle, (rest - middle.astype(F32)).astype(BF16)


def iota(shape, dim):
    return lax.broadcasted_iota(jnp.int32, shape, dim)


def row_index(count):
    return iota((count, 1), 0)


def lane_index(count):
    return iota((1, count), 1)


def one_hot(condition):
    return jnp.where(condition, 1.0, 0.0).astype(BF16)


def place(index, fine_ch):
    main = fine_ch * RATIO
    over = index - main
    channel = jnp.where(index < main, index // RATIO, over % fine_ch)
    z = jnp.where(index < main, index % RATIO, jnp.where(over < fine_ch, -1, RATIO))
    return channel, z


def lane_shift(values, by):
    width = values.shape[1]
    lane = iota(values.shape, 1)
    if by > 0:
        return jnp.where(lane < by, 0.0, pltpu.roll(values, by, 1))
    return jnp.where(lane >= width + by, 0.0, pltpu.roll(values, width + by, 1))


def store_shifts(ref, block, values, top=0, stride=None):
    rows, width = values.shape
    stride = stride or rows
    lanes = slice(block * width, (block + 1) * width)
    parts = (lane_shift(values, 1), values, lane_shift(values, -1))
    for e, part in enumerate(parts):
        ref[top + e * stride : top + e * stride + rows, lanes] = part.astype(BF16)


def band_taps(dec_ref, conv_ref, back_ref):
    fine_ch = dec_ref.shape[0]
    rows = fine_ch * (RATIO + 2)
    square = fine_ch * fine_ch
    group = 9 * fine_ch
    block = 256
    column = lane_index(6 * block)
    rest = column % block
    base = 9 * (rest // (3 * fine_ch)) + (rest // fine_ch) % 3 + 3 * (column // block % 3)
    tap = jnp.where(column < 3 * block, base, 26 - base)
    chosen_taps = one_hot(iota((27, 6 * block), 0) == jnp.where(rest < group, tap, -1))
    cell = row_index(square)
    last_index = iota((square, block), 1) % fine_ch
    same_in = last_index == cell % fine_ch
    same_out = last_index == cell // fine_ch
    shape = (fine_ch, square)
    pick_out = one_hot(iota(shape, 0) == lane_index(square) // fine_ch)
    pick_in = one_hot(iota(shape, 0) == lane_index(square) % fine_ch)
    wide = group * SPAN
    spread = one_hot(iota((group, wide), 0) == lane_index(wide) // SPAN)
    spread = jnp.concatenate([spread, jnp.zeros((block - group, wide), BF16)], 0)
    back_wide = 9 * rows
    column = lane_index(back_wide)
    channel, _ = place(column % rows, fine_ch)
    spread_back = one_hot(iota((group, back_wide), 0) == column // rows * fine_ch + channel)
    spread_back = jnp.concatenate([spread_back, jnp.zeros((block - group, back_wide), BF16)], 0)
    chosen = dot(dec_ref[...].reshape(square, 27), chosen_taps)
    taps = []
    for n in range(6):
        part = chosen[:, n * block : (n + 1) * block]
        part = jnp.where(same_in if n < 3 else same_out, part, 0.0).astype(BF16)
        taps.append(dot(pick_out if n < 3 else pick_in, part).astype(BF16))
    forward = dot(jnp.concatenate(taps[:3], 0), spread)
    backward = dot(jnp.concatenate(taps[3:], 0), spread_back)

    def banded(parts, masks):
        blocks = []
        for first in range(0, parts[0].shape[1], 128):
            total = jnp.zeros(masks[0].shape, F32)
            for part, mask in zip(parts, masks):
                part = jnp.broadcast_to(part[:, first : first + 128], mask.shape)
                total = jnp.where(mask, part, total)
            blocks.append(total)
        return jnp.concatenate(blocks, 1)

    def rows_of(field, channel):
        return [
            field[b * fine_ch + channel : b * fine_ch + channel + 1] for b in range(3)
        ]

    slot = iota((RATIO, 128), 1) % SPAN
    masks = [10 - slot - iota((RATIO, 128), 0) == b for b in range(3)]
    pieces = [banded(rows_of(forward, o), masks) for o in range(fine_ch)]
    slot = iota((fine_ch, 128), 1) % SPAN
    parts = [forward[b * fine_ch : (b + 1) * fine_ch] for b in range(3)]
    pieces += [banded(parts, [base - slot == b for b in range(3)]) for base in (11, 2)]
    field = jnp.concatenate(pieces, 0).astype(BF16)
    for a in range(3):
        conv_ref[a] = field[:, a * (wide // 3) : (a + 1) * (wide // 3)]
    _, z_in = place(lane_index(back_wide) % rows, fine_ch)
    offset = z_in - iota((RATIO, back_wide), 0) + 1
    masks = [offset == b for b in range(3)]
    pieces = []
    for c in range(fine_ch):
        total = jnp.zeros(offset.shape, F32)
        for part, mask in zip(rows_of(backward, c), masks):
            total = jnp.where(mask, jnp.broadcast_to(part, offset.shape), total)
        pieces.append(total)
    back_ref[...] = jnp.concatenate(pieces, 0).astype(BF16)


def table_kernel(
    place_ref, table_hbm, cot_hbm, wide_ref, first_ref, second_ref, table_ref, sems
):
    last = cot_hbm.shape[1] - 1
    even = lax.rem(place_ref[0], 2) == 0
    fine_ch, chans, subs = table_ref.shape
    half = fine_ch // 2
    loads = [
        pltpu.make_async_copy(
            table_hbm.at[n * half : (n + 1) * half],
            table_ref.at[n * half : (n + 1) * half],
            sems.at[n],
        )
        for n in range(2)
    ]
    planes = [
        pltpu.make_async_copy(cot_hbm.at[:, jnp.where(even, last, 0)], first_ref, sems.at[2]),
        pltpu.make_async_copy(cot_hbm.at[:, jnp.where(even, 0, last)], second_ref, sems.at[3]),
    ]
    for copy in loads + planes:
        copy.start()
    pairs = RATIO * RATIO
    row = row_index(subs)
    position = row % pairs // RATIO * pairs + (RATIO - 1 - row % RATIO) * RATIO + row // pairs
    pick = one_hot(iota((subs, subs), 1) == position)
    two = 2 * chans
    low = iota((pairs, two), 1) < chans
    for n in range(2):
        loads[n].wait()
        part = table_ref[n * half : (n + 1) * half].reshape(half * chans, subs)
        turned = dot_nt(pick, part)
        for p in range(half // 2):
            lanes = slice(p * two, (p + 1) * two)
            top = (n * half // 2 + p) * SPAN
            for q in range(RATIO // 2):
                even = turned[2 * q * pairs : (2 * q + 1) * pairs, lanes]
                odd = turned[(2 * q + 1) * pairs : (2 * q + 2) * pairs, lanes]
                first = jnp.where(low, even, pltpu.roll(odd, chans, 1))
                second = jnp.where(low, pltpu.roll(even, chans, 1), odd)
                both = jnp.concatenate(
                    [first.reshape(RATIO, RATIO, two), second.reshape(RATIO, RATIO, two)], 1
                )
                wide_ref[:, top : top + SPAN, q * two : (q + 1) * two] = both.astype(BF16)
    for copy in planes:
        copy.wait()


def shift_rows(values, width):
    count = values.shape[0]
    block = min(count, 256)
    row = iota((block, block), 0)
    column = iota((block, block), 1)
    down = one_hot((column == row - 1) & (row % width > 0))
    up = one_hot((column == row + 1) & (row % width < width - 1))
    pieces = []
    for first in range(0, count, block):
        part = values[first : first + block]
        pieces.append(
            jnp.concatenate([dot(down, part).astype(BF16), part, dot(up, part).astype(BF16)], 1)
        )
    return jnp.concatenate(pieces, 0)


def store_padded(ref, values, width):
    rows, lanes = ref.shape
    ref[0:width] = jnp.zeros((width, lanes), BF16)
    ref[rows - width : rows] = jnp.zeros((width, lanes), BF16)
    ref[width : rows - width] = shift_rows(values, width)


def encode_kernel(
    place_ref, dec_ref, enc_ref, wide_ref, *refs, depth
):
    *dark_refs, conv_ref, back_ref, pre_ref, encoded_ref, dark3_ref, up_ref, pad_ref = refs
    planes, width, chans = dark_refs[0].shape[-3:]
    main = wide_ref.shape[1]
    fine_ch = main // RATIO
    cells = planes * width
    fine_width = width * RATIO
    blank = jnp.zeros((chans, chans), BF16)
    weights = []
    for a in range(3):
        rows = []
        for z_out in range(depth):
            blocks = []
            for e in range(3):
                for z_in in range(depth):
                    b = z_in - z_out + 1
                    blocks.append(enc_ref[9 * a + 3 * b + e] if 0 <= b < 3 else blank)
            rows.append(jnp.concatenate(blocks, 1))
        weights.append(jnp.concatenate(rows, 0))
    if len(dark_refs) == 2:
        own, other = (ref[...].reshape(cells, chans) for ref in dark_refs)
        first = place_ref[1] == 0
        parts = [jnp.where(first, own, other), jnp.where(first, other, own)]
    else:
        parts = [dark_refs[0][z].reshape(cells, chans) for z in range(depth)]
    dark = jnp.concatenate(parts, 1)
    store_padded(dark3_ref, dark, width)
    pre = sum(
        dot_nt(dark3_ref[a * width : a * width + cells], weights[a]) for a in range(3)
    )
    pre_ref[...] = pre
    band_taps(dec_ref, conv_ref, back_ref)
    encoded = jax.nn.silu(pre).astype(BF16)
    encoded_ref[...] = encoded
    pad_ref[...] = jnp.zeros(pad_ref.shape, F32)
    for z in range(depth):
        part = encoded[:, z * chans : (z + 1) * chans].astype(F32)
        pad_ref[1 : planes + 1, z + 1] = jnp.concatenate([part, part], 1).reshape(
            planes, width, 2 * chans
        )
    first_x = place_ref[0]
    first_z = place_ref[1]
    repeat = one_hot(
        iota((fine_width, width), 0) // RATIO == iota((fine_width, width), 1)
    )
    two = 2 * chans
    cells = jnp.concatenate(
        [pad_ref[first_x + dx, first_z + dz] for dx in range(3) for dz in range(3)], 1
    )
    repeated = dot(repeat, cells.astype(BF16))
    lane = iota((fine_width, two), 1) // chans
    phase = iota((fine_width, two), 0) % RATIO
    low = iota((fine_ch, RATIO, fine_width), 1) < 2
    columns = []
    for n in range(9):
        cell = repeated[:, n * two : (n + 1) * two]
        columns.append(
            jnp.concatenate(
                [jnp.where(phase == 2 * q + lane, cell, 0.0) for q in range(RATIO // 2)], 1
            ).astype(BF16)
        )
    plan = (
        (0, 2, ((1, 2), (2, RATIO + 2))),
        (2, RATIO - 4, ((1, 2),)),
        (RATIO - 2, 2, ((0, 2 - RATIO), (1, 2))),
    )
    for first, count, needed in plan:
        field = dot_nt(
            wide_ref[first : first + count].reshape(count * main, RATIO * chans),
            jnp.concatenate([columns[3 * dx + dz] for dx, _ in needed for dz in range(3)], 0),
        )
        for n in range(count):
            for m, (_, base) in enumerate(needed):
                under, own, over = (
                    pltpu.roll(
                        field[
                            n * main : (n + 1) * main,
                            (3 * m + dz) * fine_width : (3 * m + dz + 1) * fine_width,
                        ].reshape(fine_ch, RATIO, fine_width),
                        2,
                        1,
                    )
                    for dz in range(3)
                )
                plane = jnp.concatenate([jnp.where(low, over, own), jnp.where(low, own, under)], 1)
                store_shifts(up_ref, base + first + n, plane.reshape(fine_ch * SPAN, fine_width))


def decode_kernel(cot_ref, conv_ref, up_ref, grad_ref, outer_ref, edge_ref, total_ref):
    fine_ch, planes, depth, width = cot_ref.shape
    main = fine_ch * depth
    own = planes * width

    def convolve(first, count):
        low, high = first * width, (first + count) * width
        return sum(
            dot(conv_ref[a], up_ref[:, a * width + low : a * width + high]) for a in range(3)
        )

    step = 2
    ahead = convolve(0, step)
    for x in range(planes + 2):
        if x % step == 0:
            pre = ahead
            if x + step < planes + 2:
                ahead = convolve(x + step, step)
        here = pre[:, x % step * width : (x % step + 1) * width]
        if 0 < x <= planes:
            cot = cot_ref[:, x - 1].astype(F32).reshape(main, width)
            grad = (cot * slope_of(here[:main])).astype(BF16)
            store_shifts(grad_ref, x - 1, grad.astype(F32))
            edge_ref[:, (x - 1) * width : x * width] = here[main:]
        else:
            outer_ref[0 if x == 0 else 1] = here
    grads = jnp.concatenate([grad_ref[e * main : (e + 1) * main] for e in (2, 1, 0)], 0)
    taps = fine_ch * SPAN
    sums = []
    for a in range(3):
        fields = up_ref[taps : 2 * taps, (a + 1) * width : (a + 1) * width + own]
        product = dot_nt(grads, fields)
        halves = []
        for first in range(0, taps, 128):
            part = product[:, first : first + 128].reshape(3 * fine_ch, RATIO, 128)
            halves.append(jnp.sum(pltpu.roll(part, 0, 2, stride=1, stride_axis=1), 1))
        sums.append(jnp.concatenate(halves, 1))
    shape = (3 * fine_ch, taps)
    fold = one_hot(
        iota(shape, 1)
        == row_index(shape[0]) % fine_ch * SPAN + 10 - row_index(shape[0]) // fine_ch
    )
    total = sum(dot_nt(fold, part) for part in split(jnp.concatenate(sums, 0)))
    total = jnp.concatenate([total[b * fine_ch : (b + 1) * fine_ch] for b in range(3)], 1)
    rest = total[:, 3 * 128 :]
    rest = jnp.concatenate([rest[:8], rest[8:], jnp.zeros((8, 32), F32)], 1)
    total_ref[...] = jnp.concatenate([total[:, n * 128 : (n + 1) * 128] for n in range(3)] + [rest], 0)


def spread_kernel(
    place_ref, cot_ref, x_low_ref, x_high_ref, z_low_ref, z_high_ref, own_ref, outer_ref, edge_ref,
    back_ref, wide_ref, send_ref, grad_ref, *, planes_x, planes_z
):
    fine_ch, planes, depth, width = cot_ref.shape
    main = fine_ch * depth
    own = planes * width
    rows = outer_ref.shape[1]
    chans = wide_ref.shape[2] // RATIO
    owners, chunk, _ = send_ref.shape
    span = chunk - RATIO
    own_x = place_ref[0]
    own_z = place_ref[1]
    valid = (own_z > 0, own_z < planes_z - 1)
    for e in range(3):
        grad_ref[e * rows : e * rows + main, width : width + own] = own_ref[
            e * main : (e + 1) * main
        ]
    for x, outer in ((0, x_low_ref), (planes + 1, x_high_ref)):
        inside = own_x > 0 if x == 0 else own_x < planes_x - 1
        cot = [jnp.where(inside, outer[:main].astype(F32), 0.0)]
        for side in range(2):
            first = main + side * (outer.shape[0] - main - fine_ch)
            corner = outer[first : first + fine_ch].astype(F32)
            cot.append(jnp.where(valid[side] & inside, corner, 0.0))
        pre = outer_ref[0 if x == 0 else 1]
        grad = (jnp.concatenate(cot, 0) * slope_of(pre)).astype(BF16)
        store_shifts(grad_ref, x, grad.astype(F32))
    shape = (main, main)
    turn = iota(shape, 1) == row_index(main) % fine_ch * planes + row_index(main) // fine_ch
    sides = [
        dot(one_hot(turn & valid[side]), ref[...].astype(F32).reshape(main, width).astype(BF16))
        for side, ref in enumerate((z_low_ref, z_high_ref))
    ]
    for x in range(planes):
        cot = jnp.concatenate([side[x * fine_ch : (x + 1) * fine_ch] for side in sides], 0)
        grad = (cot * slope_of(edge_ref[:, x * width : (x + 1) * width])).astype(BF16)
        store_shifts(grad_ref, x + 1, grad.astype(F32), main, rows)
    taps = grad_ref.shape[0]
    back = sum(
        dot(back_ref[:, a * taps : (a + 1) * taps], grad_ref[:, a * width : a * width + own])
        for a in range(3)
    )
    cot = jnp.concatenate(
        [cot_ref[:, x].astype(F32).reshape(main, width) for x in range(planes)], 1
    )
    up = (cot + back).astype(BF16)
    row = row_index(main)
    order = jnp.concatenate(
        [row % fine_ch * RATIO + row // fine_ch, row // RATIO * RATIO + RATIO - 1 - row % RATIO], 0
    )
    both = dot(one_hot(iota((2 * main, main), 1) == order), up).astype(BF16)
    turned, flipped = both[:main], both[main:]
    for owner in range(owners):
        first = owner * RATIO * RATIO // owners
        x = first // RATIO
        top = first % RATIO * fine_ch
        send_ref[owner, :span] = turned[top : top + span, x * width : (x + 1) * width]
    parts = dot_tn(
        jnp.concatenate([flipped[:, x * width : (x + 1) * width] for x in range(planes)], 0),
        wide_ref[...].reshape(planes * main, RATIO * chans),
    )
    two = 2 * chans
    phase = iota((width, two), 0) % RATIO
    lane = iota((width, two), 1) // chans
    both = sum(
        jnp.where(phase == 2 * q + lane, parts[:, q * two : (q + 1) * two], 0.0)
        for q in range(RATIO // 2)
    )
    cells = jnp.sum((both + pltpu.roll(both, chans, 1)).reshape(-1, RATIO, two), 1)
    half = cells.shape[0] // 2
    cells = jnp.where(iota((half, two), 1) < chans, cells[:half], cells[half:]).astype(BF16)
    for owner in range(owners):
        send_ref[owner, span:] = cells


def widen_kernel(
    place_ref, encoded_ref, pre_ref, enc_ref, out_ref, slope_ref, taps_ref, order_ref
):
    cells, lanes = encoded_ref.shape
    chans = enc_ref.shape[1]
    depth = lanes // chans
    block = 32
    repeat = one_hot(
        iota((block * RATIO, block), 0) // RATIO == iota((block * RATIO, block), 1)
    )
    for first in range(0, cells, block):
        out_ref[first * RATIO : (first + block) * RATIO] = dot(
            repeat, encoded_ref[first : first + block]
        ).astype(BF16)
    slope_ref[...] = slope_of(pre_ref[...])
    own_z = place_ref[1]
    for a in range(3):
        for e in range(3):
            for z in range(depth):
                b = z - own_z + 1
                tap = enc_ref[26 - (9 * a + 3 * jnp.clip(b, 0, 2) + e)]
                first = (3 * e * depth + 3 * z) * chans // 3
                taps_ref[a, first : first + chans] = jnp.where(
                    (b >= 0) & (b <= 2), tap.astype(F32), 0.0
                ).astype(BF16)
    shape = order_ref.shape
    fine_ch = shape[0] // 27
    step = shape[1] // fine_ch
    row = row_index(shape[0])
    tap = row // fine_ch
    tap = tap // 9 * 3 + tap // 3 % 3 * 9 + tap % 3
    order_ref[...] = one_hot(iota(shape, 1) == row % fine_ch * step + tap)


def final_kernel(order_ref, done_ref, *refs, scale):
    *parts, out_ref = refs
    total = sum(part[...] for part in parts) * scale
    fine_ch = out_ref.shape[0]
    rest = total[3 * fine_ch :]
    rest = jnp.concatenate([rest[:, :48], rest[:, 48:96]], 0)
    total = jnp.concatenate(
        [total[n * fine_ch : (n + 1) * fine_ch] for n in range(3)] + [rest], 1
    )
    field = dot(jnp.concatenate(split(total), 0), order_ref[...])
    field = field[:fine_ch] + field[fine_ch : 2 * fine_ch] + field[2 * fine_ch :]
    step = field.shape[1] // fine_ch
    for o in range(fine_ch):
        first = o * step // 128 * 128
        part = field[:, first : first + 128]
        if o * step > first:
            part = pltpu.roll(part, 128 - (o * step - first), 1)
        out_ref[o] = part[:, :27]


def finish_kernel(
    got_ref, spread_ref, slope_ref, dark3_ref, taps_ref,
    dark_out, enc_out, up_out, done_ref, pad_ref, *, scale
):
    done_ref[...] = jnp.zeros(done_ref.shape, F32)
    owners, chunk, fine_width = got_ref.shape
    cells, lanes = slope_ref.shape
    chans = taps_ref.shape[2]
    depth = lanes // chans
    planes = owners // depth
    width = cells // planes
    span = chunk - RATIO
    fine_ch = up_out.shape[1]
    rows = []
    for x in range(planes):
        parts = [got_ref[x * depth + z, span:].astype(F32) for z in range(depth)]
        for half in range(2):
            rows.append(
                jnp.concatenate([part[:, half * chans : (half + 1) * chans] for part in parts], 1)
            )
    grad = (jnp.concatenate(rows, 0) * slope_ref[...]).astype(BF16)
    store_padded(pad_ref, grad, width)
    dark_out[...] = sum(
        dot(pad_ref[a * width : a * width + cells], taps_ref[a]) for a in range(3)
    ).reshape(planes, width, chans)
    turned = grad.astype(F32).T.astype(BF16)
    for a in range(3):
        product = dot(turned, dark3_ref[a * width : a * width + cells]) * scale
        for b in range(3):
            for e in range(3):
                total = None
                for z in range(depth):
                    z_in = z + b - 1
                    if 0 <= z_in < depth:
                        first = (e * depth + z_in) * chans
                        part = product[z * chans : (z + 1) * chans, first : first + chans]
                        total = part if total is None else total + part
                enc_out[9 * a + 3 * b + e] = (
                    jnp.zeros((chans, chans), F32) if total is None else total
                )
    pairs = span // fine_ch
    lane = iota((RATIO * fine_ch, fine_width), 1) % RATIO
    masks = one_hot(lane == iota((RATIO * fine_ch, fine_width), 0) // fine_ch)
    sums = None
    for z in range(depth):
        pieces = []
        for x in range(planes):
            arrived = got_ref[x * depth + z, :span]
            pieces.append(
                jnp.concatenate(
                    [
                        jnp.concatenate([arrived[p * fine_ch : (p + 1) * fine_ch]] * RATIO, 0)
                        * masks
                        for p in range(pairs)
                    ],
                    0,
                )
            )
        part = dot(jnp.concatenate(pieces, 1), spread_ref[...])
        part = part[:, z * chans : (z + 1) * chans]
        sums = part if sums is None else sums + part
    up_out[...] = (sums * scale).reshape(pairs * RATIO, fine_ch, chans)


def call(kernel, out_shape, args, scratch=(), scalars=0, flops=1e8, hbm=()):
    specs = [pl.BlockSpec(memory_space=pltpu.SMEM)] * scalars
    specs += [
        pl.BlockSpec(memory_space=pltpu.HBM if n in hbm else VMEM)
        for n in range(scalars, len(args))
    ]
    args = [
        pltpu.with_memory_space_constraint(arg, pltpu.HBM) if n in hbm else arg
        for n, arg in enumerate(args)
    ]
    return pl.pallas_call(
        kernel,
        out_shape=[jax.ShapeDtypeStruct(*s) for s in out_shape],
        in_specs=specs,
        out_specs=[pl.BlockSpec(memory_space=VMEM)] * len(out_shape),
        scratch_shapes=list(scratch),
        compiler_params=pltpu.CompilerParams(vmem_limit_bytes=VMEM_LIMIT),
        cost_estimate=pl.CostEstimate(
            flops=int(flops), bytes_accessed=2_000_000, transcendentals=0
        ),
    )(*args)


def shift(block, axis, by):
    count = lax.axis_size(axis)
    pairs = [(i, i + by) for i in range(count) if 0 <= i + by < count]
    return lax.ppermute(block, axis, pairs)


def swapped(value, step):
    count = lax.axis_size(AXES)
    return lax.ppermute(value, AXES, [(i, i ^ step) for i in range(count)])


def exchange_depth(dark_rows, cotangent):
    count = lax.axis_size("narrow")
    last = cotangent.shape[2] - 1
    if count == 2:
        swap = [(0, 1), (1, 0)]
        dark = lax.ppermute(dark_rows, "narrow", swap)
        z = jnp.where(lax.axis_index("narrow") == 0, last, 0)
        face = lax.ppermute(lax.dynamic_index_in_dim(cotangent, z, 2, False), "narrow", swap)
        return (dark_rows, dark), (face,)
    planes = lax.all_gather(dark_rows, "narrow", axis=0)
    low = shift(cotangent[:, :, last], "narrow", 1)
    return (planes,), (low, shift(cotangent[:, :, 0], "narrow", -1))


def exchange_width(planes, faces):
    count = lax.axis_size("wide")
    depth = lax.axis_size("narrow")
    last = faces[0].shape[1] - 1
    even = lax.axis_index("wide") % 2 == 0
    got = []
    for odd in range(2):
        partner = {}
        for x in range(count):
            other = x + 1 if x % 2 == odd else x - 1
            for z in range(depth):
                if 0 <= other < count:
                    partner[x * depth + z] = other * depth + z
                elif depth % 2 == 0:
                    partner[x * depth + z] = x * depth + (z ^ 1)
        plane = jnp.where(even, 0, last) if odd else jnp.where(even, last, 0)
        edges = [lax.dynamic_index_in_dim(face, plane, 1, False) for face in faces]
        send = jnp.concatenate([planes[odd], *edges], 0)
        got.append(lax.ppermute(send, AXES, list(partner.items())))
    return jnp.where(even, got[1], got[0]), jnp.where(even, got[0], got[1])


def on_device(dark, w_enc, up_weight, w_dec, cotangent):
    chans, planes, own_depth, width = dark.shape
    fine_ch, own_fine, fine_depth, fine_width = cotangent.shape
    subs = up_weight.shape[0]
    depth = lax.axis_size("narrow")
    owners = lax.axis_size(AXES)
    cells = planes * width
    lanes = depth * chans
    own_rows = subs // owners
    where = jnp.stack([lax.axis_index("wide"), lax.axis_index("narrow")]).astype(jnp.int32)

    dark_planes, faces = exchange_depth(dark[:, :, 0].transpose(1, 2, 0), cotangent)

    rows = fine_ch * (RATIO + 2)
    taps = fine_ch * SPAN
    main = fine_ch * RATIO
    face = (fine_ch * fine_depth, fine_width)
    outer = (fine_ch, fine_depth, fine_width)
    wide_table, first_plane, second_plane = call(
        table_kernel,
        [((RATIO, main, RATIO * chans), BF16), (outer, BF16), (outer, BF16)],
        (where, up_weight.transpose(1, 2, 0), cotangent),
        scratch=[VMEM((fine_ch, chans, subs), BF16), pltpu.SemaphoreType.DMA((4,))],
        scalars=1,
        hbm=(1, 2),
        flops=1e9,
    )
    outer_planes = [plane.reshape(face) for plane in (first_plane, second_plane)]
    x_low, x_high = exchange_width(outer_planes, faces)
    conv, back, enc_pre, encoded, dark3, upsampled = call(
        functools.partial(encode_kernel, depth=depth),
        [
            ((3, rows, 3 * taps), BF16),
            ((main, 9 * rows), BF16),
            ((cells, lanes), F32),
            ((cells, lanes), BF16),
            ((cells + 2 * width, 3 * lanes), BF16),
            ((3 * taps, (RATIO + 4) * fine_width), BF16),
        ],
        (where, w_dec.transpose(1, 2, 0), w_enc, wide_table, *dark_planes),
        scratch=[VMEM((planes + 2, depth + 2, width, 2 * chans), F32)],
        scalars=1,
        flops=2e9,
    )
    own = own_fine * fine_width
    dec_grad, outer_pre, edge_pre, dec_sum = call(
        decode_kernel,
        [
            ((3 * main, own), BF16),
            ((2, rows, fine_width), F32),
            ((rows - main, own), F32),
            ((3 * fine_ch + 8, 128), F32),
        ],
        (cotangent, conv, upsampled),
        flops=2e9,
    )
    chunk = max(1, RATIO * RATIO // owners) * fine_ch + RATIO
    (send,) = call(
        functools.partial(spread_kernel, planes_x=planes, planes_z=depth),
        [((owners, chunk, fine_width), BF16)],
        (
            where, cotangent, x_low, x_high, faces[0], faces[-1], dec_grad, outer_pre, edge_pre,
            back, wide_table,
        ),
        scratch=[
            VMEM((3 * rows, own + 2 * fine_width), BF16),
        ],
        scalars=1,
        flops=2e9,
    )
    steps = [1 << n for n in range(owners.bit_length() - 1)]
    if owners & (owners - 1):
        dec_sum = lax.psum(dec_sum, AXES)
        steps = []
    steps = sorted(steps)
    one_by_one = steps[: max(1, len(steps) - LAST_STEPS)]
    for step in one_by_one:
        other = swapped(dec_sum, step)
        if step == steps[0]:
            send, other, dec_sum = lax.optimization_barrier((send, other, dec_sum))
        dec_sum = dec_sum + other
    sums = [0]
    for step in steps[len(one_by_one) :]:
        sums += [step + other for other in sums]
    received = [swapped(dec_sum, step) for step in sums[1:]]
    got = lax.all_to_all(send, AXES, 0, 0, tiled=True)
    enc_spread, enc_slope, enc_taps, order = call(
        widen_kernel,
        [
            ((cells * RATIO, lanes), BF16),
            ((cells, lanes), F32),
            ((3, 3 * lanes, chans), BF16),
            ((27 * fine_ch, 32 * fine_ch), BF16),
        ],
        (where, encoded, enc_pre, w_enc),
        scalars=1,
        flops=1e9,
    )
    coarse_scale = 1.0 / math.sqrt(cells * depth)
    fine_scale = 1.0 / math.sqrt(cells * depth * subs)
    pairs = (chunk - RATIO) // fine_ch
    grad_dark, grad_enc, grad_up, done = call(
        functools.partial(finish_kernel, scale=coarse_scale),
        [
            ((planes, width, chans), F32),
            ((27, chans, chans), F32),
            ((pairs * RATIO, fine_ch, chans), F32),
            ((8, 128), F32),
        ],
        (got, enc_spread, enc_slope, dark3, enc_taps),
        scratch=[VMEM((cells + 2 * width, 3 * lanes), BF16)],
        flops=2e9,
    )
    if own_rows < pairs * RATIO:
        own = lax.axis_index(AXES) * own_rows % RATIO
        grad_up = lax.dynamic_slice_in_dim(grad_up, own, own_rows, 0)
    (grad_dec,) = call(
        functools.partial(final_kernel, scale=fine_scale),
        [((fine_ch, fine_ch, 27), F32)],
        (order, done, dec_sum, *received),
        flops=1e8,
    )
    return grad_dark.transpose(2, 0, 1)[:, :, None], grad_enc, grad_up, grad_dec.transpose(2, 0, 1)


def solution(mesh):
    in_specs = (P(None, None, "narrow", None), P(), P(), P(), P(None, "wide", "narrow", None))
    out_specs = (P(None, None, "narrow", None), P(), P(("wide", "narrow"), None, None), P())
    return jax.shard_map(
        on_device, mesh=mesh, in_specs=in_specs, out_specs=out_specs, check_vma=False
    )
```
